32 devices in a mesh: wide: 16 (over z, x, core), narrow: 2 (over y).
Axes of the slice: x: 2, y: 2, z: 4, core: 2. Of those that a mesh axis runs over, the one named last changes fastest.
Arguments:
- joint_in: bfloat16 [20480, 768], P(('wide', 'narrow')), may hold values from -6 to 6
- cotangent: bfloat16 [20480, 768], P(('wide', 'narrow')), may hold values from -6 to 6
- segment_ids: int32 [20480], replicated, may hold values from 0 to 31, never falling along the last dimension, each value on 1 to 1280 neighbouring positions
- layer_index: int32 [1], replicated, may hold values from 0 to 11
- step_index: int32 [1], replicated, may hold values from 0 to 99999
- gain_one: float32 [768], P(('wide', 'narrow')), may hold values from 0.5 to 1.5
- w_qkv: float32 [768, 2304], P(('wide', 'narrow')), may hold values from -0.21875 to 0.21875
- w_attn_out: float32 [768, 768], P(('wide', 'narrow')), may hold values from -0.875 to 0.875
- gain_two: float32 [768], P(('wide', 'narrow')), may hold values from 0.5 to 1.5
- w_hidden: float32 [768, 3072], P(('wide', 'narrow')), may hold values from -0.21875 to 0.21875
- w_proj: float32 [3072, 768], P(('wide', 'narrow')), may hold values from -0.109375 to 0.109375
- mom_gain_one: float32 [768], P(('wide', 'narrow')), may hold values from -96 to 96
- mom_qkv: float32 [768, 2304], P(('wide', 'narrow')), may hold values from -6 to 6
- mom_attn_out: float32 [768, 768], P(('wide', 'narrow')), may hold values from -6 to 6
- mom_gain_two: float32 [768], P(('wide', 'narrow')), may hold values from -96 to 96
- mom_hidden: float32 [768, 3072], P(('wide', 'narrow')), may hold values from -96 to 96
- mom_proj: float32 [3072, 768], P(('wide', 'narrow')), may hold values from -192 to 192
Outputs:
- joint_out: bfloat16 [20480, 768], P(('wide', 'narrow'))
- grad_in: bfloat16 [20480, 768], P(('wide', 'narrow'))
- step_gain_one: float32 [768], P(('wide', 'narrow'))
- step_qkv: float32 [768, 2304], P(('wide', 'narrow'))
- step_attn_out: float32 [768, 768], P(('wide', 'narrow'))
- step_gain_two: float32 [768], P(('wide', 'narrow'))
- step_hidden: float32 [768, 3072], P(('wide', 'narrow'))
- step_proj: float32 [3072, 768], P(('wide', 'narrow'))
- next_gain_one: float32 [768], P(('wide', 'narrow'))
- next_qkv: float32 [768, 2304], P(('wide', 'narrow'))
- next_attn_out: float32 [768, 768], P(('wide', 'narrow'))
- next_gain_two: float32 [768], P(('wide', 'narrow'))
- next_hidden: float32 [768, 3072], P(('wide', 'narrow'))
- next_proj: float32 [3072, 768], P(('wide', 'narrow'))
The draws below stay inside these ranges and needn't reach their ends.
Inputs may be any that keep to these rules, and one draw needn't show every extreme that they name: `segment_ids`: segment ids never fall along the rows; each sequence has 1 to 1280 tokens and one has exactly 1280.
All inputs are finite; a program needn't handle non-finite values.
Results may differ from the reference program's by a relative error of at most 0.013.
The reference program's roundings to bfloat16 on the way count: a program that leaves them out, or rounds other values in their place, can miss the bound.
Values may be sent and summed in bfloat16 or wider, within the bound.
No kernel may reach another device: no remote copies, remote signals or barrier semaphores. Data moves between devices by JAX's collectives and lax.ppermute only.
A program may use at most 256 MiB of HBM per device.

```python
import math
import jax
import jax.numpy as jnp
import numpy as np
from jax import lax

D = 768
HEADS = 12
FF = 3072
TOK_DEV = 640
HEAD = 64
TOKENS = 20480
SEQ_MAX = 1280
N_WIDE = 16
N_NARROW = 2


def block_scale(rng, dims, pieces, smallest, high):
    def one(axis_at, blocks):
        draws = jax.random.uniform(jax.random.fold_in(jax.random.fold_in(rng, 6), axis_at), (blocks,), jnp.float32, smallest / len(pieces), high / len(pieces))
        return jnp.repeat(jnp.exp(draws), dims[axis_at] // blocks).reshape((-1,) + (1,) * (len(dims) - axis_at - 1))

    level = one(*pieces[0])
    for cut in pieces[1:]:
        level = level * one(*cut)
    return level


def profile(amount, total, reach, slope):
    portions = [(1 << 20) // math.isqrt(standing ** slope) + 1 for standing in range(2, amount + 1)]
    surplus, counts = total - reach - (amount - 1), [1] * (amount - 1)
    while surplus > 0:
        movable = [i for i in range(amount - 1) if counts[i] < reach]
        mass, remaining = sum([portions[i] for i in movable]), surplus
        for i in movable:
            addition = min(reach - counts[i], max(1, remaining * portions[i] // mass), surplus)
            counts[i] = counts[i] + addition
            surplus = surplus - addition
    return np.array([reach] + counts)


def ragged(key, number_of, total, reach, skew):
    if number_of == 2:
        one = jax.random.randint(key, (), max(1, total - reach), min(reach, total - 1) + 1)
        return jnp.stack([one, total - one])
    tallies = jnp.asarray(profile(number_of, total, reach, skew), jnp.int32)
    twos = (number_of - 1) // 2
    giver, sink = tallies[1:1 + 2 * twos:2], tallies[2:2 + 2 * twos:2]
    room = jnp.minimum(giver - 1, reach - sink)
    moved = jax.random.randint(jax.random.fold_in(key, 1), (twos,), 0, 1 << 20) % (room + 1)
    tallies = tallies.at[1:1 + 2 * twos:2].set(giver - moved).at[2:2 + 2 * twos:2].set(sink + moved)
    return tallies[jax.random.permutation(jax.random.fold_in(key, 2), number_of)]


def normal_values(stream_key, dims, spread, bound, pieces=(), kind=jnp.bfloat16):
    array = spread * jax.random.normal(stream_key, dims, jnp.float32)
    if pieces:
        array = array * block_scale(stream_key, dims, pieces, -0.22, 0.18)
    return jnp.clip(array, -bound, bound).astype(kind)


def setup_inputs(seed: int = 0) -> dict:
    splits = jax.random.split(jax.random.key(seed), 18)
    return {
        "joint_in": normal_values(splits[0], (TOKENS, D), 1.0, 6.0, ((0, 32),)),
        "cotangent": normal_values(splits[1], (TOKENS, D), 1.0, 6.0, ((0, 32),)),
        "segment_ids": jnp.searchsorted(jnp.cumsum(ragged(splits[2], 2 * TOKENS // SEQ_MAX, TOKENS, SEQ_MAX, 0)), jnp.arange(TOKENS), side="right").astype(jnp.int32),
        "layer_index": jax.random.randint(splits[3], (1,), 0, 12).astype(jnp.int32),
        "step_index": jax.random.randint(splits[4], (1,), 0, 100000).astype(jnp.int32),
        "gain_one": jnp.clip(1.0 + 0.1 * jax.random.normal(splits[5], (D,), jnp.float32), 0.5, 1.5),
        "w_qkv": normal_values(splits[6], (D, 3 * D), D ** -0.5, 0.21875, ((0, 32),), jnp.float32),
        "w_attn_out": normal_values(splits[7], (D, D), (D // 16) ** -0.5, 0.875, ((0, 32),), jnp.float32),
        "gain_two": jnp.clip(1.0 + 0.1 * jax.random.normal(splits[8], (D,), jnp.float32), 0.5, 1.5),
        "w_hidden": normal_values(splits[9], (D, FF), D ** -0.5, 0.21875, ((0, 32),), jnp.float32),
        "w_proj": normal_values(splits[10], (FF, D), FF ** -0.5, 0.109375, ((0, 32),), jnp.float32),
        "mom_gain_one": normal_values(splits[11], (D,), 16.0, 96.0, ((0, 32),), jnp.float32),
        "mom_qkv": normal_values(splits[12], (D, 3 * D), 1.0, 6.0, ((0, 32),), jnp.float32),
        "mom_attn_out": normal_values(splits[13], (D, D), 1.0, 6.0, ((0, 32),), jnp.float32),
        "mom_gain_two": normal_values(splits[14], (D,), 16.0, 96.0, ((0, 32),), jnp.float32),
        "mom_hidden": normal_values(splits[15], (D, FF), 16.0, 96.0, ((0, 32),), jnp.float32),
        "mom_proj": normal_values(splits[16], (FF, D), 32.0, 192.0, ((0, 32),), jnp.float32),
    }


@jax.custom_vjp
def low(v):
    return lax.optimization_barrier(v.astype(jnp.bfloat16)).astype(jnp.float32)

@jax.custom_vjp
def low_back(v):
    return v

def low_keep(v):
    return (low(v), None)

def low_pass(kept, grad):
    return (grad,)

def back_keep(v):
    return (v, None)

def back_low(kept, grad):
    return (low(grad),)
low.defvjp(low_keep, low_pass)
low_back.defvjp(back_keep, back_low)
eps = 1e-06
base_rate = 0.01
decay_rate = 0.65
total_steps = 100000.0
momentum_rate = 0.9

def matmul(left, right):
    return jnp.dot(left, right, precision=lax.Precision.HIGHEST)

def normalize(values, gain):
    centre = lax.optimization_barrier(jnp.mean(values, axis=-1, keepdims=True))
    centred = values - centre
    inverse = lax.rsqrt(lax.optimization_barrier(jnp.mean(centred * centred, axis=-1, keepdims=True)) + eps)
    return centred * inverse * gain

def attend_group(query, keys, values, own_ids, key_ids):
    scores = jnp.einsum('qhd,khd->hqk', query, keys, precision=lax.Precision.HIGHEST) * HEAD ** (-0.5)
    scores = low_back(scores)
    allowed = own_ids[:, None] == key_ids[None, :]
    scores = jnp.where(allowed[None], scores, -1e+30)
    top = lax.optimization_barrier(jnp.max(scores, axis=-1, keepdims=True))
    expo = jnp.exp(scores - top)
    probs = expo / lax.optimization_barrier(jnp.sum(expo, axis=-1, keepdims=True))
    return jnp.einsum('hqk,khd->qhd', low(probs), values, precision=lax.Precision.HIGHEST)

def forward(joint, gain_one, w_qkv, w_attn_out, gain_two, w_hidden, w_proj, segment_ids):
    group = N_NARROW * TOK_DEV
    normed = low(normalize(joint, low(gain_one)))
    qkv = low_back(low(matmul(normed, low(w_qkv))))
    query = qkv[:, :D].reshape(TOKENS, HEADS, HEAD)
    keys = jnp.pad(qkv[:, D:2 * D].reshape(TOKENS, HEADS, HEAD), ((group, group), (0, 0), (0, 0)))
    values = jnp.pad(qkv[:, 2 * D:].reshape(TOKENS, HEADS, HEAD), ((group, group), (0, 0), (0, 0)))
    padded_ids = jnp.pad(segment_ids, (group, group), constant_values=-1)

    def one_group(index):
        start = (index * group).astype(jnp.int32)
        return attend_group(lax.dynamic_slice_in_dim(query, start, group, 0), lax.dynamic_slice_in_dim(keys, start, 3 * group, 0), lax.dynamic_slice_in_dim(values, start, 3 * group, 0), lax.dynamic_slice_in_dim(segment_ids, start, group, 0), lax.dynamic_slice_in_dim(padded_ids, start, 3 * group, 0))
    attended = lax.map(jax.checkpoint(one_group), jnp.arange(N_WIDE, dtype=jnp.int32))
    attended = low_back(low(attended.reshape(TOKENS, D)))
    mid = joint + low_back(matmul(attended, low(w_attn_out)))
    second = low(normalize(mid, low(gain_two)))
    hidden_pre = low_back(matmul(second, low(w_hidden)))
    hidden = low(jax.nn.gelu(hidden_pre, approximate=False))
    return mid + low_back(matmul(hidden, low(w_proj)))

def reference(joint_in, cotangent, segment_ids, layer_index, step_index, gain_one, w_qkv, w_attn_out, gain_two, w_hidden, w_proj, mom_gain_one, mom_qkv, mom_attn_out, mom_gain_two, mom_hidden, mom_proj):
    joint = joint_in.astype(jnp.float32)

    def layer(joint, gain_one, w_qkv, w_attn_out, gain_two, w_hidden, w_proj):
        return forward(joint, gain_one, w_qkv, w_attn_out, gain_two, w_hidden, w_proj, segment_ids)
    output, pull = jax.vjp(layer, joint, gain_one, w_qkv, w_attn_out, gain_two, w_hidden, w_proj)
    grads = pull(cotangent.astype(jnp.float32))
    rate = base_rate * jnp.power(jnp.float32(decay_rate), (11 - layer_index[0]).astype(jnp.float32))
    rate = rate * jnp.power(1.0 - step_index[0].astype(jnp.float32) / total_steps, 0.9)
    next_g1 = momentum_rate * mom_gain_one + grads[1]
    next_qkv = momentum_rate * mom_qkv + grads[2]
    next_out = momentum_rate * mom_attn_out + grads[3]
    next_g2 = momentum_rate * mom_gain_two + grads[4]
    next_hid = momentum_rate * mom_hidden + grads[5]
    next_prj = momentum_rate * mom_proj + grads[6]
    return (output.astype(jnp.bfloat16), grads[0].astype(jnp.bfloat16), rate * next_g1, rate * next_qkv, rate * next_out, rate * next_g2, rate * next_hid, rate * next_prj, next_g1, next_qkv, next_out, next_g2, next_hid, next_prj)
```

```python
import functools

import jax
import jax.numpy as jnp
from jax import lax
from jax.experimental import pallas as pl
from jax.experimental.pallas import tpu as pltpu
from jax.sharding import PartitionSpec as P

HEAD = 64
PAIR = 2 * HEAD
QT = 128
KT = 320
GROUP = 3
BRIEF = pl.CostEstimate(flops=1, bytes_accessed=1, transcendentals=0)

eps = 1e-06
base_rate = 0.01
decay_rate = 0.65
total_steps = 100000.0
momentum_rate = 0.9

bf = jnp.bfloat16
f32 = jnp.float32


def dot(left, right):
    return jnp.dot(left, right, preferred_element_type=f32)


def contract_rows(left, right):
    return lax.dot_general(
        left, right, (((0,), (0,)), ((), ())), preferred_element_type=f32
    )


def contract_cols(left, right):
    return lax.dot_general(
        left, right, (((1,), (1,)), ((), ())), preferred_element_type=f32
    )


def normalize_parts(values):
    centre = jnp.mean(values, axis=-1, keepdims=True)
    centred = values - centre
    inverse = lax.rsqrt(jnp.mean(centred * centred, axis=-1, keepdims=True) + eps)
    return (centred * inverse, inverse)


def normalize_back(grad_out, normed, inverse, gain):
    grad_normed = grad_out * gain
    inner = grad_normed - jnp.mean(grad_normed, axis=-1, keepdims=True)
    inner = inner - normed * jnp.mean(grad_normed * normed, axis=-1, keepdims=True)
    return inverse * inner


def diag_wide(block):
    row = lax.broadcasted_iota(jnp.int32, block.shape, 0)
    zero = jnp.zeros_like(block)
    return jnp.concatenate(
        [jnp.where(row < HEAD, block, zero), jnp.where(row >= HEAD, block, zero)], axis=1
    )


def diag_tall(block):
    col = lax.broadcasted_iota(jnp.int32, block.shape, 1)
    zero = jnp.zeros_like(block)
    return jnp.concatenate(
        [jnp.where(col < HEAD, block, zero), jnp.where(col >= HEAD, block, zero)], axis=0
    )


def tile_bias(kseg_ref, qseg_ref, t):
    bias = jnp.where(kseg_ref[...] == qseg_ref[t, 0:1, :], 0.0, -1e30).astype(f32)
    return jnp.concatenate([bias, bias], axis=1)


def columns_of(pair):
    return slice(pair * PAIR, (pair + 1) * PAIR)


def copy_rows(odd, step, refs, out):
    for ref, at in zip(refs, block_starts(odd)):
        @pl.when((step >= at) & (step < at + 2))
        def _(ref=ref):
            out[...] = ref[...]


def block_starts(odd):
    return (0, 6 - 4 * odd, 2 + 4 * odd, 8)


def attend_kernel(begin, end, odd, *refs, pieces):
    blocks, (kseg_ref, own_ref, qseg_ref, order_ref) = refs[:4], refs[4:8]
    parts = refs[8:8 + 2 * pieces]
    (w_ref, gains_ref, a_ref, k_ref, v_ref, q_ref, o_ref, lse_ref,
     qbd, top, total, acc, x_ref, rel_ref) = refs[8 + 2 * pieces:]
    step = pl.program_id(0)
    width = x_ref.shape[1]
    pairs = width // PAIR
    tiles = qseg_ref.shape[0]
    scale = HEAD ** (-0.5)

    @pl.when(step == 0)
    def _():
        rows = parts[0].shape[0] // 2
        cut = parts[0].shape[1]
        for j in range(pieces):
            for h in range(2):
                of = slice(h * rows, (h + 1) * rows)
                core, other = j // 2 * 4 * rows, j % 2
                lo = core + (2 * h + other) * rows
                rel_ref[lo:lo + rows, :cut] = parts[j][of, :]
                lo = core + (2 * other + h) * rows
                rel_ref[lo:lo + rows, cut:] = parts[pieces + j][of, :]
        w_ref[...] = dot(order_ref[...], rel_ref[...]).astype(bf)
        gains_ref[...] = w_ref[:, 3 * width:].astype(f32).T[:8]
        n, _ = normalize_parts(own_ref[...].astype(f32))
        q = dot((n * gains_ref[0:1, :]).astype(bf), w_ref[:, :width]).astype(bf)
        q_ref[...] = q
        q = q.astype(f32) * scale
        for t in range(tiles):
            for p in range(pairs):
                qbd[t, p] = diag_wide(q[t * QT:(t + 1) * QT, columns_of(p)].T.astype(bf))
        top[...] = jnp.full(top.shape, -1e30, f32)
        total[...] = jnp.zeros(total.shape, f32)
        acc[...] = jnp.zeros(acc.shape, f32)

    def visit(t, carry):
        bias = tile_bias(kseg_ref, qseg_ref, t)
        group = range(pairs)
        scores = [dot(k_ref[:, columns_of(p)], qbd[t, p]) + bias for p in group]
        olds = [top[t, p:p + 1, :] for p in group]
        news = [jnp.maximum(olds[p], jnp.max(scores[p], axis=0, keepdims=True)) for p in group]
        expo = [jnp.exp(scores[p] - news[p]) for p in group]
        shrinks = [jnp.exp(olds[p] - news[p]) for p in group]
        sums = [
            total[t, p:p + 1, :] * shrinks[p] + jnp.sum(expo[p], axis=0, keepdims=True)
            for p in group
        ]
        gots = [contract_rows(v_ref[:, columns_of(p)], expo[p].astype(bf)) for p in group]
        for p in group:
            top[t, p:p + 1, :] = news[p]
            total[t, p:p + 1, :] = sums[p]
            lo, mid, hi = p * PAIR, p * PAIR + HEAD, (p + 1) * PAIR
            acc[t, lo:mid, :] = acc[t, lo:mid, :] * shrinks[p][:, :QT] + gots[p][:HEAD, :QT]
            acc[t, mid:hi, :] = acc[t, mid:hi, :] * shrinks[p][:, QT:] + gots[p][HEAD:, QT:]
        return carry

    @pl.when(begin[step] < end[step])
    def _():
        copy_rows(odd[0], step, blocks, x_ref)

        @pl.when((step >= 4) & (step < 6))
        def _():
            x_ref[...] = own_ref[pl.ds(pl.multiple_of((step - 4) * KT, KT), KT), :]

        n, _ = normalize_parts(x_ref[...].astype(f32))
        a = (n * gains_ref[0:1, :]).astype(bf)
        a_ref[...] = a
        k_ref[...] = dot(a, w_ref[:, width:2 * width]).astype(bf)
        v_ref[...] = dot(a, w_ref[:, 2 * width:3 * width]).astype(bf)
        lax.fori_loop(begin[step], end[step], visit, 0)

    @pl.when(step == pl.num_programs(0) - 1)
    def _():
        for t in range(tiles):
            for p in range(pairs):
                sums = total[t, p:p + 1, :]
                lse_ref[t, p] = top[t, p:p + 1, :] + jnp.log(sums)
                inv = 1.0 / sums
                lo, mid, hi = p * PAIR, p * PAIR + HEAD, (p + 1) * PAIR
                out = jnp.concatenate(
                    [acc[t, lo:mid, :] * inv[:, :QT], acc[t, mid:hi, :] * inv[:, QT:]], axis=0
                )
                o_ref[t * QT:(t + 1) * QT, lo:hi] = out.T.astype(bf)


def block_specs(width, key):
    def spec(number):
        def index(step, begin, end, span, odd):
            return (jnp.clip(key(step) - block_starts(odd[0])[number], 0, 1), 0)

        return pl.BlockSpec((KT, width), index)

    return [spec(number) for number in range(4)]


def attend(scalars, blocks, kseg, x_own, qseg, order, ones, twos):
    rows, width = x_own.shape
    window = 5 * rows
    tiles = rows // QT
    pairs = width // PAIR
    columns = ones[0].shape[1] + twos[0].shape[1]
    whole = pl.BlockSpec(memory_space=pltpu.VMEM)

    def at_used(j, begin, end, span, odd):
        return (jnp.clip(j, span[0], span[1] - 1), 0)

    def kernel(begin, end, span, odd, *refs):
        attend_kernel(begin, end, odd, *refs, pieces=len(ones))

    tile = pl.BlockSpec((KT, width), at_used)
    return pl.pallas_call(
        kernel,
        grid_spec=pltpu.PrefetchScalarGridSpec(
            num_scalar_prefetch=4,
            grid=(window // KT,),
            in_specs=block_specs(width, lambda j: j)
            + [pl.BlockSpec((KT, QT), at_used)]
            + [whole] * (3 + 2 * len(ones)),
            out_specs=[whole, whole, tile, tile, tile, whole, whole, whole],
            scratch_shapes=[
                pltpu.VMEM((tiles, pairs, PAIR, 2 * QT), bf),
                pltpu.VMEM((tiles, 8, 2 * QT), f32),
                pltpu.VMEM((tiles, 8, 2 * QT), f32),
                pltpu.VMEM((tiles, width, QT), f32),
                pltpu.VMEM((KT, width), bf),
                pltpu.VMEM((width, columns), bf),
            ],
        ),
        out_shape=[
            jax.ShapeDtypeStruct((width, columns), bf),
            jax.ShapeDtypeStruct((8, width), f32),
            jax.ShapeDtypeStruct((window, width), bf),
            jax.ShapeDtypeStruct((window, width), bf),
            jax.ShapeDtypeStruct((window, width), bf),
            jax.ShapeDtypeStruct((rows, width), bf),
            jax.ShapeDtypeStruct((rows, width), bf),
            jax.ShapeDtypeStruct((tiles, pairs, 1, 2 * QT), f32),
        ],
        compiler_params=pltpu.CompilerParams(vmem_limit_bytes=56 * 1024 * 1024),
        cost_estimate=BRIEF,
        name="attend",
    )(*scalars, *blocks, kseg, x_own, qseg, order, *ones, *twos)


def back_tile(begin, end, j, refs, scratch):
    k_ref, v_ref, kseg_ref, qseg_ref, lse_ref = refs
    qbd, dobd, qn, don, delta, dq_acc, dk_acc, dv_acc = scratch
    pairs = qbd.shape[1]
    dk_acc[...] = jnp.zeros(dk_acc.shape, f32)
    dv_acc[...] = jnp.zeros(dv_acc.shape, f32)

    def visit(t, carry):
        bias = tile_bias(kseg_ref, qseg_ref, t)
        for base in range(0, pairs, GROUP):
            group = range(base, min(pairs, base + GROUP))
            keys = [k_ref[:, columns_of(p)] for p in group]
            scores = [dot(kp, qbd[t, p]) for kp, p in zip(keys, group)]
            dprobs = [dot(v_ref[:, columns_of(p)], dobd[t, p]) for p in group]
            probs = [jnp.exp(s + bias - lse_ref[t, p]) for s, p in zip(scores, group)]
            ds = [
                (pr * (dp - delta[t, p:p + 1, :])).astype(bf)
                for pr, dp, p in zip(probs, dprobs, group)
            ]
            got_v = [dot(pr.astype(bf), don[t, p]) for pr, p in zip(probs, group)]
            got_k = [dot(d, qn[t, p]) for d, p in zip(ds, group)]
            got_q = [contract_rows(kp, d) for kp, d in zip(keys, ds)]
            for i, p in enumerate(group):
                lo, mid, hi = p * PAIR, p * PAIR + HEAD, (p + 1) * PAIR
                dv_acc[:, lo:hi] += got_v[i]
                dk_acc[:, lo:hi] += got_k[i]
                dq_acc[t, lo:mid, :] += got_q[i][:HEAD, :QT]
                dq_acc[t, mid:hi, :] += got_q[i][HEAD:, QT:]
        return carry

    lax.fori_loop(begin[j], end[j], visit, 0)
    return dk_acc[...].astype(bf), dv_acc[...].astype(bf)


def back_prepare(q_ref, do_ref, o_ref, scratch):
    qbd, dobd, qn, don, delta = scratch
    tiles, pairs = qbd.shape[:2]
    scale = HEAD ** (-0.5)
    for t in range(tiles):
        at = slice(t * QT, (t + 1) * QT)
        for p in range(pairs):
            cols = columns_of(p)
            q = q_ref[at, cols].astype(f32) * scale
            do = do_ref[at, cols].astype(f32)
            do_t = do.T
            qbd[t, p] = diag_wide(q.T.astype(bf))
            dobd[t, p] = diag_wide(do_t.astype(bf))
            qn[t, p] = diag_tall(q.astype(bf))
            don[t, p] = diag_tall(do.astype(bf))
            both = do_t * o_ref[at, cols].astype(f32).T
            delta[t, p:p + 1, :QT] = jnp.sum(both[:HEAD], axis=0, keepdims=True)
            delta[t, p:p + 1, QT:] = jnp.sum(both[HEAD:], axis=0, keepdims=True)


def back_share(dk, dv, a, w_ref, acc):
    width = dk.shape[1]
    da = contract_cols(dk, w_ref[:, width:2 * width]) + contract_cols(dv, w_ref[:, 2 * width:3 * width])
    acc[:, :width] += contract_rows(a, dk)
    acc[:, width:] += contract_rows(a, dv)
    return da


def outer_kernel(begin, end, span, odd, k_ref, v_ref, a_ref, kseg_ref, q_ref, do_ref, o_ref,
                 lse_ref, qseg_ref, w_ref, b0, b1, b2, b3, *refs, own):
    da_refs = refs[-15:-11]
    acc_ref, dq_ref, gg_ref, qbd, dobd, qn, don, delta, dk_acc, dv_acc, x_ref = refs[-11:]
    step = pl.program_id(0)
    j = jnp.where(step < own[0], step, step + own[1] - own[0])

    @pl.when(step == 0)
    def _():
        back_prepare(q_ref, do_ref, o_ref, (qbd, dobd, qn, don, delta))
        acc_ref[...] = jnp.zeros(acc_ref.shape, f32)
        dq_ref[...] = jnp.zeros(dq_ref.shape, f32)
        gg_ref[...] = jnp.zeros(gg_ref.shape, f32)

    used = begin[j] < end[j]

    def put(value):
        for ref, at in zip(da_refs, block_starts(odd[0])):
            @pl.when((j >= at) & (j < at + 2))
            def _(ref=ref):
                ref[...] = value

    @pl.when(used)
    def _():
        dk, dv = back_tile(
            begin, end, j, (k_ref, v_ref, kseg_ref, qseg_ref, lse_ref),
            (qbd, dobd, qn, don, delta, dq_ref, dk_acc, dv_acc),
        )
        da = back_share(dk, dv, a_ref[...], w_ref, acc_ref)
        put(da.astype(bf))
        copy_rows(odd[0], j, (b0, b1, b2, b3), x_ref)
        n, _ = normalize_parts(x_ref[...].astype(f32))
        gg_ref[0:1, :] += jnp.sum(da * n, axis=0, keepdims=True)

    @pl.when(jnp.logical_not(used))
    def _():
        put(jnp.zeros(x_ref.shape, bf))


def inner_kernel(begin, end, span, odd, k_ref, v_ref, a_ref, kseg_ref, q_ref, do_ref, o_ref,
                 lse_ref, qseg_ref, w_ref, x_ref, order_ref, gb_ref, acc_in, dq_in, gg_in,
                 *refs, own):
    (da_ref, keep_ref, send_ref,
     qbd, dobd, qn, don, delta, dk_acc, dv_acc, acc, dq_acc, gg, dq_all, a_all) = refs[-15:]
    step = pl.program_id(0)
    width = k_ref.shape[1]
    half = width // 2
    tiles, pairs = qbd.shape[:2]

    @pl.when(step == 0)
    def _():
        back_prepare(q_ref, do_ref, o_ref, (qbd, dobd, qn, don, delta))
        acc[...] = acc_in[...]
        dq_acc[...] = dq_in[...]
        gg[...] = jnp.zeros(gg.shape, f32)
        gg[0:1, :] = gg_in[0:1, :]
        gg[1:2, :] = gb_ref[0:1, :]

    dk, dv = back_tile(
        begin, end, step + own[0], (k_ref, v_ref, kseg_ref, qseg_ref, lse_ref),
        (qbd, dobd, qn, don, delta, dq_acc, dk_acc, dv_acc),
    )
    at = pl.ds(pl.multiple_of(step * KT, KT), KT)
    da_ref[at, :] = back_share(dk, dv, a_ref[...], w_ref, acc)
    a_all[at, :] = a_ref[...]

    @pl.when(step == pl.num_programs(0) - 1)
    def _():
        scale = HEAD ** (-0.5)
        for t in range(tiles):
            for p in range(pairs):
                cols = columns_of(p)
                dq_all[t * QT:(t + 1) * QT, cols] = (dq_acc[t, cols, :] * scale).T.astype(bf)
        dq = dq_all[...]
        da = da_ref[...] + contract_cols(dq, w_ref[:, :width])
        da_ref[...] = da
        n, _ = normalize_parts(x_ref[...].astype(f32))
        gg[0:1, :] += jnp.sum(da * n, axis=0, keepdims=True)
        order = order_ref[...]

        def put(lo, grad):
            both = contract_rows(order, grad.astype(bf)).astype(bf)
            keep_ref[:, lo:lo + both.shape[1]] = both[:half]
            send_ref[:, lo:lo + both.shape[1]] = both[half:]

        put(0, contract_rows(a_all[...], dq))
        put(width, acc[...])
        put(3 * width, gg[...].T)


def back_specs(window, rows, width, own, at_key):
    tiles = rows // QT
    pairs = width // PAIR
    whole = pl.BlockSpec(memory_space=pltpu.VMEM)
    tile = pl.BlockSpec((KT, width), at_key)
    specs = [tile, tile, tile, pl.BlockSpec((KT, QT), at_key)] + [whole] * 6
    scratch = [
        pltpu.VMEM((tiles, pairs, PAIR, 2 * QT), bf),
        pltpu.VMEM((tiles, pairs, PAIR, 2 * QT), bf),
        pltpu.VMEM((tiles, pairs, 2 * QT, PAIR), bf),
        pltpu.VMEM((tiles, pairs, 2 * QT, PAIR), bf),
        pltpu.VMEM((tiles, 8, 2 * QT), f32),
        pltpu.VMEM((KT, width), f32),
        pltpu.VMEM((KT, width), f32),
    ]
    return specs, scratch, whole


def outer_back(scalars, k, v, a, kseg, q, do, o, lse, qseg, weight, blocks, *deps):
    window, width = k.shape
    rows = q.shape[0]
    own = (2 * rows // KT, 3 * rows // KT)
    steps = window // KT - own[1] + own[0]

    def key(step):
        return jnp.where(step < own[0], step, step + own[1] - own[0])

    def at_key(step, begin, end, span, odd):
        return (jnp.clip(key(step), span[0], span[1] - 1), 0)

    specs, scratch, whole = back_specs(window, rows, width, own, at_key)
    return pl.pallas_call(
        functools.partial(outer_kernel, own=own),
        grid_spec=pltpu.PrefetchScalarGridSpec(
            num_scalar_prefetch=4,
            grid=(steps,),
            in_specs=specs
            + block_specs(width, key)
            + [pl.BlockSpec(memory_space=pl.ANY)] * len(deps),
            out_specs=block_specs(width, key) + [whole, whole, whole],
            scratch_shapes=scratch + [pltpu.VMEM((KT, width), bf)],
        ),
        out_shape=[
            *[jax.ShapeDtypeStruct((rows, width), bf)] * 4,
            jax.ShapeDtypeStruct((width, 2 * width), f32),
            jax.ShapeDtypeStruct((rows // QT, width, QT), f32),
            jax.ShapeDtypeStruct((8, width), f32),
        ],
        compiler_params=pltpu.CompilerParams(vmem_limit_bytes=60 * 1024 * 1024),
        cost_estimate=BRIEF,
        name="outer_back",
    )(*scalars, k, v, a, kseg, q, do, o, lse, qseg, weight, *blocks, *deps)


def inner_back(scalars, k, v, a, kseg, q, do, o, lse, qseg, weight, x_own, order, gain_grad,
               partial, *deps):
    window, width = k.shape
    rows = q.shape[0]
    own = (2 * rows // KT, 3 * rows // KT)
    half = width // 2
    columns = weight.shape[1]

    def at_key(step, *_):
        return (step + own[0], 0)

    specs, scratch, whole = back_specs(window, rows, width, own, at_key)
    scratch += [
        pltpu.VMEM((width, 2 * width), f32),
        pltpu.VMEM((rows // QT, width, QT), f32),
        pltpu.VMEM((columns - 3 * width, width), f32),
        pltpu.VMEM((rows, width), bf),
        pltpu.VMEM((rows, width), bf),
    ]
    return pl.pallas_call(
        functools.partial(inner_kernel, own=own),
        grid_spec=pltpu.PrefetchScalarGridSpec(
            num_scalar_prefetch=4,
            grid=(own[1] - own[0],),
            in_specs=specs + [whole] * 6 + [pl.BlockSpec(memory_space=pl.ANY)] * len(deps),
            out_specs=[whole, whole, whole],
            scratch_shapes=scratch,
        ),
        out_shape=[
            jax.ShapeDtypeStruct((rows, width), f32),
            jax.ShapeDtypeStruct((half, columns), bf),
            jax.ShapeDtypeStruct((half, columns), bf),
        ],
        compiler_params=pltpu.CompilerParams(vmem_limit_bytes=62 * 1024 * 1024),
        cost_estimate=BRIEF,
        name="inner_back",
    )(*scalars, k, v, a, kseg, q, do, o, lse, qseg, weight, x_own, order, gain_grad, *partial, *deps)


def middle_kernel(x_ref, o_ref, dz_ref, gain_ref, order_ref, wo_ref, wh_ref, wp_ref,
                  out_ref, keep_ref, send_ref, dx_ref, do_ref, gg_ref,
                  normed, inverse, second, ordered, acc, dsec):
    step = pl.program_id(0)
    steps = pl.num_programs(0)
    width = x_ref.shape[1]
    half = width // 2

    @pl.when(step == 0)
    def _():
        value = x_ref[...].astype(f32) + dot(o_ref[...], wo_ref[...])
        acc[...] = value
        n, r = normalize_parts(value)
        normed[...] = n
        inverse[...] = jnp.broadcast_to(r, inverse.shape)
        b = (n * gain_ref[1:2, :]).astype(bf)
        second[...] = b
        ordered[...] = dot(b, order_ref[...]).astype(bf)
        dsec[...] = jnp.zeros(dsec.shape, f32)

    dz = dz_ref[...]
    wh = wh_ref[...]
    wp = wp_ref[...]
    u = dot(second[...], wh)
    cdf = 0.5 * (1.0 + lax.erf(u * (0.5 ** 0.5)))
    pdf = jnp.exp(-0.5 * u * u) * 0.3989422804014327
    hid = (u * cdf).astype(bf)
    du = (contract_cols(dz, wp) * (cdf + u * pdf)).astype(bf)
    acc[...] += dot(hid, wp)

    def put(number, grad):
        at = pl.ds(pl.multiple_of(number * width, 128), width)
        grad = grad.astype(bf)
        keep_ref[:, at] = grad[:half]
        send_ref[:, at] = grad[half:]

    put(step, contract_rows(ordered[...], du))
    put(steps + step, contract_rows(dot(hid, order_ref[...]).astype(bf), dz))
    dsec[...] += contract_cols(du, wh)

    @pl.when(step == steps - 1)
    def _():
        out_ref[...] = acc[...].astype(bf)
        n = normed[...]
        db = dsec[...]
        gg_ref[...] = jnp.broadcast_to(jnp.sum(db * n, axis=0, keepdims=True), gg_ref.shape)
        dx = dz.astype(f32) + normalize_back(db, n, inverse[:, 0:1], gain_ref[1:2, :])
        dx_ref[...] = dx
        dproj = dx.astype(bf)
        put(2 * steps, contract_rows(dot(o_ref[...], order_ref[...]).astype(bf), dproj))
        do_ref[...] = contract_cols(dproj, wo_ref[...]).astype(bf)


def middle(x, o, dz, gains, order, packed):
    rows, width = x.shape
    ratio = (packed.shape[1] - width) // (2 * width)
    whole = pl.BlockSpec(memory_space=pltpu.VMEM)
    line = jax.ShapeDtypeStruct((rows, width), f32)
    low = jax.ShapeDtypeStruct((rows, width), bf)
    message = jax.ShapeDtypeStruct((width // 2, packed.shape[1]), bf)
    return pl.pallas_call(
        middle_kernel,
        grid=(ratio,),
        in_specs=[whole] * 5
        + [
            pl.BlockSpec((width, width), lambda s: (0, 0)),
            pl.BlockSpec((width, width), lambda s: (0, 1 + s)),
            pl.BlockSpec((width, width), lambda s: (0, 1 + ratio + s)),
        ],
        out_specs=[whole] * 6,
        out_shape=[low, message, message, line, low, jax.ShapeDtypeStruct((8, width), f32)],
        scratch_shapes=[
            pltpu.VMEM((rows, width), f32),
            pltpu.VMEM((rows, 128), f32),
            pltpu.VMEM((rows, width), bf),
            pltpu.VMEM((rows, width), bf),
            pltpu.VMEM((rows, width), f32),
            pltpu.VMEM((rows, width), f32),
        ],
        compiler_params=pltpu.CompilerParams(vmem_limit_bytes=62 * 1024 * 1024),
        cost_estimate=BRIEF,
        name="middle",
    )(x, o, dz, gains, order, packed, packed, packed)


def add(*arrays):
    total = arrays[0].astype(f32)
    for array in arrays[1:]:
        total += array.astype(f32)
    return total


class Links:
    def __init__(self, wide):
        self.wide = wide
        self.outer = wide // 4

    def swap(self, array, name):
        if name == "y":
            return lax.ppermute(array, "narrow", [(0, 1), (1, 0)])
        flip = 1 if name == "core" else 2
        return lax.ppermute(array, "wide", [(j, j ^ flip) for j in range(self.wide)])

    def shift(self, array, s):
        perm = [(j, (j + 4 * s) % self.wide) for j in range(self.wide)]
        return lax.ppermute(array, "wide", perm)

    def order(self, width):
        place = lax.axis_index("wide")
        rows = width // (2 * self.wide)
        at = jnp.arange(width, dtype=jnp.int32)
        row, at = at % rows, at // rows
        z, at = (at + place // 4) % self.outer, at // self.outer
        y, at = (at + lax.axis_index("narrow")) % 2, at // 2
        x, at = (at + place // 2) % 2, at // 2
        core = (at + place) % 2
        source = (((z * 2 + x) * 2 + core) * 2 + y) * rows + row
        return (jnp.arange(width, dtype=jnp.int32)[:, None] == source[None, :]).astype(bf)

    def along_z(self, shard):
        parts = [shard] + [self.shift(shard, self.outer - s) for s in range(1, self.outer)]
        return jnp.concatenate(parts, axis=0)

    def along_xy(self, mine):
        cut = halfway(mine)
        one, two = mine[:, :cut], mine[:, cut:]
        one = jnp.concatenate([one, self.swap(one, "x")], axis=0)
        two = jnp.concatenate([two, self.swap(two, "y")], axis=0)
        one = (one, self.swap(one, "y"))
        two = (two, self.swap(two, "x"))
        return (
            one + tuple(self.swap(piece, "core") for piece in one),
            two + tuple(self.swap(piece, "core") for piece in two),
        )

    def first(self, pairs, *deps):
        rows = pairs[0][0].shape[0] // 4
        cuts = [halfway(keep) for keep, _ in pairs]
        wide = [sum(cuts), sum(keep.shape[1] for keep, _ in pairs) - sum(cuts)]

        def kernel(*refs):
            count = 2 * len(pairs)
            keep_x, send_x, keep_y, send_y = refs[-4:]
            at = [0, 0]
            for keep, got, cut in zip(refs[0:count:2], refs[1:count:2], cuts):
                rest = keep.shape[1] - cut
                one, two = slice(0, cut), slice(cut, cut + rest)
                to = slice(at[0], at[0] + cut)
                keep_x[:, to] = add(keep[:2 * rows, one], got[:2 * rows, one]).astype(bf)
                send_x[:, to] = add(keep[2 * rows:, one], got[2 * rows:, one]).astype(bf)
                to = slice(at[1], at[1] + rest)
                for j, out in enumerate((keep_y, send_y, keep_y, send_y)):
                    of = slice(j * rows, (j + 1) * rows)
                    into = slice(j // 2 * rows, (j // 2 + 1) * rows)
                    out[into, to] = add(keep[of, two], got[of, two]).astype(bf)
                at = [at[0] + cut, at[1] + rest]

        shapes = [(2 * rows, wide[0])] * 2 + [(2 * rows, wide[1])] * 2
        keep_x, send_x, keep_y, send_y = stage(kernel, sum(pairs, ()), deps, shapes)
        return (keep_x, keep_y), (self.swap(send_x, "x"), self.swap(send_y, "y"))

    def second(self, keep, got, *deps):
        rows = keep[0].shape[0] // 2

        def kernel(keep_x, keep_y, got_x, got_y, *refs):
            for keep, got, hold, send in ((keep_x, got_x, *refs[-4:-2]), (keep_y, got_y, *refs[-2:])):
                hold[...] = add(keep[:rows], got[:rows]).astype(bf)
                send[...] = add(keep[rows:], got[rows:]).astype(bf)

        shapes = [(rows, keep[0].shape[1])] * 2 + [(rows, keep[1].shape[1])] * 2
        keep_x, send_x, keep_y, send_y = stage(kernel, keep + got, deps, shapes)
        return (keep_x, keep_y), (self.swap(send_x, "y"), self.swap(send_y, "x"))

    def third(self, keep, got, *deps):
        cut = keep[0].shape[1]

        def kernel(keep_x, keep_y, got_x, got_y, *refs):
            refs[-1][:, :cut] = add(keep_x[...], got_x[...]).astype(bf)
            refs[-1][:, cut:] = add(keep_y[...], got_y[...]).astype(bf)

        rows = keep[0].shape[0]
        (total,) = stage(kernel, keep + got, deps, [(rows, cut + keep[1].shape[1])])
        rows = rows // self.outer
        parts = [total[s * rows:(s + 1) * rows] for s in range(self.outer)]
        return total, (parts[0],) + tuple(self.shift(parts[s], s) for s in range(1, self.outer))


def collect(parts, *deps):
    def kernel(*refs):
        refs[-1][...] = add(*(ref[...] for ref in refs[:len(parts)]))

    return stage(kernel, parts, deps, [parts[0].shape], f32)[0]


def stage(kernel, operands, deps, shapes, kind=bf):
    whole = pl.BlockSpec(memory_space=pltpu.VMEM)
    elsewhere = pl.BlockSpec(memory_space=pl.ANY)
    return pl.pallas_call(
        kernel,
        in_specs=[whole] * len(operands) + [elsewhere] * len(deps),
        out_specs=[whole] * len(shapes),
        out_shape=[jax.ShapeDtypeStruct(shape, kind) for shape in shapes],
        compiler_params=pltpu.CompilerParams(vmem_limit_bytes=40 * 1024 * 1024),
        cost_estimate=BRIEF,
        name="stage",
    )(*operands, *deps)


def hold(values, *deps):
    count = len(values)

    def kernel(*refs):
        for source, out in zip(refs[:count], refs[-count:]):
            out[...] = source[...]

    whole = pl.BlockSpec(memory_space=pltpu.VMEM)
    elsewhere = pl.BlockSpec(memory_space=pl.ANY)
    return pl.pallas_call(
        kernel,
        in_specs=[whole] * count + [elsewhere] * len(deps),
        out_specs=[whole] * count,
        out_shape=[jax.ShapeDtypeStruct(v.shape, v.dtype) for v in values],
        cost_estimate=BRIEF,
        name="hold",
    )(*values, *deps)


def halfway(array):
    return (array.shape[1] // 2 + 127) // 128 * 128


def finish_kernel(x_ref, dx_ref, own_ref, other_ref, gain_ref, out_ref):
    n, r = normalize_parts(x_ref[...].astype(f32))
    da = add(own_ref[...], other_ref[...])
    out_ref[...] = (dx_ref[...] + normalize_back(da, n, r, gain_ref[0:1, :])).astype(bf)


def finish(x, dx, own, other, gains):
    rows, width = x.shape
    tile = pl.BlockSpec((QT, width), lambda i: (i, 0))
    return pl.pallas_call(
        finish_kernel,
        grid=(rows // QT,),
        in_specs=[tile] * 4 + [pl.BlockSpec(gains.shape, lambda i: (0, 0))],
        out_specs=tile,
        out_shape=jax.ShapeDtypeStruct((rows, width), bf),
        cost_estimate=BRIEF,
        name="finish",
    )(x, dx, own, other, gains)


def settle_kernel(own_ref, before_ref, behind_ref, partner_ref, fourth_ref, send_ref, *refs):
    own_out, partner_out, send_out = refs[-3:]
    own_out[...] = add(own_ref[...], before_ref[...], behind_ref[...])
    partner_out[...] = add(partner_ref[...], fourth_ref[...]).astype(bf)
    send_out[...] = send_ref[...]


def settle(own, before, behind, partner, fourth, send, *deps):
    whole = pl.BlockSpec(memory_space=pltpu.VMEM)
    return pl.pallas_call(
        settle_kernel,
        in_specs=[whole] * 6 + [pl.BlockSpec(memory_space=pl.ANY)] * len(deps),
        out_specs=[whole] * 3,
        out_shape=[jax.ShapeDtypeStruct(v.shape, v.dtype) for v in (own, partner, send)],
        compiler_params=pltpu.CompilerParams(vmem_limit_bytes=40 * 1024 * 1024),
        cost_estimate=BRIEF,
        name="settle",
    )(own, before, behind, partner, fourth, send, *deps)


def body(
    joint_in,
    cotangent,
    segment_ids,
    layer_index,
    step_index,
    gain_one,
    w_qkv,
    w_attn_out,
    gain_two,
    w_hidden,
    w_proj,
    mom_gain_one,
    mom_qkv,
    mom_attn_out,
    mom_gain_two,
    mom_hidden,
    mom_proj,
):
    rows, width = joint_in.shape
    wide = lax.axis_size("wide")
    both = ("wide", "narrow")
    shard = w_qkv.shape[0]
    hidden = w_hidden.shape[1]
    ratio = hidden // width
    odd = lax.axis_index("narrow")
    place = lax.axis_index("wide") * 2 + odd
    window = 5 * rows
    is_even = odd == 0

    links = Links(wide)
    order = links.order(width)
    gains = jnp.stack([gain_one, gain_two], axis=1)
    gains = jnp.pad(gains, ((0, 0), (0, 126)))
    pack_a = jnp.concatenate([w_qkv.astype(bf), gains.astype(bf)], axis=1)
    hid_order = w_hidden.astype(bf).reshape(shard, width, ratio).transpose(0, 2, 1)
    pack_b = jnp.concatenate(
        [
            w_attn_out.astype(bf),
            hid_order.reshape(shard, hidden),
            w_proj.astype(bf).reshape(shard, hidden),
        ],
        axis=1,
    )

    fill = jnp.full((2 * rows,), -1, jnp.int32)
    ids = jnp.concatenate([fill, segment_ids, fill])
    key_ids = lax.dynamic_slice_in_dim(ids, place * rows, window, 0)
    own_ids = lax.dynamic_slice_in_dim(segment_ids, place * rows, rows, 0)
    tiles = own_ids.reshape(rows // QT, QT)
    kseg = jnp.broadcast_to(key_ids[:, None], (window, QT))
    qseg = jnp.broadcast_to(tiles[:, None, :], (rows // QT, 8, QT))
    origin = (place - 2) * rows
    low = jnp.sum(segment_ids[None, :] < tiles[:, :1], axis=1, dtype=jnp.int32) - origin
    high = jnp.sum(segment_ids[None, :] <= tiles[:, -1:], axis=1, dtype=jnp.int32) - origin
    low = jnp.clip(low, 0, window)
    high = jnp.clip(high, 0, window)
    edges = jnp.arange(window // KT, dtype=jnp.int32)[:, None] * KT
    begin = jnp.sum(high[None, :] <= edges, axis=1, dtype=jnp.int32)
    end = jnp.sum(low[None, :] < edges + KT, axis=1, dtype=jnp.int32)
    span = jnp.stack([low[0] // KT, (high[-1] + KT - 1) // KT])
    scalars = (begin, end, span, odd.reshape(1))

    swap = [(0, 1), (1, 0)]
    up = [(j, j + 1) for j in range(wide - 1)]
    down = [(j + 1, j) for j in range(wide - 1)]
    across = [(2 * j, 2 * j + 2) for j in range(wide - 1)]
    across += [(2 * j + 3, 2 * j + 1) for j in range(wide - 1)]
    across_back = [(t, s) for s, t in across]
    partner = lax.ppermute(joint_in, "narrow", swap)
    before = lax.ppermute(joint_in, "wide", up)
    behind = lax.ppermute(joint_in, "wide", down)
    mine_a = links.along_z(pack_a)
    fourth = lax.ppermute(partner, both, across)
    mine_a, order, kseg = hold((mine_a, order, kseg), qseg, *scalars)
    ones, twos = links.along_xy(mine_a)
    blocks = (before, partner, fourth, behind)
    (pack_b,) = hold((pack_b,), before, mine_a)
    full_b = lax.all_gather(pack_b, both, axis=0, tiled=True)

    weight, gains, a_win, k, v, q, o, lse = attend(
        scalars, blocks, kseg, joint_in, qseg, order, ones, twos
    )

    joint_out, keep_b, send_b, dx, do, gg_b = middle(
        joint_in, o, cotangent, gains, order, full_b
    )
    got_b = links.swap(send_b, "core")
    keep_b, got_b = links.first([(keep_b, got_b)], do)
    args = (scalars, k, v, a_win, kseg, q, do, o, lse, qseg, weight)
    da_before, da_partner, da_fourth, da_behind, *partial = outer_back(*args, blocks, *keep_b)

    keep_b, got_b = links.second(keep_b, got_b, da_before)
    from_fourth = lax.ppermute(da_fourth, both, across_back)
    from_behind = lax.ppermute(da_before, "wide", down)
    from_before = lax.ppermute(da_behind, "wide", up)
    da_own, keep_a, send_a = inner_back(*args, joint_in, order, gg_b, partial, *keep_b)

    total_b, parts_b = links.third(keep_b, got_b, keep_a)
    da_own, da_partner, send_a = settle(
        da_own, from_before, from_behind, da_partner, from_fourth, send_a, total_b
    )
    got_a = links.swap(send_a, "core")
    from_partner = lax.ppermute(da_partner, "narrow", swap)
    keep_a, got_a = links.first([(keep_a, got_a)])
    keep_a, got_a = links.second(keep_a, got_a)
    sum_b = collect(parts_b, *keep_a)
    total_a, parts_a = links.third(keep_a, got_a, sum_b)
    (gains,) = hold((gains,), total_a)
    grad_in = finish(joint_in, dx, da_own, from_partner, gains)

    sum_a = collect(parts_a)
    sum_hid = sum_b[:, :hidden].reshape(shard, ratio, width)
    sum_hid = sum_hid.transpose(0, 2, 1).reshape(shard, hidden)
    sum_proj = sum_b[:, hidden:2 * hidden].reshape(shard * ratio, width)
    sum_out = sum_b[:, 2 * hidden:]
    sum_qkv = sum_a[:, :3 * width]

    rate = base_rate * jnp.power(jnp.float32(decay_rate), (11 - layer_index[0]).astype(f32))
    rate = rate * jnp.power(1.0 - step_index[0].astype(f32) / total_steps, 0.9)
    next_g1 = momentum_rate * mom_gain_one + sum_a[:, 3 * width]
    next_qkv = momentum_rate * mom_qkv + sum_qkv
    next_out = momentum_rate * mom_attn_out + sum_out
    next_g2 = momentum_rate * mom_gain_two + sum_a[:, 3 * width + 1]
    next_hid = momentum_rate * mom_hidden + sum_hid
    next_prj = momentum_rate * mom_proj + sum_proj
    return (
        joint_out,
        grad_in,
        rate * next_g1,
        rate * next_qkv,
        rate * next_out,
        rate * next_g2,
        rate * next_hid,
        rate * next_prj,
        next_g1,
        next_qkv,
        next_out,
        next_g2,
        next_hid,
        next_prj,
    )


def solution(mesh):
    split = P(("wide", "narrow"), None)
    line = P(("wide", "narrow"))
    params = (line, split, split, line, split, split)
    return jax.shard_map(
        body,
        mesh=mesh,
        in_specs=(split, split, P(), P(), P()) + params + params,
        out_specs=(split, split) + params + params,
        check_vma=False,
    )
```

```python
import functools

import jax
import jax.numpy as jnp
from jax import lax
from jax.experimental import pallas as pl
from jax.experimental.pallas import tpu as pltpu
from jax.sharding import PartitionSpec as P

HEAD = 64
PAIR = 2 * HEAD
QT = 128
KT = 320
GROUP = 3
BRIEF = pl.CostEstimate(flops=1, bytes_accessed=1, transcendentals=0)

eps = 1e-06
base_rate = 0.01
decay_rate = 0.65
total_steps = 100000.0
momentum_rate = 0.9

bf = jnp.bfloat16
f32 = jnp.float32


def dot(left, right):
    return jnp.dot(left, right, preferred_element_type=f32)


def contract_rows(left, right):
    return lax.dot_general(
        left, right, (((0,), (0,)), ((), ())), preferred_element_type=f32
    )


def contract_cols(left, right):
    return lax.dot_general(
        left, right, (((1,), (1,)), ((), ())), preferred_element_type=f32
    )


def normalize_parts(values):
    centre = jnp.mean(values, axis=-1, keepdims=True)
    centred = values - centre
    inverse = lax.rsqrt(jnp.mean(centred * centred, axis=-1, keepdims=True) + eps)
    return (centred * inverse, inverse)


def normalize_back(grad_out, normed, inverse, gain):
    grad_normed = grad_out * gain
    inner = grad_normed - jnp.mean(grad_normed, axis=-1, keepdims=True)
    inner = inner - normed * jnp.mean(grad_normed * normed, axis=-1, keepdims=True)
    return inverse * inner


def diag_wide(block):
    row = lax.broadcasted_iota(jnp.int32, block.shape, 0)
    zero = jnp.zeros_like(block)
    return jnp.concatenate(
        [jnp.where(row < HEAD, block, zero), jnp.where(row >= HEAD, block, zero)], axis=1
    )


def diag_tall(block):
    col = lax.broadcasted_iota(jnp.int32, block.shape, 1)
    zero = jnp.zeros_like(block)
    return jnp.concatenate(
        [jnp.where(col < HEAD, block, zero), jnp.where(col >= HEAD, block, zero)], axis=0
    )


def tile_bias(kseg_ref, qseg_ref, t):
    bias = jnp.where(kseg_ref[...] == qseg_ref[t, 0:1, :], 0.0, -1e30).astype(f32)
    return jnp.concatenate([bias, bias], axis=1)


def columns_of(pair):
    return slice(pair * PAIR, (pair + 1) * PAIR)


def copy_rows(odd, step, refs, out):
    for ref, at in zip(refs, block_starts(odd)):
        @pl.when((step >= at) & (step < at + 2))
        def _(ref=ref):
            out[...] = ref[...]


def block_starts(odd):
    return (0, 6 - 4 * odd, 2 + 4 * odd, 8)


def attend_kernel(begin, end, odd, *refs, pieces):
    blocks, (kseg_ref, own_ref, qseg_ref, order_ref) = refs[:4], refs[4:8]
    parts = refs[8:8 + 2 * pieces]
    (w_ref, gains_ref, a_ref, k_ref, v_ref, q_ref, o_ref, lse_ref,
     qbd, top, total, acc, x_ref, rel_ref) = refs[8 + 2 * pieces:]
    step = pl.program_id(0)
    width = x_ref.shape[1]
    pairs = width // PAIR
    tiles = qseg_ref.shape[0]
    scale = HEAD ** (-0.5)

    @pl.when(step == 0)
    def _():
        rows = parts[0].shape[0] // 2
        cut = parts[0].shape[1]
        for j in range(pieces):
            for h in range(2):
                of = slice(h * rows, (h + 1) * rows)
                core, other = j // 2 * 4 * rows, j % 2
                lo = core + (2 * h + other) * rows
                rel_ref[lo:lo + rows, :cut] = parts[j][of, :]
                lo = core + (2 * other + h) * rows
                rel_ref[lo:lo + rows, cut:] = parts[pieces + j][of, :]
        w_ref[...] = dot(order_ref[...], rel_ref[...]).astype(bf)
        gains_ref[...] = w_ref[:, 3 * width:].astype(f32).T[:8]
        n, _ = normalize_parts(own_ref[...].astype(f32))
        q = dot((n * gains_ref[0:1, :]).astype(bf), w_ref[:, :width]).astype(bf)
        q_ref[...] = q
        q = q.astype(f32) * scale
        for t in range(tiles):
            for p in range(pairs):
                qbd[t, p] = diag_wide(q[t * QT:(t + 1) * QT, columns_of(p)].T.astype(bf))
        top[...] = jnp.full(top.shape, -1e30, f32)
        total[...] = jnp.zeros(total.shape, f32)
        acc[...] = jnp.zeros(acc.shape, f32)

    def visit(queries):
        group = [(t, p) for t in queries for p in range(pairs)]
        bias = {i: tile_bias(kseg_ref, qseg_ref, t) for i, t in enumerate(queries)}
        scores = [
            dot(k_ref[:, columns_of(p)], qbd[t, p]) + bias[j // pairs]
            for j, (t, p) in enumerate(group)
        ]
        olds = [top[t, p:p + 1, :] for t, p in group]
        news = [jnp.maximum(old, jnp.max(s, axis=0, keepdims=True)) for old, s in zip(olds, scores)]
        expo = [jnp.exp(s - new) for s, new in zip(scores, news)]
        shrinks = [jnp.exp(old - new) for old, new in zip(olds, news)]
        sums = [
            total[t, p:p + 1, :] * shrink + jnp.sum(e, axis=0, keepdims=True)
            for (t, p), shrink, e in zip(group, shrinks, expo)
        ]
        gots = [
            contract_rows(v_ref[:, columns_of(p)], e.astype(bf)) for (t, p), e in zip(group, expo)
        ]
        for (t, p), new, shrink, summed, got in zip(group, news, shrinks, sums, gots):
            top[t, p:p + 1, :] = new
            total[t, p:p + 1, :] = summed
            lo, mid, hi = p * PAIR, p * PAIR + HEAD, (p + 1) * PAIR
            acc[t, lo:mid, :] = acc[t, lo:mid, :] * shrink[:, :QT] + got[:HEAD, :QT]
            acc[t, mid:hi, :] = acc[t, mid:hi, :] * shrink[:, QT:] + got[HEAD:, QT:]

    def visits(first, last):
        twos = (last - first) // 2

        def two(j, carry):
            visit([first + 2 * j, first + 2 * j + 1])
            return carry

        lax.fori_loop(0, twos, two, 0)

        @pl.when(first + 2 * twos < last)
        def _():
            visit([last - 1])

    @pl.when(begin[step] < end[step])
    def _():
        copy_rows(odd[0], step, blocks, x_ref)

        @pl.when((step >= 4) & (step < 6))
        def _():
            x_ref[...] = own_ref[pl.ds(pl.multiple_of((step - 4) * KT, KT), KT), :]

        n, _ = normalize_parts(x_ref[...].astype(f32))
        a = (n * gains_ref[0:1, :]).astype(bf)
        a_ref[...] = a
        k_ref[...] = dot(a, w_ref[:, width:2 * width]).astype(bf)
        v_ref[...] = dot(a, w_ref[:, 2 * width:3 * width]).astype(bf)
        visits(begin[step], end[step])

    @pl.when(step == pl.num_programs(0) - 1)
    def _():
        for t in range(tiles):
            for p in range(pairs):
                sums = total[t, p:p + 1, :]
                lse_ref[t, p] = top[t, p:p + 1, :] + jnp.log(sums)
                inv = 1.0 / sums
                lo, mid, hi = p * PAIR, p * PAIR + HEAD, (p + 1) * PAIR
                out = jnp.concatenate(
                    [acc[t, lo:mid, :] * inv[:, :QT], acc[t, mid:hi, :] * inv[:, QT:]], axis=0
                )
                o_ref[t * QT:(t + 1) * QT, lo:hi] = out.T.astype(bf)


def block_specs(width, key):
    def spec(number):
        def index(step, begin, end, span, odd):
            return (jnp.clip(key(step) - block_starts(odd[0])[number], 0, 1), 0)

        return pl.BlockSpec((KT, width), index)

    return [spec(number) for number in range(4)]


def attend(scalars, blocks, kseg, x_own, qseg, order, ones, twos):
    rows, width = x_own.shape
    window = 5 * rows
    tiles = rows // QT
    pairs = width // PAIR
    columns = ones[0].shape[1] + twos[0].shape[1]
    whole = pl.BlockSpec(memory_space=pltpu.VMEM)

    def at_used(j, begin, end, span, odd):
        return (jnp.clip(j, span[0], span[1] - 1), 0)

    def kernel(begin, end, span, odd, *refs):
        attend_kernel(begin, end, odd, *refs, pieces=len(ones))

    tile = pl.BlockSpec((KT, width), at_used)
    return pl.pallas_call(
        kernel,
        grid_spec=pltpu.PrefetchScalarGridSpec(
            num_scalar_prefetch=4,
            grid=(window // KT,),
            in_specs=block_specs(width, lambda j: j)
            + [pl.BlockSpec((KT, QT), at_used)]
            + [whole] * (3 + 2 * len(ones)),
            out_specs=[whole, whole, tile, tile, tile, whole, whole, whole],
            scratch_shapes=[
                pltpu.VMEM((tiles, pairs, PAIR, 2 * QT), bf),
                pltpu.VMEM((tiles, 8, 2 * QT), f32),
                pltpu.VMEM((tiles, 8, 2 * QT), f32),
                pltpu.VMEM((tiles, width, QT), f32),
                pltpu.VMEM((KT, width), bf),
                pltpu.VMEM((width, columns), bf),
            ],
        ),
        out_shape=[
            jax.ShapeDtypeStruct((width, columns), bf),
            jax.ShapeDtypeStruct((8, width), f32),
            jax.ShapeDtypeStruct((window, width), bf),
            jax.ShapeDtypeStruct((window, width), bf),
            jax.ShapeDtypeStruct((window, width), bf),
            jax.ShapeDtypeStruct((rows, width), bf),
            jax.ShapeDtypeStruct((rows, width), bf),
            jax.ShapeDtypeStruct((tiles, pairs, 1, 2 * QT), f32),
        ],
        compiler_params=pltpu.CompilerParams(vmem_limit_bytes=56 * 1024 * 1024),
        cost_estimate=BRIEF,
        name="attend",
    )(*scalars, *blocks, kseg, x_own, qseg, order, *ones, *twos)


def back_tile(begin, end, j, refs, scratch):
    k_ref, v_ref, kseg_ref, qseg_ref, lse_ref = refs
    qbd, dobd, qn, don, delta, dq_acc, dk_acc, dv_acc = scratch
    pairs = qbd.shape[1]
    dk_acc[...] = jnp.zeros(dk_acc.shape, f32)
    dv_acc[...] = jnp.zeros(dv_acc.shape, f32)

    def visit(t):
        bias = tile_bias(kseg_ref, qseg_ref, t)
        for base in range(0, pairs, GROUP):
            group = range(base, min(pairs, base + GROUP))
            keys = [k_ref[:, columns_of(p)] for p in group]
            scores = [dot(kp, qbd[t, p]) for kp, p in zip(keys, group)]
            dprobs = [dot(v_ref[:, columns_of(p)], dobd[t, p]) for p in group]
            probs = [jnp.exp(s + bias - lse_ref[t, p]) for s, p in zip(scores, group)]
            ds = [
                (pr * (dp - delta[t, p:p + 1, :])).astype(bf)
                for pr, dp, p in zip(probs, dprobs, group)
            ]
            got_v = [dot(pr.astype(bf), don[t, p]) for pr, p in zip(probs, group)]
            got_k = [dot(d, qn[t, p]) for d, p in zip(ds, group)]
            got_q = [contract_rows(kp, d) for kp, d in zip(keys, ds)]
            for i, p in enumerate(group):
                lo, mid, hi = p * PAIR, p * PAIR + HEAD, (p + 1) * PAIR
                dv_acc[:, lo:hi] += got_v[i]
                dk_acc[:, lo:hi] += got_k[i]
                dq_acc[t, lo:mid, :] += got_q[i][:HEAD, :QT]
                dq_acc[t, mid:hi, :] += got_q[i][HEAD:, QT:]

    first = begin[j]
    twos = (end[j] - first) // 2

    def two(i, carry):
        visit(first + 2 * i)
        visit(first + 2 * i + 1)
        return carry

    lax.fori_loop(0, twos, two, 0)

    @pl.when(first + 2 * twos < end[j])
    def _():
        visit(end[j] - 1)

    return dk_acc[...].astype(bf), dv_acc[...].astype(bf)


def back_prepare(q_ref, do_ref, o_ref, scratch):
    qbd, dobd, qn, don, delta = scratch
    tiles, pairs = qbd.shape[:2]
    scale = HEAD ** (-0.5)
    for t in range(tiles):
        at = slice(t * QT, (t + 1) * QT)
        for p in range(pairs):
            cols = columns_of(p)
            q = q_ref[at, cols].astype(f32) * scale
            do = do_ref[at, cols].astype(f32)
            do_t = do.T
            qbd[t, p] = diag_wide(q.T.astype(bf))
            dobd[t, p] = diag_wide(do_t.astype(bf))
            qn[t, p] = diag_tall(q.astype(bf))
            don[t, p] = diag_tall(do.astype(bf))
            both = do_t * o_ref[at, cols].astype(f32).T
            delta[t, p:p + 1, :QT] = jnp.sum(both[:HEAD], axis=0, keepdims=True)
            delta[t, p:p + 1, QT:] = jnp.sum(both[HEAD:], axis=0, keepdims=True)


def back_share(dk, dv, a, w_ref, acc):
    width = dk.shape[1]
    da = contract_cols(dk, w_ref[:, width:2 * width]) + contract_cols(dv, w_ref[:, 2 * width:3 * width])
    acc[:, :width] += contract_rows(a, dk)
    acc[:, width:] += contract_rows(a, dv)
    return da


def outer_kernel(begin, end, span, odd, k_ref, v_ref, a_ref, kseg_ref, q_ref, do_ref, o_ref,
                 lse_ref, qseg_ref, w_ref, b0, b1, b2, b3, *refs, own):
    da_refs = refs[-15:-11]
    acc_ref, dq_ref, gg_ref, qbd, dobd, qn, don, delta, dk_acc, dv_acc, x_ref = refs[-11:]
    step = pl.program_id(0)
    j = jnp.where(step < own[0], step, step + own[1] - own[0])

    @pl.when(step == 0)
    def _():
        back_prepare(q_ref, do_ref, o_ref, (qbd, dobd, qn, don, delta))
        acc_ref[...] = jnp.zeros(acc_ref.shape, f32)
        dq_ref[...] = jnp.zeros(dq_ref.shape, f32)
        gg_ref[...] = jnp.zeros(gg_ref.shape, f32)

    used = begin[j] < end[j]

    def put(value):
        for ref, at in zip(da_refs, block_starts(odd[0])):
            @pl.when((j >= at) & (j < at + 2))
            def _(ref=ref):
                ref[...] = value

    @pl.when(used)
    def _():
        dk, dv = back_tile(
            begin, end, j, (k_ref, v_ref, kseg_ref, qseg_ref, lse_ref),
            (qbd, dobd, qn, don, delta, dq_ref, dk_acc, dv_acc),
        )
        da = back_share(dk, dv, a_ref[...], w_ref, acc_ref)
        put(da.astype(bf))
        copy_rows(odd[0], j, (b0, b1, b2, b3), x_ref)
        n, _ = normalize_parts(x_ref[...].astype(f32))
        gg_ref[0:1, :] += jnp.sum(da * n, axis=0, keepdims=True)

    @pl.when(jnp.logical_not(used))
    def _():
        put(jnp.zeros(x_ref.shape, bf))


def inner_kernel(begin, end, span, odd, k_ref, v_ref, a_ref, kseg_ref, q_ref, do_ref, o_ref,
                 lse_ref, qseg_ref, w_ref, x_ref, order_ref, gb_ref, acc_in, dq_in, gg_in,
                 *refs, own):
    (da_ref, keep_ref, send_ref,
     qbd, dobd, qn, don, delta, dk_acc, dv_acc, acc, dq_acc, gg, dq_all, a_all) = refs[-15:]
    step = pl.program_id(0)
    width = k_ref.shape[1]
    half = width // 2
    tiles, pairs = qbd.shape[:2]

    @pl.when(step == 0)
    def _():
        back_prepare(q_ref, do_ref, o_ref, (qbd, dobd, qn, don, delta))
        acc[...] = acc_in[...]
        dq_acc[...] = dq_in[...]
        gg[...] = jnp.zeros(gg.shape, f32)
        gg[0:1, :] = gg_in[0:1, :]
        gg[1:2, :] = gb_ref[0:1, :]

    dk, dv = back_tile(
        begin, end, step + own[0], (k_ref, v_ref, kseg_ref, qseg_ref, lse_ref),
        (qbd, dobd, qn, don, delta, dq_acc, dk_acc, dv_acc),
    )
    at = pl.ds(pl.multiple_of(step * KT, KT), KT)
    da_ref[at, :] = back_share(dk, dv, a_ref[...], w_ref, acc)
    a_all[at, :] = a_ref[...]

    @pl.when(step == pl.num_programs(0) - 1)
    def _():
        scale = HEAD ** (-0.5)
        for t in range(tiles):
            for p in range(pairs):
                cols = columns_of(p)
                dq_all[t * QT:(t + 1) * QT, cols] = (dq_acc[t, cols, :] * scale).T.astype(bf)
        dq = dq_all[...]
        da = da_ref[...] + contract_cols(dq, w_ref[:, :width])
        da_ref[...] = da
        n, _ = normalize_parts(x_ref[...].astype(f32))
        gg[0:1, :] += jnp.sum(da * n, axis=0, keepdims=True)
        order = order_ref[...]

        def put(lo, grad):
            both = contract_rows(order, grad.astype(bf)).astype(bf)
            keep_ref[:, lo:lo + both.shape[1]] = both[:half]
            send_ref[:, lo:lo + both.shape[1]] = both[half:]

        put(0, contract_rows(a_all[...], dq))
        put(width, acc[...])
        put(3 * width, gg[...].T)


def back_specs(window, rows, width, own, at_key):
    tiles = rows // QT
    pairs = width // PAIR
    whole = pl.BlockSpec(memory_space=pltpu.VMEM)
    tile = pl.BlockSpec((KT, width), at_key)
    specs = [tile, tile, tile, pl.BlockSpec((KT, QT), at_key)] + [whole] * 6
    scratch = [
        pltpu.VMEM((tiles, pairs, PAIR, 2 * QT), bf),
        pltpu.VMEM((tiles, pairs, PAIR, 2 * QT), bf),
        pltpu.VMEM((tiles, pairs, 2 * QT, PAIR), bf),
        pltpu.VMEM((tiles, pairs, 2 * QT, PAIR), bf),
        pltpu.VMEM((tiles, 8, 2 * QT), f32),
        pltpu.VMEM((KT, width), f32),
        pltpu.VMEM((KT, width), f32),
    ]
    return specs, scratch, whole


def outer_back(scalars, k, v, a, kseg, q, do, o, lse, qseg, weight, blocks, *deps):
    window, width = k.shape
    rows = q.shape[0]
    own = (2 * rows // KT, 3 * rows // KT)
    steps = window // KT - own[1] + own[0]

    def key(step):
        return jnp.where(step < own[0], step, step + own[1] - own[0])

    def at_key(step, begin, end, span, odd):
        return (jnp.clip(key(step), span[0], span[1] - 1), 0)

    specs, scratch, whole = back_specs(window, rows, width, own, at_key)
    return pl.pallas_call(
        functools.partial(outer_kernel, own=own),
        grid_spec=pltpu.PrefetchScalarGridSpec(
            num_scalar_prefetch=4,
            grid=(steps,),
            in_specs=specs
            + block_specs(width, key)
            + [pl.BlockSpec(memory_space=pl.ANY)] * len(deps),
            out_specs=block_specs(width, key) + [whole, whole, whole],
            scratch_shapes=scratch + [pltpu.VMEM((KT, width), bf)],
        ),
        out_shape=[
            *[jax.ShapeDtypeStruct((rows, width), bf)] * 4,
            jax.ShapeDtypeStruct((width, 2 * width), f32),
            jax.ShapeDtypeStruct((rows // QT, width, QT), f32),
            jax.ShapeDtypeStruct((8, width), f32),
        ],
        compiler_params=pltpu.CompilerParams(vmem_limit_bytes=50 * 1024 * 1024),
        cost_estimate=BRIEF,
        name="outer_back",
    )(*scalars, k, v, a, kseg, q, do, o, lse, qseg, weight, *blocks, *deps)


def inner_back(scalars, k, v, a, kseg, q, do, o, lse, qseg, weight, x_own, order, gain_grad,
               partial, *deps):
    window, width = k.shape
    rows = q.shape[0]
    own = (2 * rows // KT, 3 * rows // KT)
    half = width // 2
    columns = weight.shape[1]

    def at_key(step, *_):
        return (step + own[0], 0)

    specs, scratch, whole = back_specs(window, rows, width, own, at_key)
    scratch += [
        pltpu.VMEM((width, 2 * width), f32),
        pltpu.VMEM((rows // QT, width, QT), f32),
        pltpu.VMEM((columns - 3 * width, width), f32),
        pltpu.VMEM((rows, width), bf),
        pltpu.VMEM((rows, width), bf),
    ]
    return pl.pallas_call(
        functools.partial(inner_kernel, own=own),
        grid_spec=pltpu.PrefetchScalarGridSpec(
            num_scalar_prefetch=4,
            grid=(own[1] - own[0],),
            in_specs=specs + [whole] * 6 + [pl.BlockSpec(memory_space=pl.ANY)] * len(deps),
            out_specs=[whole, whole, whole],
            scratch_shapes=scratch,
        ),
        out_shape=[
            jax.ShapeDtypeStruct((rows, width), f32),
            jax.ShapeDtypeStruct((half, columns), bf),
            jax.ShapeDtypeStruct((half, columns), bf),
        ],
        compiler_params=pltpu.CompilerParams(vmem_limit_bytes=46 * 1024 * 1024),
        cost_estimate=BRIEF,
        name="inner_back",
    )(*scalars, k, v, a, kseg, q, do, o, lse, qseg, weight, x_own, order, gain_grad, *partial, *deps)


def middle_kernel(x_ref, o_ref, dz_ref, gain_ref, order_ref, wo_ref, wh_ref, wp_ref,
                  out_ref, hkeep_ref, hsend_ref, pkeep_ref, psend_ref, okeep_ref, osend_ref,
                  dx_ref, do_ref, gg_ref, normed, inverse, second, ordered, acc, dsec):
    step = pl.program_id(0)
    width = x_ref.shape[1]
    half = width // 2

    @pl.when(step == 0)
    def _():
        value = x_ref[...].astype(f32) + dot(o_ref[...], wo_ref[...])
        acc[...] = value
        n, r = normalize_parts(value)
        normed[...] = n
        inverse[...] = jnp.broadcast_to(r, inverse.shape)
        b = (n * gain_ref[1:2, :]).astype(bf)
        second[...] = b
        ordered[...] = dot(b, order_ref[...]).astype(bf)
        dsec[...] = jnp.zeros(dsec.shape, f32)

    dz = dz_ref[...]
    wh = wh_ref[...]
    wp = wp_ref[...]
    u = dot(second[...], wh)
    cdf = 0.5 * (1.0 + lax.erf(u * (0.5 ** 0.5)))
    pdf = jnp.exp(-0.5 * u * u) * 0.3989422804014327
    hid = (u * cdf).astype(bf)
    du = (contract_cols(dz, wp) * (cdf + u * pdf)).astype(bf)
    acc[...] += dot(hid, wp)

    def put(keep_ref, send_ref, grad):
        grad = grad.astype(bf)
        keep_ref[...] = grad[:half]
        send_ref[...] = grad[half:]

    put(hkeep_ref, hsend_ref, contract_rows(ordered[...], du))
    put(pkeep_ref, psend_ref, contract_rows(dot(hid, order_ref[...]).astype(bf), dz))
    dsec[...] += contract_cols(du, wh)

    @pl.when(step == pl.num_programs(0) - 1)
    def _():
        out_ref[...] = acc[...].astype(bf)
        n = normed[...]
        db = dsec[...]
        gg_ref[...] = jnp.broadcast_to(jnp.sum(db * n, axis=0, keepdims=True), gg_ref.shape)
        dx = dz.astype(f32) + normalize_back(db, n, inverse[:, 0:1], gain_ref[1:2, :])
        dx_ref[...] = dx
        dproj = dx.astype(bf)
        put(okeep_ref, osend_ref, contract_rows(dot(o_ref[...], order_ref[...]).astype(bf), dproj))
        do_ref[...] = contract_cols(dproj, wo_ref[...]).astype(bf)


def middle(x, o, dz, gains, order, packed):
    rows, width = x.shape
    ratio = (packed.shape[1] - width) // (2 * width)
    whole = pl.BlockSpec(memory_space=pltpu.VMEM)
    line = jax.ShapeDtypeStruct((rows, width), f32)
    low = jax.ShapeDtypeStruct((rows, width), bf)
    half = width // 2
    part = pl.BlockSpec((half, width), lambda s: (0, s))
    message = jax.ShapeDtypeStruct((half, ratio * width), bf)
    small = jax.ShapeDtypeStruct((half, width), bf)
    return pl.pallas_call(
        middle_kernel,
        grid=(ratio,),
        in_specs=[whole] * 5
        + [
            pl.BlockSpec((width, width), lambda s: (0, 0)),
            pl.BlockSpec((width, width), lambda s: (0, 1 + s)),
            pl.BlockSpec((width, width), lambda s: (0, 1 + ratio + s)),
        ],
        out_specs=[whole] + [part] * 4 + [whole] * 5,
        out_shape=[low] + [message] * 4 + [small, small, line, low, jax.ShapeDtypeStruct((8, width), f32)],
        scratch_shapes=[
            pltpu.VMEM((rows, width), f32),
            pltpu.VMEM((rows, 128), f32),
            pltpu.VMEM((rows, width), bf),
            pltpu.VMEM((rows, width), bf),
            pltpu.VMEM((rows, width), f32),
            pltpu.VMEM((rows, width), f32),
        ],
        compiler_params=pltpu.CompilerParams(vmem_limit_bytes=52 * 1024 * 1024),
        cost_estimate=BRIEF,
        name="middle",
    )(x, o, dz, gains, order, packed, packed, packed)


def add(*arrays):
    total = arrays[0].astype(f32)
    for array in arrays[1:]:
        total += array.astype(f32)
    return total


class Links:
    def __init__(self, wide):
        self.wide = wide
        self.outer = wide // 4

    def swap(self, array, name):
        if name == "y":
            return lax.ppermute(array, "narrow", [(0, 1), (1, 0)])
        flip = 1 if name == "core" else 2
        return lax.ppermute(array, "wide", [(j, j ^ flip) for j in range(self.wide)])

    def flip_z(self, array, s):
        return lax.ppermute(array, "wide", [(j, j ^ (4 * s)) for j in range(self.wide)])

    def distance(self, at):
        bits = self.outer.bit_length() - 1
        return sum(((at >> b) & 1) << (bits - 1 - b) for b in range(bits))

    def order(self, width):
        place = lax.axis_index("wide")
        rows = width // (2 * self.wide)
        at = jnp.arange(width, dtype=jnp.int32)
        row, at = at % rows, at // rows
        z, at = self.distance(at % self.outer) ^ (place // 4), at // self.outer
        y, at = (at + lax.axis_index("narrow")) % 2, at // 2
        x, at = (at + place // 2) % 2, at // 2
        core = (at + place) % 2
        source = (((z * 2 + x) * 2 + core) * 2 + y) * rows + row
        return (jnp.arange(width, dtype=jnp.int32)[:, None] == source[None, :]).astype(bf)

    def along_z(self, shard):
        parts = [shard] + [self.flip_z(shard, self.distance(j)) for j in range(1, self.outer)]
        return jnp.concatenate(parts, axis=0)

    def along_xy(self, mine):
        cut = halfway(mine)
        one, two = mine[:, :cut], mine[:, cut:]
        one = jnp.concatenate([one, self.swap(one, "x")], axis=0)
        two = jnp.concatenate([two, self.swap(two, "y")], axis=0)
        one = (one, self.swap(one, "y"))
        two = (two, self.swap(two, "x"))
        return (
            one + tuple(self.swap(piece, "core") for piece in one),
            two + tuple(self.swap(piece, "core") for piece in two),
        )

    def first(self, pairs, *deps):
        rows = pairs[0][0].shape[0] // 4
        cuts = [halfway(keep) for keep, _ in pairs]
        wide = [sum(cuts), sum(keep.shape[1] for keep, _ in pairs) - sum(cuts)]

        def kernel(*refs):
            count = 2 * len(pairs)
            keep_x, send_x, keep_y, send_y = refs[-4:]
            at = [0, 0]
            for keep, got, cut in zip(refs[0:count:2], refs[1:count:2], cuts):
                rest = keep.shape[1] - cut
                one, two = slice(0, cut), slice(cut, cut + rest)
                to = slice(at[0], at[0] + cut)
                keep_x[:, to] = add(keep[:2 * rows, one], got[:2 * rows, one]).astype(bf)
                send_x[:, to] = add(keep[2 * rows:, one], got[2 * rows:, one]).astype(bf)
                to = slice(at[1], at[1] + rest)
                for j, out in enumerate((keep_y, send_y, keep_y, send_y)):
                    of = slice(j * rows, (j + 1) * rows)
                    into = slice(j // 2 * rows, (j // 2 + 1) * rows)
                    out[into, to] = add(keep[of, two], got[of, two]).astype(bf)
                at = [at[0] + cut, at[1] + rest]

        shapes = [(2 * rows, wide[0])] * 2 + [(2 * rows, wide[1])] * 2
        keep_x, send_x, keep_y, send_y = stage(kernel, sum(pairs, ()), deps, shapes)
        return (keep_x, keep_y), (self.swap(send_x, "x"), self.swap(send_y, "y"))

    def second(self, keep, got, *deps):
        rows = keep[0].shape[0] // 2

        def kernel(keep_x, keep_y, got_x, got_y, *refs):
            for keep, got, hold, send in ((keep_x, got_x, *refs[-4:-2]), (keep_y, got_y, *refs[-2:])):
                hold[...] = add(keep[:rows], got[:rows]).astype(bf)
                send[...] = add(keep[rows:], got[rows:]).astype(bf)

        shapes = [(rows, keep[0].shape[1])] * 2 + [(rows, keep[1].shape[1])] * 2
        keep_x, send_x, keep_y, send_y = stage(kernel, keep + got, deps, shapes)
        return (keep_x, keep_y), (self.swap(send_x, "y"), self.swap(send_y, "x"))

    def third(self, keep, got, *deps):
        cut = keep[0].shape[1]
        rows = keep[0].shape[0] // 2

        def kernel(keep_x, keep_y, got_x, got_y, *refs):
            hold, send = refs[-2:]
            for cols, keep, got in ((slice(0, cut), keep_x, got_x), (slice(cut, None), keep_y, got_y)):
                hold[:, cols] = add(keep[:rows], got[:rows]).astype(bf)
                send[:, cols] = add(keep[rows:], got[rows:]).astype(bf)

        hold, send = stage(kernel, keep + got, deps, [(rows, cut + keep[1].shape[1])] * 2)
        return hold, self.flip_z(send, 1)

    def fourth(self, keep, got, *deps):
        for bit in range(1, self.outer.bit_length() - 1):
            rows = keep.shape[0] // 2
            if rows % 8:
                total = add(keep, got).astype(bf)
                keep, send = total[:rows], total[rows:]
            else:
                keep, send = stage(halves_kernel, (keep, got), deps, [(rows, keep.shape[1])] * 2)
            got = self.flip_z(send, 1 << bit)
        return keep, got


def halves_kernel(keep, got, *refs):
    hold, send = refs[-2:]
    total = add(keep[...], got[...])
    hold[...] = total[:hold.shape[0]].astype(bf)
    send[...] = total[hold.shape[0]:].astype(bf)


def first_kernel(hidk, hidg, projk, projg, outk_x, outg_x, outk_y, outg_y,
                 keep_x, send_x, keep_y, send_y):
    rows = hidk.shape[0] // 4
    last = pl.num_programs(0) - 1

    def write(one, two):
        cols = slice(0, one[0].shape[1])
        keep_x[:, cols] = add(*(v[:2 * rows, :] for v in one)).astype(bf)
        send_x[:, cols] = add(*(v[2 * rows:, :] for v in one)).astype(bf)
        for j, out in enumerate((keep_y, send_y, keep_y, send_y)):
            of = slice(j * rows, (j + 1) * rows)
            out[j // 2 * rows:(j // 2 + 1) * rows, cols] = add(*(v[of, :] for v in two)).astype(bf)

    @pl.when(pl.program_id(0) < last)
    def _():
        write((hidk, hidg), (projk, projg))

    @pl.when(pl.program_id(0) == last)
    def _():
        write((outk_x, outg_x), (outk_y, outg_y))


class Middle:
    def __init__(self, links):
        self.links = links

    def first(self, hid, proj, out):
        rows, columns = hid[0].shape
        block = out[0].shape[1]
        steps = columns // block
        tile = pl.BlockSpec((rows, block), lambda j: (0, jnp.minimum(j, steps - 1)))
        half = [pl.BlockSpec((rows, block // 2), lambda j, at=at: (0, at)) for at in range(2)]
        shape = jax.ShapeDtypeStruct((rows // 2, columns + block // 2), bf)
        keep_x, send_x, keep_y, send_y = pl.pallas_call(
            first_kernel,
            grid=(steps + 1,),
            in_specs=[tile] * 4 + [half[0]] * 2 + [half[1]] * 2,
            out_specs=[pl.BlockSpec((rows // 2, block), lambda j: (0, j))] * 4,
            out_shape=[shape] * 4,
            cost_estimate=BRIEF,
            name="first",
        )(*hid, *proj, *out, *out)
        return (keep_x, keep_y), (self.links.swap(send_x, "x"), self.links.swap(send_y, "y"))

    def second(self, keep, got, *deps):
        rows = keep[0].shape[0] // 4
        cut = keep[0].shape[1]

        def kernel(keep_x, keep_y, got_x, got_y, *refs):
            hold_x, hold_y, send = refs[-3:]
            halves = ((hold_x, slice(0, cut), keep_x, got_x), (hold_y, slice(cut, None), keep_y, got_y))
            for hold, cols, keep, got in halves:
                for j in range(2):
                    into = slice(j * rows, (j + 1) * rows)
                    of = slice(2 * j * rows, (2 * j + 1) * rows)
                    hold[into, :] = add(keep[of, :], got[of, :]).astype(bf)
                    of = slice((2 * j + 1) * rows, (2 * j + 2) * rows)
                    send[into, cols] = add(keep[of, :], got[of, :]).astype(bf)

        wide = keep[1].shape[1]
        shapes = [(2 * rows, cut), (2 * rows, wide), (2 * rows, cut + wide)]
        hold_x, hold_y, send = stage(kernel, keep + got, deps, shapes)
        return (hold_x, hold_y), self.links.flip_z(send, 1)

    def third(self, keep, got, *deps):
        rows = keep[0].shape[0] // 2
        cut = keep[0].shape[1]

        def kernel(keep_x, keep_y, got, *refs):
            for keep, cols, hold, send in (
                (keep_x, slice(0, cut), *refs[-4:-2]), (keep_y, slice(cut, None), *refs[-2:])
            ):
                hold[...] = add(keep[:rows, :], got[:rows, cols]).astype(bf)
                send[...] = add(keep[rows:, :], got[rows:, cols]).astype(bf)

        shapes = [(rows, cut)] * 2 + [(rows, keep[1].shape[1])] * 2
        hold_x, send_x, hold_y, send_y = stage(kernel, keep + (got,), deps, shapes)
        return (hold_x, hold_y), (self.links.swap(send_x, "y"), self.links.swap(send_y, "x"))

    def fourth(self, keep, got, *deps):
        rows = keep[0].shape[0] // 2
        cut = keep[0].shape[1]
        if rows % 8:
            total = jnp.concatenate([add(k, g).astype(bf) for k, g in zip(keep, got)], axis=1)
            hold, send = total[:rows], total[rows:]
        else:
            def kernel(keep_x, keep_y, got_x, got_y, *refs):
                hold, send = refs[-2:]
                for cols, keep, got in ((slice(0, cut), keep_x, got_x), (slice(cut, None), keep_y, got_y)):
                    total = add(keep[...], got[...])
                    hold[:, cols] = total[:rows].astype(bf)
                    send[:, cols] = total[rows:].astype(bf)

            hold, send = stage(kernel, keep + got, deps, [(rows, cut + keep[1].shape[1])] * 2)
        got = self.links.flip_z(send, 2)
        for bit in range(2, self.links.outer.bit_length() - 1):
            total = add(hold, got).astype(bf)
            rows = rows // 2
            hold, send = total[:rows], total[rows:]
            got = self.links.flip_z(send, 1 << bit)
        return hold, got


def collect(parts, *deps):
    def kernel(*refs):
        refs[-1][...] = add(*(ref[...] for ref in refs[:len(parts)]))

    return stage(kernel, parts, deps, [parts[0].shape], f32)[0]


def stage(kernel, operands, deps, shapes, kind=bf):
    whole = pl.BlockSpec(memory_space=pltpu.VMEM)
    elsewhere = pl.BlockSpec(memory_space=pl.ANY)
    return pl.pallas_call(
        kernel,
        in_specs=[whole] * len(operands) + [elsewhere] * len(deps),
        out_specs=[whole] * len(shapes),
        out_shape=[jax.ShapeDtypeStruct(shape, kind) for shape in shapes],
        compiler_params=pltpu.CompilerParams(vmem_limit_bytes=24 * 1024 * 1024),
        cost_estimate=BRIEF,
        name="stage",
    )(*operands, *deps)


def hold(values, *deps):
    count = len(values)

    def kernel(*refs):
        for source, out in zip(refs[:count], refs[-count:]):
            out[...] = source[...]

    whole = pl.BlockSpec(memory_space=pltpu.VMEM)
    elsewhere = pl.BlockSpec(memory_space=pl.ANY)
    return pl.pallas_call(
        kernel,
        in_specs=[whole] * count + [elsewhere] * len(deps),
        out_specs=[whole] * count,
        out_shape=[jax.ShapeDtypeStruct(v.shape, v.dtype) for v in values],
        cost_estimate=BRIEF,
        name="hold",
    )(*values, *deps)


def halfway(array):
    return (array.shape[1] // 2 + 127) // 128 * 128


def finish_kernel(x_ref, dx_ref, da_ref, gain_ref, out_ref):
    n, r = normalize_parts(x_ref[...].astype(f32))
    out_ref[...] = (dx_ref[...] + normalize_back(da_ref[...], n, r, gain_ref[0:1, :])).astype(bf)


def finish(x, dx, da, gains):
    rows, width = x.shape
    tile = pl.BlockSpec((QT, width), lambda i: (i, 0))
    return pl.pallas_call(
        finish_kernel,
        grid=(rows // QT,),
        in_specs=[tile] * 3 + [pl.BlockSpec(gains.shape, lambda i: (0, 0))],
        out_specs=tile,
        out_shape=jax.ShapeDtypeStruct((rows, width), bf),
        cost_estimate=BRIEF,
        name="finish",
    )(x, dx, da, gains)


def settle_kernel(own_ref, before_ref, partner_ref, across_ref, behind_ref, send_ref, *refs):
    own_out, send_out = refs[-2:]
    own_out[...] = add(*(r[...] for r in (own_ref, before_ref, partner_ref, across_ref, behind_ref)))
    send_out[...] = send_ref[...]


def settle(own, others, send, *deps):
    whole = pl.BlockSpec(memory_space=pltpu.VMEM)
    return pl.pallas_call(
        settle_kernel,
        in_specs=[whole] * 6 + [pl.BlockSpec(memory_space=pl.ANY)] * len(deps),
        out_specs=[whole] * 2,
        out_shape=[jax.ShapeDtypeStruct(v.shape, v.dtype) for v in (own, send)],
        compiler_params=pltpu.CompilerParams(vmem_limit_bytes=24 * 1024 * 1024),
        cost_estimate=BRIEF,
        name="settle",
    )(own, *others, send, *deps)


def update_kernel(rate_ref, sum_ref, hid_ref, proj_ref, mom_out, mom_hid, mom_proj,
                  step_out, step_hid, step_proj, next_out, next_hid, next_proj):
    rate = rate_ref[0]
    hidden = hid_ref.shape[1]
    width = mom_out.shape[1]
    half = width // 2
    far = hidden + half

    def put(step, following, at, momentum, grad):
        value = momentum_rate * momentum + grad
        following[at] = value
        step[at] = rate * value

    whole = slice(None)
    put(step_hid, next_hid, (whole, whole), mom_hid[...], hid_ref[...])
    for at, lo in ((slice(0, half), hidden), (slice(half, width), far + hidden)):
        put(step_out, next_out, (whole, at), mom_out[:, at], sum_ref[:, lo:lo + half])
    put(step_proj, next_proj, (whole, whole), mom_proj[...], proj_ref[...])


def update(rate, total, hid, proj, mom_out, mom_hid, mom_proj):
    whole = pl.BlockSpec(memory_space=pltpu.VMEM)
    moms = (mom_out, mom_hid, mom_proj)
    return pl.pallas_call(
        update_kernel,
        in_specs=[pl.BlockSpec(memory_space=pltpu.SMEM)] + [whole] * 6,
        out_specs=[whole] * 6,
        out_shape=[jax.ShapeDtypeStruct(m.shape, f32) for m in moms + moms],
        cost_estimate=BRIEF,
        name="update",
    )(rate, total, hid, proj, *moms)


def update_first_kernel(rate_ref, keep_ref, got_ref, mom_ref, step_ref, next_ref, gain_ref):
    total = add(keep_ref[...], got_ref[...])
    columns = mom_ref.shape[1]
    value = momentum_rate * mom_ref[...] + total[:, :columns]
    next_ref[...] = value
    step_ref[...] = rate_ref[0] * value
    gain_ref[...] = total[:, columns:]


def update_first(rate, keep, got, mom, *deps):
    whole = pl.BlockSpec(memory_space=pltpu.VMEM)
    rest = jax.ShapeDtypeStruct((mom.shape[0], keep.shape[1] - mom.shape[1]), f32)
    return pl.pallas_call(
        update_first_kernel,
        in_specs=[pl.BlockSpec(memory_space=pltpu.SMEM)] + [whole] * 3,
        out_specs=[whole] * 3,
        out_shape=[jax.ShapeDtypeStruct(mom.shape, f32)] * 2 + [rest],
        cost_estimate=BRIEF,
        name="update_first",
    )(rate, keep, got, mom)


def body(
    joint_in,
    cotangent,
    segment_ids,
    layer_index,
    step_index,
    gain_one,
    w_qkv,
    w_attn_out,
    gain_two,
    w_hidden,
    w_proj,
    mom_gain_one,
    mom_qkv,
    mom_attn_out,
    mom_gain_two,
    mom_hidden,
    mom_proj,
):
    rows, width = joint_in.shape
    wide = lax.axis_size("wide")
    both = ("wide", "narrow")
    shard = w_qkv.shape[0]
    hidden = w_hidden.shape[1]
    ratio = hidden // width
    odd = lax.axis_index("narrow")
    place = lax.axis_index("wide") * 2 + odd
    window = 5 * rows
    is_even = odd == 0

    links = Links(wide)
    order = links.order(width)
    gains = jnp.stack([gain_one, gain_two], axis=1)
    gains = jnp.pad(gains, ((0, 0), (0, 126)))
    pack_a = jnp.concatenate([w_qkv.astype(bf), gains.astype(bf)], axis=1)
    hid_order = w_hidden.astype(bf).reshape(shard, width, ratio).transpose(0, 2, 1)
    pack_b = jnp.concatenate(
        [
            w_attn_out.astype(bf),
            hid_order.reshape(shard, hidden),
            w_proj.astype(bf).reshape(shard, hidden),
        ],
        axis=1,
    )

    fill = jnp.full((2 * rows,), -1, jnp.int32)
    ids = jnp.concatenate([fill, segment_ids, fill])
    key_ids = lax.dynamic_slice_in_dim(ids, place * rows, window, 0)
    own_ids = lax.dynamic_slice_in_dim(segment_ids, place * rows, rows, 0)
    tiles = own_ids.reshape(rows // QT, QT)
    kseg = jnp.broadcast_to(key_ids[:, None], (window, QT))
    qseg = jnp.broadcast_to(tiles[:, None, :], (rows // QT, 8, QT))
    origin = (place - 2) * rows
    low = jnp.sum(segment_ids[None, :] < tiles[:, :1], axis=1, dtype=jnp.int32) - origin
    high = jnp.sum(segment_ids[None, :] <= tiles[:, -1:], axis=1, dtype=jnp.int32) - origin
    low = jnp.clip(low, 0, window)
    high = jnp.clip(high, 0, window)
    edges = jnp.arange(window // KT, dtype=jnp.int32)[:, None] * KT
    begin = jnp.sum(high[None, :] <= edges, axis=1, dtype=jnp.int32)
    end = jnp.sum(low[None, :] < edges + KT, axis=1, dtype=jnp.int32)
    span = jnp.stack([low[0] // KT, (high[-1] + KT - 1) // KT])
    scalars = (begin, end, span, odd.reshape(1))

    swap = [(0, 1), (1, 0)]
    up = [(j, j + 1) for j in range(wide - 1)]
    down = [(j + 1, j) for j in range(wide - 1)]
    across = [(2 * j, 2 * j + 2) for j in range(wide - 1)]
    across += [(2 * j + 3, 2 * j + 1) for j in range(wide - 1)]
    partner = lax.ppermute(joint_in, "narrow", swap)
    before = lax.ppermute(joint_in, "wide", up)
    behind = lax.ppermute(joint_in, "wide", down)
    mine_a = links.along_z(pack_a)
    fourth = lax.ppermute(partner, both, across)
    (mine_a,) = hold((mine_a,), order, kseg, qseg, *scalars)
    ones, twos = links.along_xy(mine_a)
    blocks = (before, partner, fourth, behind)
    (pack_b,) = hold((pack_b,), before, partner, behind, mine_a)
    full_b = lax.all_gather(pack_b, both, axis=0, tiled=True)

    weight, gains, a_win, k, v, q, o, lse = attend(
        scalars, blocks, kseg, joint_in, qseg, order, ones, twos
    )

    joint_out, hid_keep, hid_send, proj_keep, proj_send, out_keep, out_send, dx, do, gg_b = middle(
        joint_in, o, cotangent, gains, order, full_b
    )
    chain = Middle(links)
    keep_b, got_b = chain.first(
        (hid_keep, links.swap(hid_send, "core")),
        (proj_keep, links.swap(proj_send, "core")),
        (out_keep, links.swap(out_send, "core")),
    )
    args = (scalars, k, v, a_win, kseg, q, do, o, lse, qseg, weight)
    da_before, da_partner, da_fourth, da_behind, *partial = outer_back(*args, blocks, *keep_b)

    keep_b, got_b = chain.second(keep_b, got_b, da_before)
    home = [(2 * j + 2, 2 * j + 1) for j in range(wide - 1)]
    home += [(t, s) for s, t in home]
    others = (
        lax.ppermute(da_before, "wide", down),
        lax.ppermute(da_partner, "narrow", swap),
        lax.ppermute(da_fourth, both, home),
        lax.ppermute(da_behind, "wide", up),
    )
    da_own, keep_a, send_a = inner_back(*args, joint_in, order, gg_b, partial, *keep_b)

    keep_b, got_b = chain.third(keep_b, got_b, keep_a)
    da_own, send_a = settle(da_own, others, send_a, *keep_b)
    got_a = links.swap(send_a, "core")
    keep_a, got_a = links.first([(keep_a, got_a)])
    (gains,) = hold((gains,), *keep_a)
    grad_in = finish(joint_in, dx, da_own, gains)
    keep_a, got_a = links.second(keep_a, got_a, grad_in)
    keep_b, got_b = chain.fourth(keep_b, got_b, *keep_a)
    keep_a, got_a = links.third(keep_a, got_a, keep_b)
    keep_a, got_a = links.fourth(keep_a, got_a)
    sum_b = collect((keep_b, got_b), keep_a)

    rate = base_rate * jnp.power(jnp.float32(decay_rate), (11 - layer_index).astype(f32))
    rate = rate * jnp.power(1.0 - step_index.astype(f32) / total_steps, 0.9)
    sum_hid = sum_b[:, :hidden].reshape(shard, ratio, width).transpose(0, 2, 1)
    sum_hid = sum_hid.reshape(shard, hidden)
    far = hidden + width // 2
    sum_proj = sum_b[:, far:far + hidden].reshape(shard * ratio, width)
    step_out, step_hid, step_proj, next_out, next_hid, next_proj = update(
        rate, sum_b, sum_hid, sum_proj, mom_attn_out, mom_hidden, mom_proj
    )
    step_qkv, next_qkv, sum_gains = update_first(rate, keep_a, got_a, mom_qkv)
    next_g1 = momentum_rate * mom_gain_one + sum_gains[:, 0]
    next_g2 = momentum_rate * mom_gain_two + sum_gains[:, 1]
    return (
        joint_out,
        grad_in,
        rate * next_g1,
        step_qkv,
        step_out,
        rate * next_g2,
        step_hid,
        step_proj,
        next_g1,
        next_qkv,
        next_out,
        next_g2,
        next_hid,
        next_proj,
    )


def solution(mesh):
    split = P(("wide", "narrow"), None)
    line = P(("wide", "narrow"))
    params = (line, split, split, line, split, split)
    return jax.shard_map(
        body,
        mesh=mesh,
        in_specs=(split, split, P(), P(), P()) + params + params,
        out_specs=(split, split) + params + params,
        check_vma=False,
    )
```

```python
import functools

import jax
import jax.numpy as jnp
from jax import lax
from jax.experimental import pallas as pl
from jax.experimental.pallas import tpu as pltpu
from jax.sharding import PartitionSpec as P

HEAD = 64
PAIR = 2 * HEAD
QT = 128
OWN = 320
OUTER = 256
GROUP = 3
BRIEF = pl.CostEstimate(flops=1, bytes_accessed=1, transcendentals=0)

eps = 1e-06
base_rate = 0.01
decay_rate = 0.65
total_steps = 100000.0
momentum_rate = 0.9

bf = jnp.bfloat16
f32 = jnp.float32


def dot(left, right):
    return jnp.dot(left, right, preferred_element_type=f32)


def contract_rows(left, right):
    return lax.dot_general(
        left, right, (((0,), (0,)), ((), ())), preferred_element_type=f32
    )


def contract_cols(left, right):
    return lax.dot_general(
        left, right, (((1,), (1,)), ((), ())), preferred_element_type=f32
    )


def normalize_parts(values):
    centre = jnp.mean(values, axis=-1, keepdims=True)
    centred = values - centre
    inverse = lax.rsqrt(jnp.mean(centred * centred, axis=-1, keepdims=True) + eps)
    return (centred * inverse, inverse)


def normalize_back(grad_out, normed, inverse, gain):
    grad_normed = grad_out * gain
    inner = grad_normed - jnp.mean(grad_normed, axis=-1, keepdims=True)
    inner = inner - normed * jnp.mean(grad_normed * normed, axis=-1, keepdims=True)
    return inverse * inner


def diag_wide(block):
    row = lax.broadcasted_iota(jnp.int32, block.shape, 0)
    zero = jnp.zeros_like(block)
    return jnp.concatenate(
        [jnp.where(row < HEAD, block, zero), jnp.where(row >= HEAD, block, zero)], axis=1
    )


def diag_tall(block):
    col = lax.broadcasted_iota(jnp.int32, block.shape, 1)
    zero = jnp.zeros_like(block)
    return jnp.concatenate(
        [jnp.where(col < HEAD, block, zero), jnp.where(col >= HEAD, block, zero)], axis=0
    )


def tile_bias(segments, qseg_ref, t):
    bias = jnp.where(segments == qseg_ref[t, 0:1, :], 0.0, -1e30).astype(f32)
    return jnp.concatenate([bias, bias], axis=1)


def columns_of(pair):
    return slice(pair * PAIR, (pair + 1) * PAIR)


def block_starts(odd, size):
    return (0, (2 - odd) * size, (1 + odd) * size, 3 * size)


def pieces_of(tile, odd, refs, size):
    for part in range(OUTER // QT):
        at = tile * (OUTER // QT) + part
        for ref, start in zip(refs, block_starts(odd, size)):
            yield (at >= start) & (at < start + size), ref, at - start, part


def copy_rows(tile, odd, refs, size, out):
    for number, (here, _, _, part) in enumerate(pieces_of(tile, odd, refs[:4], size)):
        ref = refs[number]

        @pl.when(here)
        def _(ref=ref, part=part):
            out[part * QT:(part + 1) * QT, :] = ref[...]


def block_specs(width, size, key):
    def spec(part, number):
        def index(step, begin, end, span, odd, places):
            at = key(step) * (OUTER // QT) + part
            return (jnp.clip(at - block_starts(odd[0], size)[number], 0, size - 1), 0)

        return pl.BlockSpec((QT, width), index)

    return [spec(part, number) for part in range(OUTER // QT) for number in range(4)]


def in_pairs(first, last, visit):
    twos = (last - first) // 2

    def two(j, carry):
        visit([first + 2 * j, first + 2 * j + 1])
        return carry

    lax.fori_loop(0, twos, two, 0)

    @pl.when(first + 2 * twos < last)
    def _():
        visit([last - 1])


def attend_kernel(begin, end, span, odd, places, *refs, pieces):
    count = 4 * OUTER // QT
    blocks, (kseg_ref, oseg_ref, own_ref, qseg_ref, order_ref) = refs[:count], refs[count:count + 5]
    parts = refs[count + 5:count + 5 + 2 * pieces]
    (w_ref, gains_ref, ao_ref, ko_ref, vo_ref, a_ref, k_ref, v_ref, q_ref, o_ref, lse_ref,
     qbd, top, total, acc, x_ref, rel_ref) = refs[count + 5 + 2 * pieces:]
    step = pl.program_id(0)
    rows, width = own_ref.shape
    pairs = width // PAIR
    tiles = qseg_ref.shape[0]
    scale = HEAD ** (-0.5)

    def project(x):
        n, _ = normalize_parts(x.astype(f32))
        a = (n * gains_ref[0:1, :]).astype(bf)
        k = dot(a, w_ref[:, width:2 * width]).astype(bf)
        return a, k, dot(a, w_ref[:, 2 * width:3 * width]).astype(bf)

    def visit(queries, keys, values, segments):
        group = [(t, p) for t in queries for p in range(pairs)]
        bias = [tile_bias(segments, qseg_ref, t) for t in queries]
        scores = [
            dot(keys(columns_of(p)), qbd[t, p]) + bias[j // pairs] for j, (t, p) in enumerate(group)
        ]
        olds = [top[t, p:p + 1, :] for t, p in group]
        news = [jnp.maximum(old, jnp.max(s, axis=0, keepdims=True)) for old, s in zip(olds, scores)]
        expo = [jnp.exp(s - new) for s, new in zip(scores, news)]
        shrinks = [jnp.exp(old - new) for old, new in zip(olds, news)]
        sums = [
            total[t, p:p + 1, :] * shrink + jnp.sum(e, axis=0, keepdims=True)
            for (t, p), shrink, e in zip(group, shrinks, expo)
        ]
        gots = [
            contract_rows(values(columns_of(p)), e.astype(bf)) for (t, p), e in zip(group, expo)
        ]
        for (t, p), new, shrink, summed, got in zip(group, news, shrinks, sums, gots):
            top[t, p:p + 1, :] = new
            total[t, p:p + 1, :] = summed
            lo, mid, hi = p * PAIR, p * PAIR + HEAD, (p + 1) * PAIR
            acc[t, lo:mid, :] = acc[t, lo:mid, :] * shrink[:, :QT] + got[:HEAD, :QT]
            acc[t, mid:hi, :] = acc[t, mid:hi, :] * shrink[:, QT:] + got[HEAD:, QT:]

    @pl.when(step == 0)
    def _():
        size = parts[0].shape[0] // 2
        cut = parts[0].shape[1]
        shard = size // (places.shape[0] // 8)
        halves = (slice(0, cut), slice(cut, rel_ref.shape[1]))
        for j in range(pieces):
            for h in range(2):
                of = slice(h * size, (h + 1) * size)
                core, other = j // 2 * 4, j % 2
                for block, cols, part in (
                    (core + 2 * h + other, halves[0], parts[j]),
                    (core + 2 * other + h, halves[1], parts[pieces + j]),
                ):
                    value = part[of, :].astype(f32)
                    if shard % 8:
                        rel_ref[block * size:(block + 1) * size, cols] = value
                        continue
                    for z in range(size // shard):
                        to = pl.multiple_of(places[block * (size // shard) + z] * shard, 8)
                        rel_ref[pl.ds(to, shard), cols] = value[z * shard:(z + 1) * shard]
        if shard % 8:
            w_ref[...] = dot(order_ref[...], rel_ref[...].astype(bf)).astype(bf)
        else:
            w_ref[...] = rel_ref[...].astype(bf)
        gains_ref[...] = w_ref[:, 3 * width:].astype(f32).T[:8]
        a, k, v = project(own_ref[...])
        ao_ref[...] = a
        ko_ref[...] = k
        vo_ref[...] = v
        q = dot(a, w_ref[:, :width]).astype(bf)
        q_ref[...] = q
        q = q.astype(f32) * scale
        for t in range(tiles):
            for p in range(pairs):
                qbd[t, p] = diag_wide(q[t * QT:(t + 1) * QT, columns_of(p)].T.astype(bf))
        top[...] = jnp.full(top.shape, -1e30, f32)
        total[...] = jnp.zeros(total.shape, f32)
        acc[...] = jnp.zeros(acc.shape, f32)

        def own(h, carry):
            at = pl.ds(pl.multiple_of(h * OWN, OWN), OWN)
            in_pairs(
                begin[h], end[h],
                lambda ts: visit(
                    ts, lambda c: ko_ref[at, c], lambda c: vo_ref[at, c], oseg_ref[at, :]
                ),
            )
            return carry

        lax.fori_loop(0, rows // OWN, own, 0)

    number = step - 1 + rows // OWN

    @pl.when((step > 0) & (begin[number] < end[number]))
    def _():
        copy_rows(step - 1, odd[0], blocks, rows // QT, x_ref)
        a, k, v = project(x_ref[...])
        a_ref[...] = a
        k_ref[...] = k
        v_ref[...] = v
        in_pairs(
            begin[number], end[number],
            lambda ts: visit(ts, lambda c: k_ref[:, c], lambda c: v_ref[:, c], kseg_ref[...]),
        )

    @pl.when(step == pl.num_programs(0) - 1)
    def _():
        for t in range(tiles):
            for p in range(pairs):
                sums = total[t, p:p + 1, :]
                lse_ref[t, p] = top[t, p:p + 1, :] + jnp.log(sums)
                inv = 1.0 / sums
                lo, mid, hi = p * PAIR, p * PAIR + HEAD, (p + 1) * PAIR
                out = jnp.concatenate(
                    [acc[t, lo:mid, :] * inv[:, :QT], acc[t, mid:hi, :] * inv[:, QT:]], axis=0
                )
                o_ref[t * QT:(t + 1) * QT, lo:hi] = out.T.astype(bf)


def attend(scalars, blocks, kseg, oseg, x_own, qseg, order, ones, twos):
    rows, width = x_own.shape
    outer = 4 * rows
    tiles = rows // QT
    pairs = width // PAIR
    columns = ones[0].shape[1] + twos[0].shape[1]
    whole = pl.BlockSpec(memory_space=pltpu.VMEM)

    def at_used(step, begin, end, span, odd, places):
        return (jnp.clip(step - 1, span[0], span[1]), 0)

    tile = pl.BlockSpec((OUTER, width), at_used)
    own = jax.ShapeDtypeStruct((rows, width), bf)
    far = jax.ShapeDtypeStruct((outer, width), bf)
    return pl.pallas_call(
        functools.partial(attend_kernel, pieces=len(ones)),
        grid_spec=pltpu.PrefetchScalarGridSpec(
            num_scalar_prefetch=5,
            grid=(1 + outer // OUTER,),
            in_specs=block_specs(width, rows // QT, lambda step: step - 1)
            + [pl.BlockSpec((OUTER, QT), at_used)]
            + [whole] * (4 + 2 * len(ones)),
            out_specs=[whole] * 5 + [tile] * 3 + [whole] * 3,
            scratch_shapes=[
                pltpu.VMEM((tiles, pairs, PAIR, 2 * QT), bf),
                pltpu.VMEM((tiles, 8, 2 * QT), f32),
                pltpu.VMEM((tiles, 8, 2 * QT), f32),
                pltpu.VMEM((tiles, width, QT), f32),
                pltpu.VMEM((OUTER, width), bf),
                pltpu.VMEM((width, columns), f32),
            ],
        ),
        out_shape=[
            jax.ShapeDtypeStruct((width, columns), bf),
            jax.ShapeDtypeStruct((8, width), f32),
            own,
            own,
            own,
            far,
            far,
            far,
            own,
            own,
            jax.ShapeDtypeStruct((tiles, pairs, 1, 2 * QT), f32),
        ],
        compiler_params=pltpu.CompilerParams(vmem_limit_bytes=56 * 1024 * 1024),
        cost_estimate=BRIEF,
        name="attend",
    )(*scalars, *(blocks * (OUTER // QT)), kseg, oseg, x_own, qseg, order, *ones, *twos)


def back_tile(first, last, refs, scratch):
    k_ref, v_ref, kseg_ref, qseg_ref, lse_ref = refs
    qbd, dobd, qn, don, delta, dq_acc, dk_acc, dv_acc = scratch
    pairs = qbd.shape[1]
    dk_acc[...] = jnp.zeros(dk_acc.shape, f32)
    dv_acc[...] = jnp.zeros(dv_acc.shape, f32)

    def visit(t):
        bias = tile_bias(kseg_ref[...], qseg_ref, t)
        for base in range(0, pairs, GROUP):
            group = range(base, min(pairs, base + GROUP))
            keys = [k_ref[:, columns_of(p)] for p in group]
            scores = [dot(kp, qbd[t, p]) for kp, p in zip(keys, group)]
            dprobs = [dot(v_ref[:, columns_of(p)], dobd[t, p]) for p in group]
            probs = [jnp.exp(s + bias - lse_ref[t, p]) for s, p in zip(scores, group)]
            ds = [
                (pr * (dp - delta[t, p:p + 1, :])).astype(bf)
                for pr, dp, p in zip(probs, dprobs, group)
            ]
            got_v = [dot(pr.astype(bf), don[t, p]) for pr, p in zip(probs, group)]
            got_k = [dot(d, qn[t, p]) for d, p in zip(ds, group)]
            got_q = [contract_rows(kp, d) for kp, d in zip(keys, ds)]
            for i, p in enumerate(group):
                lo, mid, hi = p * PAIR, p * PAIR + HEAD, (p + 1) * PAIR
                dv_acc[:, lo:hi] += got_v[i]
                dk_acc[:, lo:hi] += got_k[i]
                dq_acc[t, lo:mid, :] += got_q[i][:HEAD, :QT]
                dq_acc[t, mid:hi, :] += got_q[i][HEAD:, QT:]

    def visits(ts):
        for t in ts:
            visit(t)

    in_pairs(first, last, visits)
    return dk_acc[...].astype(bf), dv_acc[...].astype(bf)


def back_prepare(q_ref, do_ref, o_ref, scratch):
    qbd, dobd, qn, don, delta = scratch
    tiles, pairs = qbd.shape[:2]
    scale = HEAD ** (-0.5)
    for t in range(tiles):
        at = slice(t * QT, (t + 1) * QT)
        for p in range(pairs):
            cols = columns_of(p)
            q = q_ref[at, cols].astype(f32) * scale
            do = do_ref[at, cols].astype(f32)
            do_t = do.T
            qbd[t, p] = diag_wide(q.T.astype(bf))
            dobd[t, p] = diag_wide(do_t.astype(bf))
            qn[t, p] = diag_tall(q.astype(bf))
            don[t, p] = diag_tall(do.astype(bf))
            both = do_t * o_ref[at, cols].astype(f32).T
            delta[t, p:p + 1, :QT] = jnp.sum(both[:HEAD], axis=0, keepdims=True)
            delta[t, p:p + 1, QT:] = jnp.sum(both[HEAD:], axis=0, keepdims=True)


def back_input(w_ref, *grads):
    width = w_ref.shape[0]
    total = 0.0
    for number, grad in grads:
        total += contract_cols(grad, w_ref[:, number * width:(number + 1) * width])
    return total


def back_weights(dk, dv, a, acc, lo):
    width = dk.shape[1]
    acc[:, lo:lo + width] += contract_rows(a, dk)
    acc[:, lo + width:lo + 2 * width] += contract_rows(a, dv)


def outer_kernel(begin, end, span, odd, places, k_ref, v_ref, a_ref, kseg_ref, q_ref, do_ref, o_ref,
                 lse_ref, qseg_ref, w_ref, *refs):
    da_refs = refs[-13:-9]
    acc_ref, dq_ref, qbd, dobd, qn, don, delta, dk_acc, dv_acc = refs[-9:]
    step = pl.program_id(0)
    size = q_ref.shape[0] // QT
    number = step + q_ref.shape[0] // OWN

    @pl.when(step == 0)
    def _():
        back_prepare(q_ref, do_ref, o_ref, (qbd, dobd, qn, don, delta))
        acc_ref[...] = jnp.zeros(acc_ref.shape, f32)
        dq_ref[...] = jnp.zeros(dq_ref.shape, f32)

    used = begin[number] < end[number]

    def put(value):
        for here, ref, at, part in pieces_of(step, odd[0], da_refs, size):
            @pl.when(here)
            def _(ref=ref, at=at, part=part):
                ref[pl.ds(pl.multiple_of(at * QT, QT), QT), :] = value[part * QT:(part + 1) * QT]

    @pl.when(used)
    def _():
        dk, dv = back_tile(
            begin[number], end[number], (k_ref, v_ref, kseg_ref, qseg_ref, lse_ref),
            (qbd, dobd, qn, don, delta, dq_ref, dk_acc, dv_acc),
        )
        back_weights(dk, dv, a_ref[...], acc_ref, 0)
        put(back_input(w_ref, (1, dk), (2, dv)).astype(bf))

    @pl.when(jnp.logical_not(used))
    def _():
        put(jnp.zeros(k_ref.shape, bf))


def inner_kernel(begin, end, span, odd, places, k_ref, v_ref, a_ref, kseg_ref, q_ref, do_ref, o_ref,
                 lse_ref, qseg_ref, order_ref, acc_in, dq_in, *refs):
    (dk_ref, dv_ref, dq_ref, keep_ref, send_ref, token_ref,
     qbd, dobd, qn, don, delta, dk_acc, dv_acc, acc, dq_acc, a_all) = refs[-16:]
    step = pl.program_id(0)
    width = k_ref.shape[1]
    half = width // 2
    tiles, pairs = qbd.shape[:2]

    @pl.when(step == 0)
    def _():
        back_prepare(q_ref, do_ref, o_ref, (qbd, dobd, qn, don, delta))
        token_ref[...] = jnp.zeros(token_ref.shape, f32)
        acc[:, width:3 * width] = acc_in[...]
        dq_acc[...] = dq_in[...]

    dk, dv = back_tile(
        begin[step], end[step], (k_ref, v_ref, kseg_ref, qseg_ref, lse_ref),
        (qbd, dobd, qn, don, delta, dq_acc, dk_acc, dv_acc),
    )
    dk_ref[...] = dk
    dv_ref[...] = dv
    back_weights(dk, dv, a_ref[...], acc, width)
    a_all[pl.ds(pl.multiple_of(step * OWN, OWN), OWN), :] = a_ref[...]

    @pl.when(step == pl.num_programs(0) - 1)
    def _():
        scale = HEAD ** (-0.5)
        for t in range(tiles):
            for p in range(pairs):
                cols = columns_of(p)
                dq_ref[t * QT:(t + 1) * QT, cols] = (dq_acc[t, cols, :] * scale).T.astype(bf)
        acc[:, :width] = contract_rows(a_all[...], dq_ref[...])
        blocks = places.shape[0]
        shard = width // blocks
        if shard % 8:
            both = contract_rows(order_ref[...], acc[...].astype(bf)).astype(bf)
            keep_ref[...] = both[:half]
            send_ref[...] = both[half:]
            return
        for j in range(0, blocks, 2):
            both = [
                acc[pl.ds(pl.multiple_of(places[j + i] * shard, 8), shard), :] for i in range(2)
            ]
            out, to = (keep_ref, j) if j < blocks // 2 else (send_ref, j - blocks // 2)
            out[to * shard:(to + 2) * shard, :] = jnp.concatenate(both, axis=0).astype(bf)


def back_specs(rows, width, tile_rows, at_key):
    tiles = rows // QT
    pairs = width // PAIR
    whole = pl.BlockSpec(memory_space=pltpu.VMEM)
    tile = pl.BlockSpec((tile_rows, width), at_key)
    specs = [tile, tile, tile, pl.BlockSpec((tile_rows, QT), at_key)] + [whole] * 5
    scratch = [
        pltpu.VMEM((tiles, pairs, PAIR, 2 * QT), bf),
        pltpu.VMEM((tiles, pairs, PAIR, 2 * QT), bf),
        pltpu.VMEM((tiles, pairs, 2 * QT, PAIR), bf),
        pltpu.VMEM((tiles, pairs, 2 * QT, PAIR), bf),
        pltpu.VMEM((tiles, 8, 2 * QT), f32),
        pltpu.VMEM((tile_rows, width), f32),
        pltpu.VMEM((tile_rows, width), f32),
    ]
    return specs, scratch, whole


def outer_back(scalars, k, v, a, kseg, q, do, o, lse, qseg, weight, *deps):
    rows, width = q.shape

    def at_key(step, begin, end, span, odd, places):
        return (jnp.clip(step, span[0], span[1]), 0)

    specs, scratch, whole = back_specs(rows, width, OUTER, at_key)
    return pl.pallas_call(
        outer_kernel,
        grid_spec=pltpu.PrefetchScalarGridSpec(
            num_scalar_prefetch=5,
            grid=(k.shape[0] // OUTER,),
            in_specs=specs + [whole] + [pl.BlockSpec(memory_space=pl.ANY)] * len(deps),
            out_specs=[whole] * 6,
            scratch_shapes=scratch,
        ),
        out_shape=[
            *[jax.ShapeDtypeStruct((rows, width), bf)] * 4,
            jax.ShapeDtypeStruct((width, 2 * width), f32),
            jax.ShapeDtypeStruct((rows // QT, width, QT), f32),
        ],
        compiler_params=pltpu.CompilerParams(vmem_limit_bytes=50 * 1024 * 1024),
        cost_estimate=BRIEF,
        name="outer_back",
    )(*scalars, k, v, a, kseg, q, do, o, lse, qseg, weight, *deps)


def inner_back(scalars, k, v, a, kseg, q, do, o, lse, qseg, order, partial, *deps):
    rows, width = q.shape
    half = width // 2
    specs, scratch, whole = back_specs(rows, width, OWN, lambda step, *_: (step, 0))
    scratch += [
        pltpu.VMEM((width, 3 * width), f32),
        pltpu.VMEM((rows // QT, width, QT), f32),
        pltpu.VMEM((rows, width), bf),
    ]
    own = jax.ShapeDtypeStruct((rows, width), bf)
    message = jax.ShapeDtypeStruct((half, 3 * width), bf)
    return pl.pallas_call(
        inner_kernel,
        grid_spec=pltpu.PrefetchScalarGridSpec(
            num_scalar_prefetch=5,
            grid=(rows // OWN,),
            in_specs=specs + [whole] * 3 + [pl.BlockSpec(memory_space=pl.ANY)] * len(deps),
            out_specs=[specs[0], specs[0], whole, whole, whole, whole],
            scratch_shapes=scratch,
        ),
        out_shape=[own, own, own, message, message, jax.ShapeDtypeStruct((8, 128), f32)],
        compiler_params=pltpu.CompilerParams(vmem_limit_bytes=46 * 1024 * 1024),
        cost_estimate=BRIEF,
        name="inner_back",
    )(*scalars, k, v, a, kseg, q, do, o, lse, qseg, order, *partial, *deps)


def middle_kernel(places, x_ref, o_ref, dz_ref, gain_ref, order_ref, wo_ref, wh_ref, wp_ref,
                  mid_ref, hid_ref, hkeep_ref, hsend_ref, pkeep_ref, psend_ref, okeep_ref, osend_ref,
                  dx_ref, do_ref, normed, inverse, second, ordered, dsec, grads):
    step = pl.program_id(0)
    width = x_ref.shape[1]
    half = width // 2

    @pl.when(step == 0)
    def _():
        value = x_ref[...].astype(f32) + dot(o_ref[...], wo_ref[...])
        mid_ref[...] = value
        n, r = normalize_parts(value)
        normed[...] = n
        inverse[...] = jnp.broadcast_to(r, inverse.shape)
        b = (n * gain_ref[1:2, :]).astype(bf)
        second[...] = b
        ordered[...] = dot(b, order_ref[...]).astype(bf)
        dsec[...] = jnp.zeros(dsec.shape, f32)

    dz = dz_ref[...]
    wh = wh_ref[...]
    wp = wp_ref[...]
    u = dot(second[...], wh)
    cdf = 0.5 * (1.0 + lax.erf(u * (0.5 ** 0.5)))
    pdf = jnp.exp(-0.5 * u * u) * 0.3989422804014327
    hid = (u * cdf).astype(bf)
    du = (contract_cols(dz, wp) * (cdf + u * pdf)).astype(bf)
    hid_ref[...] = hid

    def put(keep_ref, send_ref, grad):
        grad = grad.astype(bf)
        keep_ref[...] = grad[:half]
        send_ref[...] = grad[half:]

    def put_rows(keep_ref, send_ref, left, right):
        blocks = places.shape[0]
        shard = width // blocks
        if shard % 8:
            put(keep_ref, send_ref, contract_rows(dot(left, order_ref[...]).astype(bf), right))
            return
        grads[...] = contract_rows(left, right)
        for j in range(0, blocks, 2):
            both = [
                grads[pl.ds(pl.multiple_of(places[j + i] * shard, 8), shard), :] for i in range(2)
            ]
            out, to = (keep_ref, j) if j < blocks // 2 else (send_ref, j - blocks // 2)
            out[to * shard:(to + 2) * shard, :] = jnp.concatenate(both, axis=0).astype(bf)

    put(hkeep_ref, hsend_ref, contract_rows(ordered[...], du))
    put_rows(pkeep_ref, psend_ref, hid, dz)
    dsec[...] += contract_cols(du, wh)

    @pl.when(step == pl.num_programs(0) - 1)
    def _():
        n = normed[...]
        db = dsec[...]
        dx = dz.astype(f32) + normalize_back(db, n, inverse[:, 0:1], gain_ref[1:2, :])
        dx_ref[...] = dx
        dproj = dx.astype(bf)
        put_rows(okeep_ref, osend_ref, o_ref[...], dproj)
        do_ref[...] = contract_cols(dproj, wo_ref[...]).astype(bf)


def middle(places, x, o, dz, gains, order, packed):
    rows, width = x.shape
    ratio = (packed.shape[1] - width) // (2 * width)
    whole = pl.BlockSpec(memory_space=pltpu.VMEM)
    line = jax.ShapeDtypeStruct((rows, width), f32)
    low = jax.ShapeDtypeStruct((rows, width), bf)
    half = width // 2
    part = pl.BlockSpec((half, width), lambda s, *_: (0, s))
    message = jax.ShapeDtypeStruct((half, ratio * width), bf)
    small = jax.ShapeDtypeStruct((half, width), bf)
    return pl.pallas_call(
        middle_kernel,
        grid_spec=pltpu.PrefetchScalarGridSpec(
            num_scalar_prefetch=1,
            grid=(ratio,),
            in_specs=[whole] * 5
            + [
                pl.BlockSpec((width, width), lambda s, *_: (0, 0)),
                pl.BlockSpec((width, width), lambda s, *_: (0, 1 + s)),
                pl.BlockSpec((width, width), lambda s, *_: (0, 1 + ratio + s)),
            ],
            out_specs=[whole, pl.BlockSpec((rows, width), lambda s, *_: (0, s))]
            + [part] * 4
            + [whole] * 4,
            scratch_shapes=[
                pltpu.VMEM((rows, width), f32),
                pltpu.VMEM((rows, 128), f32),
                pltpu.VMEM((rows, width), bf),
                pltpu.VMEM((rows, width), bf),
                pltpu.VMEM((rows, width), f32),
                pltpu.VMEM((width, width), f32),
            ],
        ),
        out_shape=[line, jax.ShapeDtypeStruct((rows, ratio * width), bf)]
        + [message] * 4
        + [small, small, line, low],
        compiler_params=pltpu.CompilerParams(vmem_limit_bytes=52 * 1024 * 1024),
        cost_estimate=BRIEF,
        name="middle",
    )(places, x, o, dz, gains, order, packed, packed, packed)


def out_kernel(mid_ref, hid_ref, wp_ref, out_ref, acc):
    step = pl.program_id(0)

    @pl.when(step == 0)
    def _():
        acc[...] = mid_ref[...]

    acc[...] += dot(hid_ref[...], wp_ref[...])

    @pl.when(step == pl.num_programs(0) - 1)
    def _():
        out_ref[...] = acc[...].astype(bf)


def layer_out(mid, hid, packed):
    rows, width = mid.shape
    ratio = hid.shape[1] // width
    whole = pl.BlockSpec(memory_space=pltpu.VMEM)
    return pl.pallas_call(
        out_kernel,
        grid=(ratio,),
        in_specs=[
            whole,
            pl.BlockSpec((rows, width), lambda s: (0, s)),
            pl.BlockSpec((width, width), lambda s: (0, 1 + ratio + s)),
        ],
        out_specs=whole,
        out_shape=jax.ShapeDtypeStruct((rows, width), bf),
        scratch_shapes=[pltpu.VMEM((rows, width), f32)],
        compiler_params=pltpu.CompilerParams(vmem_limit_bytes=24 * 1024 * 1024),
        cost_estimate=BRIEF,
        name="layer_out",
    )(mid, hid, packed)


def add(*arrays):
    total = arrays[0].astype(f32)
    for array in arrays[1:]:
        total += array.astype(f32)
    return total


class Links:
    def __init__(self, wide):
        self.wide = wide
        self.outer = wide // 4

    def swap(self, array, name):
        if name == "y":
            return lax.ppermute(array, "narrow", [(0, 1), (1, 0)])
        flip = 1 if name == "core" else 2
        return lax.ppermute(array, "wide", [(j, j ^ flip) for j in range(self.wide)])

    def flip_z(self, array, s):
        return lax.ppermute(array, "wide", [(j, j ^ (4 * s)) for j in range(self.wide)])

    def distance(self, at):
        bits = self.outer.bit_length() - 1
        return sum(((at >> b) & 1) << (bits - 1 - b) for b in range(bits))

    def order(self, width):
        place = lax.axis_index("wide")
        count = 2 * self.wide
        rows = width // count
        at = jnp.arange(count, dtype=jnp.int32)
        z, at = self.distance(at % self.outer) ^ (place // 4), at // self.outer
        y, at = (at + lax.axis_index("narrow")) % 2, at // 2
        x, at = (at + place // 2) % 2, at // 2
        core = (at + place) % 2
        places = ((z * 2 + x) * 2 + core) * 2 + y
        source = (places[:, None] * rows + jnp.arange(rows, dtype=jnp.int32)[None, :]).reshape(width)
        matrix = (jnp.arange(width, dtype=jnp.int32)[:, None] == source[None, :]).astype(bf)
        return places, matrix

    def along_z(self, shard):
        parts = [shard] + [self.flip_z(shard, self.distance(j)) for j in range(1, self.outer)]
        return jnp.concatenate(parts, axis=0)

    def along_xy(self, mine):
        cut = halfway(mine)
        one, two = mine[:, :cut], mine[:, cut:]
        one = jnp.concatenate([one, self.swap(one, "x")], axis=0)
        two = jnp.concatenate([two, self.swap(two, "y")], axis=0)
        one = (one, self.swap(one, "y"))
        two = (two, self.swap(two, "x"))
        return (
            one + tuple(self.swap(piece, "core") for piece in one),
            two + tuple(self.swap(piece, "core") for piece in two),
        )

    def first(self, pairs, *deps):
        rows = pairs[0][0].shape[0] // 4
        cuts = [halfway(keep) for keep, _ in pairs]
        wide = [sum(cuts), sum(keep.shape[1] for keep, _ in pairs) - sum(cuts)]

        def kernel(*refs):
            count = 2 * len(pairs)
            keep_x, send_x, keep_y, send_y = refs[-4:]
            at = [0, 0]
            for keep, got, cut in zip(refs[0:count:2], refs[1:count:2], cuts):
                rest = keep.shape[1] - cut
                one, two = slice(0, cut), slice(cut, cut + rest)
                to = slice(at[0], at[0] + cut)
                keep_x[:, to] = add(keep[:2 * rows, one], got[:2 * rows, one]).astype(bf)
                send_x[:, to] = add(keep[2 * rows:, one], got[2 * rows:, one]).astype(bf)
                to = slice(at[1], at[1] + rest)
                for j, out in enumerate((keep_y, send_y, keep_y, send_y)):
                    of = slice(j * rows, (j + 1) * rows)
                    into = slice(j // 2 * rows, (j // 2 + 1) * rows)
                    out[into, to] = add(keep[of, two], got[of, two]).astype(bf)
                at = [at[0] + cut, at[1] + rest]

        shapes = [(2 * rows, wide[0])] * 2 + [(2 * rows, wide[1])] * 2
        keep_x, send_x, keep_y, send_y = stage(kernel, sum(pairs, ()), deps, shapes)
        return (keep_x, keep_y), (self.swap(send_x, "x"), self.swap(send_y, "y"))

    def second(self, keep, got, *deps):
        rows = keep[0].shape[0] // 2

        def kernel(keep_x, keep_y, got_x, got_y, *refs):
            for keep, got, hold, send in ((keep_x, got_x, *refs[-4:-2]), (keep_y, got_y, *refs[-2:])):
                hold[...] = add(keep[:rows], got[:rows]).astype(bf)
                send[...] = add(keep[rows:], got[rows:]).astype(bf)

        shapes = [(rows, keep[0].shape[1])] * 2 + [(rows, keep[1].shape[1])] * 2
        keep_x, send_x, keep_y, send_y = stage(kernel, keep + got, deps, shapes)
        return (keep_x, keep_y), (self.swap(send_x, "y"), self.swap(send_y, "x"))

    def third(self, keep, got, *deps):
        cut = keep[0].shape[1]
        rows = keep[0].shape[0] // 2

        def kernel(keep_x, keep_y, got_x, got_y, *refs):
            hold, send = refs[-2:]
            for cols, keep, got in ((slice(0, cut), keep_x, got_x), (slice(cut, None), keep_y, got_y)):
                hold[:, cols] = add(keep[:rows], got[:rows]).astype(bf)
                send[:, cols] = add(keep[rows:], got[rows:]).astype(bf)

        hold, send = stage(kernel, keep + got, deps, [(rows, cut + keep[1].shape[1])] * 2)
        return hold, self.flip_z(send, 1)

    def fourth(self, keep, got, *deps):
        for bit in range(1, self.outer.bit_length() - 1):
            rows = keep.shape[0] // 2
            if rows % 8:
                total = add(keep, got).astype(bf)
                keep, send = total[:rows], total[rows:]
            else:
                keep, send = stage(halves_kernel, (keep, got), deps, [(rows, keep.shape[1])] * 2)
            got = self.flip_z(send, 1 << bit)
        return keep, got


def halves_kernel(keep, got, *refs):
    hold, send = refs[-2:]
    total = add(keep[...], got[...])
    hold[...] = total[:hold.shape[0]].astype(bf)
    send[...] = total[hold.shape[0]:].astype(bf)


def first_kernel(hidk, hidg, projk, projg, outk_x, outg_x, outk_y, outg_y, *refs):
    keep_x, send_x, keep_y, send_y = refs[-4:]
    rows = hidk.shape[0] // 4
    last = pl.num_programs(0) - 1

    def write(one, two):
        cols = slice(0, one[0].shape[1])
        keep_x[:, cols] = add(*(v[:2 * rows, :] for v in one)).astype(bf)
        send_x[:, cols] = add(*(v[2 * rows:, :] for v in one)).astype(bf)
        for j, out in enumerate((keep_y, send_y, keep_y, send_y)):
            of = slice(j * rows, (j + 1) * rows)
            out[j // 2 * rows:(j // 2 + 1) * rows, cols] = add(*(v[of, :] for v in two)).astype(bf)

    @pl.when(pl.program_id(0) < last)
    def _():
        write((hidk, hidg), (projk, projg))

    @pl.when(pl.program_id(0) == last)
    def _():
        write((outk_x, outg_x), (outk_y, outg_y))


class Middle:
    def __init__(self, links):
        self.links = links

    def first(self, hid, proj, out, *deps):
        rows, columns = hid[0].shape
        block = out[0].shape[1]
        steps = columns // block
        tile = pl.BlockSpec((rows, block), lambda j: (0, jnp.minimum(j, steps - 1)))
        half = [pl.BlockSpec((rows, block // 2), lambda j, at=at: (0, at)) for at in range(2)]
        shape = jax.ShapeDtypeStruct((rows // 2, columns + block // 2), bf)
        keep_x, send_x, keep_y, send_y = pl.pallas_call(
            first_kernel,
            grid=(steps + 1,),
            in_specs=[tile] * 4
            + [half[0]] * 2
            + [half[1]] * 2
            + [pl.BlockSpec(memory_space=pl.ANY)] * len(deps),
            out_specs=[pl.BlockSpec((rows // 2, block), lambda j: (0, j))] * 4,
            out_shape=[shape] * 4,
            cost_estimate=BRIEF,
            name="first",
        )(*hid, *proj, *out, *out, *deps)
        return (keep_x, keep_y), (self.links.swap(send_x, "x"), self.links.swap(send_y, "y"))

    def second(self, keep, got, *deps):
        rows = keep[0].shape[0] // 4
        cut = keep[0].shape[1]

        def kernel(keep_x, keep_y, got_x, got_y, *refs):
            hold_x, hold_y, send = refs[-3:]
            halves = ((hold_x, slice(0, cut), keep_x, got_x), (hold_y, slice(cut, None), keep_y, got_y))
            for hold, cols, keep, got in halves:
                for j in range(2):
                    into = slice(j * rows, (j + 1) * rows)
                    of = slice(2 * j * rows, (2 * j + 1) * rows)
                    hold[into, :] = add(keep[of, :], got[of, :]).astype(bf)
                    of = slice((2 * j + 1) * rows, (2 * j + 2) * rows)
                    send[into, cols] = add(keep[of, :], got[of, :]).astype(bf)

        wide = keep[1].shape[1]
        shapes = [(2 * rows, cut), (2 * rows, wide), (2 * rows, cut + wide)]
        hold_x, hold_y, send = stage(kernel, keep + got, deps, shapes)
        return (hold_x, hold_y), self.links.flip_z(send, 1)

    def third(self, keep, got, *deps):
        rows = keep[0].shape[0] // 2
        cut = keep[0].shape[1]

        def kernel(keep_x, keep_y, got, *refs):
            for keep, cols, hold, send in (
                (keep_x, slice(0, cut), *refs[-4:-2]), (keep_y, slice(cut, None), *refs[-2:])
            ):
                hold[...] = add(keep[:rows, :], got[:rows, cols]).astype(bf)
                send[...] = add(keep[rows:, :], got[rows:, cols]).astype(bf)

        shapes = [(rows, cut)] * 2 + [(rows, keep[1].shape[1])] * 2
        hold_x, send_x, hold_y, send_y = stage(kernel, keep + (got,), deps, shapes)
        return (hold_x, hold_y), (self.links.swap(send_x, "y"), self.links.swap(send_y, "x"))

    def fourth(self, keep, got, *deps):
        rows = keep[0].shape[0] // 2
        cut = keep[0].shape[1]
        if rows % 8:
            total = jnp.concatenate([add(k, g).astype(bf) for k, g in zip(keep, got)], axis=1)
            hold, send = total[:rows], total[rows:]
        else:
            def kernel(keep_x, keep_y, got_x, got_y, *refs):
                hold, send = refs[-2:]
                for cols, keep, got in ((slice(0, cut), keep_x, got_x), (slice(cut, None), keep_y, got_y)):
                    total = add(keep[...], got[...])
                    hold[:, cols] = total[:rows].astype(bf)
                    send[:, cols] = total[rows:].astype(bf)

            hold, send = stage(kernel, keep + got, deps, [(rows, cut + keep[1].shape[1])] * 2)
        got = self.links.flip_z(send, 2)
        for bit in range(2, self.links.outer.bit_length() - 1):
            total = add(hold, got).astype(bf)
            rows = rows // 2
            hold, send = total[:rows], total[rows:]
            got = self.links.flip_z(send, 1 << bit)
        return hold, got


def collect(parts, *deps):
    def kernel(*refs):
        refs[-1][...] = add(*(ref[...] for ref in refs[:len(parts)]))

    return stage(kernel, parts, deps, [parts[0].shape], f32)[0]


def stage(kernel, operands, deps, shapes, kind=bf):
    whole = pl.BlockSpec(memory_space=pltpu.VMEM)
    elsewhere = pl.BlockSpec(memory_space=pl.ANY)
    return pl.pallas_call(
        kernel,
        in_specs=[whole] * len(operands) + [elsewhere] * len(deps),
        out_specs=[whole] * len(shapes),
        out_shape=[jax.ShapeDtypeStruct(shape, kind) for shape in shapes],
        compiler_params=pltpu.CompilerParams(vmem_limit_bytes=24 * 1024 * 1024),
        cost_estimate=BRIEF,
        name="stage",
    )(*operands, *deps)


def hold(values, *deps):
    count = len(values)
    elsewhere = pl.BlockSpec(memory_space=pl.ANY)
    return pl.pallas_call(
        lambda *refs: None,
        in_specs=[elsewhere] * (count + len(deps)),
        out_specs=[elsewhere] * count,
        out_shape=[jax.ShapeDtypeStruct(v.shape, v.dtype) for v in values],
        input_output_aliases={j: j for j in range(count)},
        cost_estimate=BRIEF,
        name="hold",
    )(*values, *deps)


def halfway(array):
    return (array.shape[1] // 2 + 127) // 128 * 128


def share_kernel(dq_ref, dk_ref, dv_ref, w_ref, *refs):
    refs[-1][...] = back_input(w_ref, (0, dq_ref[...]), (1, dk_ref[...]), (2, dv_ref[...]))


def own_share(own, weight, *deps):
    rows, width = own[0].shape
    tile = pl.BlockSpec((OWN, width), lambda i: (i, 0))
    return pl.pallas_call(
        share_kernel,
        grid=(rows // OWN,),
        in_specs=[tile] * 3
        + [pl.BlockSpec(memory_space=pltpu.VMEM)]
        + [pl.BlockSpec(memory_space=pl.ANY)] * len(deps),
        out_specs=tile,
        out_shape=jax.ShapeDtypeStruct((rows, width), f32),
        compiler_params=pltpu.CompilerParams(vmem_limit_bytes=58 * 1024 * 1024),
        cost_estimate=BRIEF,
        name="own_share",
    )(*own, weight, *deps)


def finish_kernel(x_ref, dx_ref, own_ref, b0, b1, b2, b3, gain_ref, out_ref):
    n, r = normalize_parts(x_ref[...].astype(f32))
    da = add(own_ref[...], b0[...], b1[...], b2[...], b3[...])
    out_ref[...] = (dx_ref[...] + normalize_back(da, n, r, gain_ref[0:1, :])).astype(bf)


def finish(x, dx, own, others, gains):
    rows, width = x.shape
    tile = pl.BlockSpec((OWN, width), lambda i: (i, 0))
    return pl.pallas_call(
        finish_kernel,
        grid=(rows // OWN,),
        in_specs=[tile] * 7 + [pl.BlockSpec(gains.shape, lambda i: (0, 0))],
        out_specs=tile,
        out_shape=jax.ShapeDtypeStruct((rows, width), bf),
        compiler_params=pltpu.CompilerParams(vmem_limit_bytes=58 * 1024 * 1024),
        cost_estimate=BRIEF,
        name="finish",
    )(x, dx, own, *others, gains)


def gain_sums(w_ref, grad, shape):
    product = w_ref[...].astype(bf).astype(f32) * grad
    return jnp.broadcast_to(jnp.sum(product, axis=1, keepdims=True), shape)


def update_kernel(rate_ref, sum_ref, hid_ref, proj_ref, w_ref, mom_out, mom_hid, mom_proj,
                  step_out, step_hid, step_proj, next_out, next_hid, next_proj, gain_ref):
    rate = rate_ref[0]
    hidden = hid_ref.shape[1]
    width = mom_out.shape[1]
    half = width // 2
    far = hidden + half

    def put(step, following, at, momentum, grad):
        value = momentum_rate * momentum + grad
        following[at] = value
        step[at] = rate * value

    gain_ref[...] = gain_sums(w_ref, hid_ref[...], gain_ref.shape)
    whole = slice(None)
    put(step_hid, next_hid, (whole, whole), mom_hid[...], hid_ref[...])
    for at, lo in ((slice(0, half), hidden), (slice(half, width), far + hidden)):
        put(step_out, next_out, (whole, at), mom_out[:, at], sum_ref[:, lo:lo + half])
    put(step_proj, next_proj, (whole, whole), mom_proj[...], proj_ref[...])


def update(rate, total, hid, proj, w_hid, mom_out, mom_hid, mom_proj):
    whole = pl.BlockSpec(memory_space=pltpu.VMEM)
    moms = (mom_out, mom_hid, mom_proj)
    return pl.pallas_call(
        update_kernel,
        in_specs=[pl.BlockSpec(memory_space=pltpu.SMEM)] + [whole] * 7,
        out_specs=[whole] * 7,
        out_shape=[jax.ShapeDtypeStruct(m.shape, f32) for m in moms + moms]
        + [jax.ShapeDtypeStruct((hid.shape[0], 128), f32)],
        cost_estimate=BRIEF,
        name="update",
    )(rate, total, hid, proj, w_hid, *moms)


def update_first_kernel(rate_ref, keep_ref, got_ref, w_ref, mom_ref, step_ref, next_ref, gain_ref):
    total = add(keep_ref[...], got_ref[...])
    gain_ref[...] = gain_sums(w_ref, total, gain_ref.shape)
    value = momentum_rate * mom_ref[...] + total
    next_ref[...] = value
    step_ref[...] = rate_ref[0] * value


def update_first(rate, keep, got, weight, mom):
    whole = pl.BlockSpec(memory_space=pltpu.VMEM)
    return pl.pallas_call(
        update_first_kernel,
        in_specs=[pl.BlockSpec(memory_space=pltpu.SMEM)] + [whole] * 4,
        out_specs=[whole] * 3,
        out_shape=[jax.ShapeDtypeStruct(mom.shape, f32)] * 2
        + [jax.ShapeDtypeStruct((mom.shape[0], 128), f32)],
        cost_estimate=BRIEF,
        name="update_first",
    )(rate, keep, got, weight, mom)


def body(
    joint_in,
    cotangent,
    segment_ids,
    layer_index,
    step_index,
    gain_one,
    w_qkv,
    w_attn_out,
    gain_two,
    w_hidden,
    w_proj,
    mom_gain_one,
    mom_qkv,
    mom_attn_out,
    mom_gain_two,
    mom_hidden,
    mom_proj,
):
    rows, width = joint_in.shape
    wide = lax.axis_size("wide")
    both = ("wide", "narrow")
    shard = w_qkv.shape[0]
    hidden = w_hidden.shape[1]
    ratio = hidden // width
    odd = lax.axis_index("narrow")
    place = lax.axis_index("wide") * 2 + odd
    window = 5 * rows
    is_even = odd == 0

    links = Links(wide)
    places, order = links.order(width)
    gains = jnp.stack([gain_one, gain_two], axis=1)
    gains = jnp.pad(gains, ((0, 0), (0, 126)))
    pack_a = jnp.concatenate([w_qkv.astype(bf), gains.astype(bf)], axis=1)
    hid_order = w_hidden.astype(bf).reshape(shard, width, ratio).transpose(0, 2, 1)
    pack_b = jnp.concatenate(
        [
            w_attn_out.astype(bf),
            hid_order.reshape(shard, hidden),
            w_proj.astype(bf).reshape(shard, hidden),
        ],
        axis=1,
    )

    fill = jnp.full((2 * rows,), -1, jnp.int32)
    ids = jnp.concatenate([fill, segment_ids, fill])
    key_ids = lax.dynamic_slice_in_dim(ids, place * rows, window, 0)
    own_ids = lax.dynamic_slice_in_dim(segment_ids, place * rows, rows, 0)
    tiles = own_ids.reshape(rows // QT, QT)
    far_ids = jnp.concatenate([key_ids[:2 * rows], key_ids[3 * rows:]])
    kseg = jnp.broadcast_to(far_ids[:, None], (4 * rows, QT))
    oseg = jnp.broadcast_to(own_ids[:, None], (rows, QT))
    qseg = jnp.broadcast_to(tiles[:, None, :], (rows // QT, 8, QT))
    origin = (place - 2) * rows
    low = jnp.sum(segment_ids[None, :] < tiles[:, :1], axis=1, dtype=jnp.int32) - origin
    high = jnp.sum(segment_ids[None, :] <= tiles[:, -1:], axis=1, dtype=jnp.int32) - origin
    low = jnp.clip(low, 0, window)
    high = jnp.clip(high, 0, window)
    side = 2 * rows // OUTER
    starts = [2 * rows + j * OWN for j in range(rows // OWN)]
    starts += [j * OUTER for j in range(side)] + [3 * rows + j * OUTER for j in range(side)]
    sizes = [OWN] * (rows // OWN) + [OUTER] * (2 * side)
    edges = jnp.asarray(starts, jnp.int32)[:, None]
    tops = jnp.asarray([at + size for at, size in zip(starts, sizes)], jnp.int32)[:, None]
    begin = jnp.sum(high[None, :] <= edges, axis=1, dtype=jnp.int32)
    end = jnp.sum(low[None, :] < tops, axis=1, dtype=jnp.int32)
    near = jnp.minimum(low[0] // OUTER, side)
    last = side - 1 + jnp.maximum(high[-1] - 3 * rows + OUTER - 1, 0) // OUTER
    span = jnp.stack([near, jnp.maximum(last, near)])
    scalars = (begin, end, span, odd.reshape(1), places)

    swap = [(0, 1), (1, 0)]
    up = [(j, j + 1) for j in range(wide - 1)]
    down = [(j + 1, j) for j in range(wide - 1)]
    across = [(2 * j, 2 * j + 2) for j in range(wide - 1)]
    across += [(2 * j + 3, 2 * j + 1) for j in range(wide - 1)]
    partner = lax.ppermute(joint_in, "narrow", swap)
    before = lax.ppermute(joint_in, "wide", up)
    behind = lax.ppermute(joint_in, "wide", down)
    mine_a = links.along_z(pack_a)
    fourth = lax.ppermute(partner, both, across)
    ones, twos = links.along_xy(mine_a)
    blocks = (before, partner, fourth, behind)
    (pack_b,) = hold((pack_b,), before, partner, behind, mine_a)
    full_b = lax.all_gather(pack_b, both, axis=0, tiled=True)

    weight, gains, a_own, k_own, v_own, a_far, k_far, v_far, q, o, lse = attend(
        scalars, blocks, kseg, oseg, joint_in, qseg, order, ones, twos
    )

    mid, hid, hid_keep, hid_send, proj_keep, proj_send, out_keep, out_send, dx, do = middle(
        places, joint_in, o, cotangent, gains, order, full_b
    )
    joint_out = layer_out(mid, hid, full_b)
    chain = Middle(links)
    keep_b, got_b = chain.first(
        (hid_keep, links.swap(hid_send, "core")),
        (proj_keep, links.swap(proj_send, "core")),
        (out_keep, links.swap(out_send, "core")),
        joint_out,
    )
    args = (q, do, o, lse, qseg)
    da_before, da_partner, da_fourth, da_behind, *partial = outer_back(
        scalars, k_far, v_far, a_far, kseg, *args, weight, *keep_b
    )

    keep_b, got_b = chain.second(keep_b, got_b, da_before)
    home = [(2 * j + 2, 2 * j + 1) for j in range(wide - 1)]
    home += [(t, s) for s, t in home]
    others = (
        lax.ppermute(da_before, "wide", down),
        lax.ppermute(da_partner, "narrow", swap),
        lax.ppermute(da_fourth, both, home),
        lax.ppermute(da_behind, "wide", up),
    )
    dk, dv, dq, keep_a, send_a, token = inner_back(
        scalars, k_own, v_own, a_own, oseg, *args, order, partial, *keep_b
    )

    keep_b, got_b = chain.third(keep_b, got_b, token)
    da_own = own_share((dq, dk, dv), weight, *keep_b)
    (send_a,) = hold((send_a,), da_own, *others, *keep_b)
    got_a = links.swap(send_a, "core")
    keep_b, got_b = chain.fourth(keep_b, got_b, send_a)
    keep_a, got_a = links.first([(keep_a, got_a)], keep_b)
    (gains,) = hold((gains,), *keep_a)
    grad_in = finish(joint_in, dx, da_own, others, gains)
    keep_a, got_a = links.second(keep_a, got_a, grad_in)
    sum_b = collect((keep_b, got_b), *keep_a)
    keep_a, got_a = links.third(keep_a, got_a, sum_b)
    keep_a, got_a = links.fourth(keep_a, got_a)

    rate = base_rate * jnp.power(jnp.float32(decay_rate), (11 - layer_index).astype(f32))
    rate = rate * jnp.power(1.0 - step_index.astype(f32) / total_steps, 0.9)
    sum_hid = sum_b[:, :hidden].reshape(shard, ratio, width).transpose(0, 2, 1)
    sum_hid = sum_hid.reshape(shard, hidden)
    far = hidden + width // 2
    sum_proj = sum_b[:, far:far + hidden].reshape(shard * ratio, width)
    step_out, step_hid, step_proj, next_out, next_hid, next_proj, gain_b = update(
        rate, sum_b, sum_hid, sum_proj, w_hidden, mom_attn_out, mom_hidden, mom_proj
    )
    step_qkv, next_qkv, gain_a = update_first(rate, keep_a, got_a, w_qkv, mom_qkv)
    next_g1 = momentum_rate * mom_gain_one + gain_a[:, 0] / gain_one.astype(bf).astype(f32)
    next_g2 = momentum_rate * mom_gain_two + gain_b[:, 0] / gain_two.astype(bf).astype(f32)
    return (
        joint_out,
        grad_in,
        rate * next_g1,
        step_qkv,
        step_out,
        rate * next_g2,
        step_hid,
        step_proj,
        next_g1,
        next_qkv,
        next_out,
        next_g2,
        next_hid,
        next_proj,
    )


def solution(mesh):
    split = P(("wide", "narrow"), None)
    line = P(("wide", "narrow"))
    params = (line, split, split, line, split, split)
    return jax.shard_map(
        body,
        mesh=mesh,
        in_specs=(split, split, P(), P(), P()) + params + params,
        out_specs=(split, split) + params + params,
        check_vma=False,
    )
```

```python
import functools

import jax
import jax.numpy as jnp
from jax import lax
from jax.experimental import pallas as pl
from jax.experimental.pallas import tpu as pltpu
from jax.sharding import PartitionSpec as P

HEAD = 64
PAIR = 2 * HEAD
QT = 128
OWN = 320
OUTER = 256
GROUP = 3
BRIEF = pl.CostEstimate(flops=1, bytes_accessed=1, transcendentals=0)

eps = 1e-06
base_rate = 0.01
decay_rate = 0.65
total_steps = 100000.0
momentum_rate = 0.9

bf = jnp.bfloat16
f32 = jnp.float32


def dot(left, right):
    return jnp.dot(left, right, preferred_element_type=f32)


def contract_rows(left, right):
    return lax.dot_general(
        left, right, (((0,), (0,)), ((), ())), preferred_element_type=f32
    )


def contract_cols(left, right):
    return lax.dot_general(
        left, right, (((1,), (1,)), ((), ())), preferred_element_type=f32
    )


def normalize_parts(values):
    centre = jnp.mean(values, axis=-1, keepdims=True)
    centred = values - centre
    inverse = lax.rsqrt(jnp.mean(centred * centred, axis=-1, keepdims=True) + eps)
    return (centred * inverse, inverse)


def normalize_back(grad_out, normed, inverse, gain):
    grad_normed = grad_out * gain
    inner = grad_normed - jnp.mean(grad_normed, axis=-1, keepdims=True)
    inner = inner - normed * jnp.mean(grad_normed * normed, axis=-1, keepdims=True)
    return inverse * inner


def diag_wide(block):
    row = lax.broadcasted_iota(jnp.int32, block.shape, 0)
    zero = jnp.zeros_like(block)
    return jnp.concatenate(
        [jnp.where(row < HEAD, block, zero), jnp.where(row >= HEAD, block, zero)], axis=1
    )


def diag_tall(block):
    col = lax.broadcasted_iota(jnp.int32, block.shape, 1)
    zero = jnp.zeros_like(block)
    return jnp.concatenate(
        [jnp.where(col < HEAD, block, zero), jnp.where(col >= HEAD, block, zero)], axis=0
    )


def tile_bias(segments, qseg_ref, t):
    bias = jnp.where(segments == qseg_ref[t, 0:1, :], 0.0, -1e30).astype(f32)
    return jnp.concatenate([bias, bias], axis=1)


def columns_of(pair):
    return slice(pair * PAIR, (pair + 1) * PAIR)


def block_starts(odd, size):
    return (0, (2 - odd) * size, (1 + odd) * size, 3 * size)


def pieces_of(tile, odd, refs, size):
    for part in range(OUTER // QT):
        at = tile * (OUTER // QT) + part
        for ref, start in zip(refs, block_starts(odd, size)):
            yield (at >= start) & (at < start + size), ref, at - start, part


def copy_rows(tile, odd, refs, size, out):
    for number, (here, _, _, part) in enumerate(pieces_of(tile, odd, refs[:4], size)):
        ref = refs[number]

        @pl.when(here)
        def _(ref=ref, part=part):
            out[part * QT:(part + 1) * QT, :] = ref[...]


def block_specs(width, size, key):
    def spec(part, number):
        def index(step, begin, end, span, odd, places):
            at = key(step) * (OUTER // QT) + part
            return (jnp.clip(at - block_starts(odd[0], size)[number], 0, size - 1), 0)

        return pl.BlockSpec((QT, width), index)

    return [spec(part, number) for part in range(OUTER // QT) for number in range(4)]


def in_pairs(first, last, visit):
    twos = (last - first) // 2

    def two(j, carry):
        visit([first + 2 * j, first + 2 * j + 1])
        return carry

    lax.fori_loop(0, twos, two, 0)

    @pl.when(first + 2 * twos < last)
    def _():
        visit([last - 1])


def attend_kernel(begin, end, span, odd, places, *refs, pieces):
    count = 4 * OUTER // QT
    blocks, (kseg_ref, oseg_ref, own_ref, qseg_ref, order_ref) = refs[:count], refs[count:count + 5]
    parts = refs[count + 5:count + 5 + 2 * pieces]
    (w_ref, gains_ref, ao_ref, ko_ref, vo_ref, a_ref, k_ref, v_ref, q_ref, o_ref, lse_ref,
     qbd, top, total, acc, x_ref, rel_ref) = refs[count + 5 + 2 * pieces:]
    step = pl.program_id(0)
    rows, width = own_ref.shape
    pairs = width // PAIR
    tiles = qseg_ref.shape[0]
    scale = HEAD ** (-0.5)

    def project(x):
        n, _ = normalize_parts(x.astype(f32))
        a = (n * gains_ref[0:1, :]).astype(bf)
        k = dot(a, w_ref[:, width:2 * width]).astype(bf)
        return a, k, dot(a, w_ref[:, 2 * width:3 * width]).astype(bf)

    def visit(queries, keys, values, segments):
        group = [(t, p) for t in queries for p in range(pairs)]
        bias = [tile_bias(segments, qseg_ref, t) for t in queries]
        scores = [
            dot(keys(columns_of(p)), qbd[t, p]) + bias[j // pairs] for j, (t, p) in enumerate(group)
        ]
        olds = [top[t, p:p + 1, :] for t, p in group]
        news = [jnp.maximum(old, jnp.max(s, axis=0, keepdims=True)) for old, s in zip(olds, scores)]
        expo = [jnp.exp(s - new) for s, new in zip(scores, news)]
        shrinks = [jnp.exp(old - new) for old, new in zip(olds, news)]
        sums = [
            total[t, p:p + 1, :] * shrink + jnp.sum(e, axis=0, keepdims=True)
            for (t, p), shrink, e in zip(group, shrinks, expo)
        ]
        gots = [
            contract_rows(values(columns_of(p)), e.astype(bf)) for (t, p), e in zip(group, expo)
        ]
        for (t, p), new, shrink, summed, got in zip(group, news, shrinks, sums, gots):
            top[t, p:p + 1, :] = new
            total[t, p:p + 1, :] = summed
            lo, mid, hi = p * PAIR, p * PAIR + HEAD, (p + 1) * PAIR
            acc[t, lo:mid, :] = acc[t, lo:mid, :] * shrink[:, :QT] + got[:HEAD, :QT]
            acc[t, mid:hi, :] = acc[t, mid:hi, :] * shrink[:, QT:] + got[HEAD:, QT:]

    @pl.when(step == 0)
    def _():
        size = parts[0].shape[0] // 2
        cut = parts[0].shape[1]
        shard = size // (places.shape[0] // 8)
        halves = (slice(0, cut), slice(cut, rel_ref.shape[1]))
        for j in range(pieces):
            for h in range(2):
                of = slice(h * size, (h + 1) * size)
                core, other = j // 2 * 4, j % 2
                for block, cols, part in (
                    (core + 2 * h + other, halves[0], parts[j]),
                    (core + 2 * other + h, halves[1], parts[pieces + j]),
                ):
                    value = part[of, :].astype(f32)
                    if shard % 8:
                        rel_ref[block * size:(block + 1) * size, cols] = value
                        continue
                    for z in range(size // shard):
                        to = pl.multiple_of(places[block * (size // shard) + z] * shard, 8)
                        rel_ref[pl.ds(to, shard), cols] = value[z * shard:(z + 1) * shard]
        if shard % 8:
            w_ref[...] = dot(order_ref[...], rel_ref[...].astype(bf)).astype(bf)
        else:
            w_ref[...] = rel_ref[...].astype(bf)
        gains_ref[...] = w_ref[:, 3 * width:].astype(f32).T[:8]
        a, k, v = project(own_ref[...])
        ao_ref[...] = a
        ko_ref[...] = k
        vo_ref[...] = v
        q = dot(a, w_ref[:, :width]).astype(bf)
        q_ref[...] = q
        q = q.astype(f32) * scale
        for t in range(tiles):
            for p in range(pairs):
                qbd[t, p] = diag_wide(q[t * QT:(t + 1) * QT, columns_of(p)].T.astype(bf))
        top[...] = jnp.full(top.shape, -1e30, f32)
        total[...] = jnp.zeros(total.shape, f32)
        acc[...] = jnp.zeros(acc.shape, f32)

        def own(h, carry):
            at = pl.ds(pl.multiple_of(h * OWN, OWN), OWN)
            in_pairs(
                begin[h], end[h],
                lambda ts: visit(
                    ts, lambda c: ko_ref[at, c], lambda c: vo_ref[at, c], oseg_ref[at, :]
                ),
            )
            return carry

        lax.fori_loop(0, rows // OWN, own, 0)

    number = step - 1 + rows // OWN

    @pl.when((step > 0) & (begin[number] < end[number]))
    def _():
        copy_rows(step - 1, odd[0], blocks, rows // QT, x_ref)
        a, k, v = project(x_ref[...])
        a_ref[...] = a
        k_ref[...] = k
        v_ref[...] = v
        in_pairs(
            begin[number], end[number],
            lambda ts: visit(ts, lambda c: k_ref[:, c], lambda c: v_ref[:, c], kseg_ref[...]),
        )

    @pl.when(step == pl.num_programs(0) - 1)
    def _():
        for t in range(tiles):
            for p in range(pairs):
                sums = total[t, p:p + 1, :]
                lse_ref[t, p] = top[t, p:p + 1, :] + jnp.log(sums)
                inv = 1.0 / sums
                lo, mid, hi = p * PAIR, p * PAIR + HEAD, (p + 1) * PAIR
                out = jnp.concatenate(
                    [acc[t, lo:mid, :] * inv[:, :QT], acc[t, mid:hi, :] * inv[:, QT:]], axis=0
                )
                o_ref[t * QT:(t + 1) * QT, lo:hi] = out.T.astype(bf)


def attend(scalars, blocks, kseg, oseg, x_own, qseg, order, ones, twos):
    rows, width = x_own.shape
    outer = 4 * rows
    tiles = rows // QT
    pairs = width // PAIR
    columns = ones[0].shape[1] + twos[0].shape[1]
    whole = pl.BlockSpec(memory_space=pltpu.VMEM)

    def at_used(step, begin, end, span, odd, places):
        return (jnp.clip(step - 1, span[0], span[1]), 0)

    tile = pl.BlockSpec((OUTER, width), at_used)
    own = jax.ShapeDtypeStruct((rows, width), bf)
    far = jax.ShapeDtypeStruct((outer, width), bf)
    return pl.pallas_call(
        functools.partial(attend_kernel, pieces=len(ones)),
        grid_spec=pltpu.PrefetchScalarGridSpec(
            num_scalar_prefetch=5,
            grid=(1 + outer // OUTER,),
            in_specs=block_specs(width, rows // QT, lambda step: step - 1)
            + [pl.BlockSpec((OUTER, QT), at_used)]
            + [whole] * (4 + 2 * len(ones)),
            out_specs=[whole] * 5 + [tile] * 3 + [whole] * 3,
            scratch_shapes=[
                pltpu.VMEM((tiles, pairs, PAIR, 2 * QT), bf),
                pltpu.VMEM((tiles, 8, 2 * QT), f32),
                pltpu.VMEM((tiles, 8, 2 * QT), f32),
                pltpu.VMEM((tiles, width, QT), f32),
                pltpu.VMEM((OUTER, width), bf),
                pltpu.VMEM((width, columns), f32),
            ],
        ),
        out_shape=[
            jax.ShapeDtypeStruct((width, columns), bf),
            jax.ShapeDtypeStruct((8, width), f32),
            own,
            own,
            own,
            far,
            far,
            far,
            own,
            own,
            jax.ShapeDtypeStruct((tiles, pairs, 1, 2 * QT), f32),
        ],
        compiler_params=pltpu.CompilerParams(vmem_limit_bytes=56 * 1024 * 1024),
        cost_estimate=BRIEF,
        name="attend",
    )(*scalars, *(blocks * (OUTER // QT)), kseg, oseg, x_own, qseg, order, *ones, *twos)


def back_tile(first, last, refs, scratch):
    k_ref, v_ref, kseg_ref, qseg_ref, lse_ref = refs
    qbd, dobd, qn, don, delta, dq_acc, dk_acc, dv_acc = scratch
    pairs = qbd.shape[1]
    dk_acc[...] = jnp.zeros(dk_acc.shape, f32)
    dv_acc[...] = jnp.zeros(dv_acc.shape, f32)

    def visit(t):
        bias = tile_bias(kseg_ref[...], qseg_ref, t)
        for base in range(0, pairs, GROUP):
            group = range(base, min(pairs, base + GROUP))
            keys = [k_ref[:, columns_of(p)] for p in group]
            scores = [dot(kp, qbd[t, p]) for kp, p in zip(keys, group)]
            dprobs = [dot(v_ref[:, columns_of(p)], dobd[t, p]) for p in group]
            probs = [jnp.exp(s + bias - lse_ref[t, p]) for s, p in zip(scores, group)]
            ds = [
                (pr * (dp - delta[t, p:p + 1, :])).astype(bf)
                for pr, dp, p in zip(probs, dprobs, group)
            ]
            got_v = [dot(pr.astype(bf), don[t, p]) for pr, p in zip(probs, group)]
            got_k = [dot(d, qn[t, p]) for d, p in zip(ds, group)]
            got_q = [contract_rows(kp, d) for kp, d in zip(keys, ds)]
            for i, p in enumerate(group):
                lo, mid, hi = p * PAIR, p * PAIR + HEAD, (p + 1) * PAIR
                dv_acc[:, lo:hi] += got_v[i]
                dk_acc[:, lo:hi] += got_k[i]
                dq_acc[t, lo:mid, :] += got_q[i][:HEAD, :QT]
                dq_acc[t, mid:hi, :] += got_q[i][HEAD:, QT:]

    def visits(ts):
        for t in ts:
            visit(t)

    in_pairs(first, last, visits)
    return dk_acc[...].astype(bf), dv_acc[...].astype(bf)


def back_prepare(q_ref, do_ref, o_ref, scratch):
    qbd, dobd, qn, don, delta = scratch
    tiles, pairs = qbd.shape[:2]
    scale = HEAD ** (-0.5)
    for t in range(tiles):
        at = slice(t * QT, (t + 1) * QT)
        for p in range(pairs):
            cols = columns_of(p)
            q = q_ref[at, cols].astype(f32) * scale
            do = do_ref[at, cols].astype(f32)
            do_t = do.T
            qbd[t, p] = diag_wide(q.T.astype(bf))
            dobd[t, p] = diag_wide(do_t.astype(bf))
            qn[t, p] = diag_tall(q.astype(bf))
            don[t, p] = diag_tall(do.astype(bf))
            both = do_t * o_ref[at, cols].astype(f32).T
            delta[t, p:p + 1, :QT] = jnp.sum(both[:HEAD], axis=0, keepdims=True)
            delta[t, p:p + 1, QT:] = jnp.sum(both[HEAD:], axis=0, keepdims=True)


def back_input(w_ref, *grads):
    width = w_ref.shape[0]
    total = 0.0
    for number, grad in grads:
        total += contract_cols(grad, w_ref[:, number * width:(number + 1) * width])
    return total


def back_weights(dk, dv, a, acc, lo):
    width = dk.shape[1]
    acc[:, lo:lo + width] += contract_rows(a, dk)
    acc[:, lo + width:lo + 2 * width] += contract_rows(a, dv)


def outer_kernel(begin, end, span, odd, places, k_ref, v_ref, a_ref, kseg_ref, q_ref, do_ref, o_ref,
                 lse_ref, qseg_ref, w_ref, *refs):
    da_refs = refs[-13:-9]
    acc_ref, dq_ref, qbd, dobd, qn, don, delta, dk_acc, dv_acc = refs[-9:]
    step = pl.program_id(0)
    size = q_ref.shape[0] // QT
    number = step + q_ref.shape[0] // OWN

    @pl.when(step == 0)
    def _():
        back_prepare(q_ref, do_ref, o_ref, (qbd, dobd, qn, don, delta))
        acc_ref[...] = jnp.zeros(acc_ref.shape, f32)
        dq_ref[...] = jnp.zeros(dq_ref.shape, f32)

    used = begin[number] < end[number]

    def put(value):
        for here, ref, at, part in pieces_of(step, odd[0], da_refs, size):
            @pl.when(here)
            def _(ref=ref, at=at, part=part):
                ref[pl.ds(pl.multiple_of(at * QT, QT), QT), :] = value[part * QT:(part + 1) * QT]

    @pl.when(used)
    def _():
        dk, dv = back_tile(
            begin[number], end[number], (k_ref, v_ref, kseg_ref, qseg_ref, lse_ref),
            (qbd, dobd, qn, don, delta, dq_ref, dk_acc, dv_acc),
        )
        back_weights(dk, dv, a_ref[...], acc_ref, 0)
        put(back_input(w_ref, (1, dk), (2, dv)).astype(bf))

    @pl.when(jnp.logical_not(used))
    def _():
        put(jnp.zeros(k_ref.shape, bf))


def inner_kernel(begin, end, span, odd, places, k_ref, v_ref, a_ref, kseg_ref, q_ref, do_ref, o_ref,
                 lse_ref, qseg_ref, order_ref, acc_in, dq_in, *refs):
    (dk_ref, dv_ref, dq_ref, keep_ref, send_ref, token_ref,
     qbd, dobd, qn, don, delta, dk_acc, dv_acc, acc, dq_acc, a_all) = refs[-16:]
    step = pl.program_id(0)
    width = k_ref.shape[1]
    half = width // 2
    tiles, pairs = qbd.shape[:2]

    @pl.when(step == 0)
    def _():
        back_prepare(q_ref, do_ref, o_ref, (qbd, dobd, qn, don, delta))
        token_ref[...] = jnp.zeros(token_ref.shape, f32)
        acc[:, width:3 * width] = acc_in[...]
        dq_acc[...] = dq_in[...]

    dk, dv = back_tile(
        begin[step], end[step], (k_ref, v_ref, kseg_ref, qseg_ref, lse_ref),
        (qbd, dobd, qn, don, delta, dq_acc, dk_acc, dv_acc),
    )
    dk_ref[...] = dk
    dv_ref[...] = dv
    back_weights(dk, dv, a_ref[...], acc, width)
    a_all[pl.ds(pl.multiple_of(step * OWN, OWN), OWN), :] = a_ref[...]

    @pl.when(step == pl.num_programs(0) - 1)
    def _():
        scale = HEAD ** (-0.5)
        for t in range(tiles):
            for p in range(pairs):
                cols = columns_of(p)
                dq_ref[t * QT:(t + 1) * QT, cols] = (dq_acc[t, cols, :] * scale).T.astype(bf)
        acc[:, :width] = contract_rows(a_all[...], dq_ref[...])
        blocks = places.shape[0]
        shard = width // blocks
        if shard % 8:
            both = contract_rows(order_ref[...], acc[...].astype(bf)).astype(bf)
            keep_ref[...] = both[:half]
            send_ref[...] = both[half:]
            return
        for j in range(0, blocks, 2):
            both = [
                acc[pl.ds(pl.multiple_of(places[j + i] * shard, 8), shard), :] for i in range(2)
            ]
            out, to = (keep_ref, j) if j < blocks // 2 else (send_ref, j - blocks // 2)
            out[to * shard:(to + 2) * shard, :] = jnp.concatenate(both, axis=0).astype(bf)


def back_specs(rows, width, tile_rows, at_key):
    tiles = rows // QT
    pairs = width // PAIR
    whole = pl.BlockSpec(memory_space=pltpu.VMEM)
    tile = pl.BlockSpec((tile_rows, width), at_key)
    specs = [tile, tile, tile, pl.BlockSpec((tile_rows, QT), at_key)] + [whole] * 5
    scratch = [
        pltpu.VMEM((tiles, pairs, PAIR, 2 * QT), bf),
        pltpu.VMEM((tiles, pairs, PAIR, 2 * QT), bf),
        pltpu.VMEM((tiles, pairs, 2 * QT, PAIR), bf),
        pltpu.VMEM((tiles, pairs, 2 * QT, PAIR), bf),
        pltpu.VMEM((tiles, 8, 2 * QT), f32),
        pltpu.VMEM((tile_rows, width), f32),
        pltpu.VMEM((tile_rows, width), f32),
    ]
    return specs, scratch, whole


def outer_back(scalars, k, v, a, kseg, q, do, o, lse, qseg, weight, *deps):
    rows, width = q.shape

    def at_key(step, begin, end, span, odd, places):
        return (jnp.clip(step, span[0], span[1]), 0)

    specs, scratch, whole = back_specs(rows, width, OUTER, at_key)
    return pl.pallas_call(
        outer_kernel,
        grid_spec=pltpu.PrefetchScalarGridSpec(
            num_scalar_prefetch=5,
            grid=(k.shape[0] // OUTER,),
            in_specs=specs + [whole] + [pl.BlockSpec(memory_space=pl.ANY)] * len(deps),
            out_specs=[whole] * 6,
            scratch_shapes=scratch,
        ),
        out_shape=[
            *[jax.ShapeDtypeStruct((rows, width), bf)] * 4,
            jax.ShapeDtypeStruct((width, 2 * width), f32),
            jax.ShapeDtypeStruct((rows // QT, width, QT), f32),
        ],
        compiler_params=pltpu.CompilerParams(vmem_limit_bytes=50 * 1024 * 1024),
        cost_estimate=BRIEF,
        name="outer_back",
    )(*scalars, k, v, a, kseg, q, do, o, lse, qseg, weight, *deps)


def inner_back(scalars, k, v, a, kseg, q, do, o, lse, qseg, order, partial, *deps):
    rows, width = q.shape
    half = width // 2
    specs, scratch, whole = back_specs(rows, width, OWN, lambda step, *_: (step, 0))
    scratch += [
        pltpu.VMEM((width, 3 * width), f32),
        pltpu.VMEM((rows // QT, width, QT), f32),
        pltpu.VMEM((rows, width), bf),
    ]
    own = jax.ShapeDtypeStruct((rows, width), bf)
    message = jax.ShapeDtypeStruct((half, 3 * width), bf)
    return pl.pallas_call(
        inner_kernel,
        grid_spec=pltpu.PrefetchScalarGridSpec(
            num_scalar_prefetch=5,
            grid=(rows // OWN,),
            in_specs=specs + [whole] * 3 + [pl.BlockSpec(memory_space=pl.ANY)] * len(deps),
            out_specs=[specs[0], specs[0], whole, whole, whole, whole],
            scratch_shapes=scratch,
        ),
        out_shape=[own, own, own, message, message, jax.ShapeDtypeStruct((8, 128), f32)],
        compiler_params=pltpu.CompilerParams(vmem_limit_bytes=46 * 1024 * 1024),
        cost_estimate=BRIEF,
        name="inner_back",
    )(*scalars, k, v, a, kseg, q, do, o, lse, qseg, order, *partial, *deps)


def middle_kernel(places, x_ref, o_ref, dz_ref, gain_ref, order_ref, wo_ref, wh_ref, wp_ref,
                  mid_ref, hid_ref, hkeep_ref, hsend_ref, pkeep_ref, psend_ref, okeep_ref, osend_ref,
                  dx_ref, do_ref, normed, inverse, second, ordered, dsec, grads):
    step = pl.program_id(0)
    width = x_ref.shape[1]
    half = width // 2

    @pl.when(step == 0)
    def _():
        value = x_ref[...].astype(f32) + dot(o_ref[...], wo_ref[...])
        mid_ref[...] = value
        n, r = normalize_parts(value)
        normed[...] = n
        inverse[...] = jnp.broadcast_to(r, inverse.shape)
        b = (n * gain_ref[1:2, :]).astype(bf)
        second[...] = b
        ordered[...] = dot(b, order_ref[...]).astype(bf)
        dsec[...] = jnp.zeros(dsec.shape, f32)

    dz = dz_ref[...]
    wh = wh_ref[...]
    wp = wp_ref[...]
    u = dot(second[...], wh)
    cdf = 0.5 * (1.0 + lax.erf(u * (0.5 ** 0.5)))
    pdf = jnp.exp(-0.5 * u * u) * 0.3989422804014327
    hid = (u * cdf).astype(bf)
    du = (contract_cols(dz, wp) * (cdf + u * pdf)).astype(bf)
    hid_ref[...] = hid

    def put(keep_ref, send_ref, grad):
        grad = grad.astype(bf)
        keep_ref[...] = grad[:half]
        send_ref[...] = grad[half:]

    def put_rows(keep_ref, send_ref, left, right):
        blocks = places.shape[0]
        shard = width // blocks
        if shard % 8:
            put(keep_ref, send_ref, contract_rows(dot(left, order_ref[...]).astype(bf), right))
            return
        grads[...] = contract_rows(left, right)
        for j in range(0, blocks, 2):
            both = [
                grads[pl.ds(pl.multiple_of(places[j + i] * shard, 8), shard), :] for i in range(2)
            ]
            out, to = (keep_ref, j) if j < blocks // 2 else (send_ref, j - blocks // 2)
            out[to * shard:(to + 2) * shard, :] = jnp.concatenate(both, axis=0).astype(bf)

    put(hkeep_ref, hsend_ref, contract_rows(ordered[...], du))
    put_rows(pkeep_ref, psend_ref, hid, dz)
    dsec[...] += contract_cols(du, wh)

    @pl.when(step == pl.num_programs(0) - 1)
    def _():
        n = normed[...]
        db = dsec[...]
        dx = dz.astype(f32) + normalize_back(db, n, inverse[:, 0:1], gain_ref[1:2, :])
        dx_ref[...] = dx
        dproj = dx.astype(bf)
        put_rows(okeep_ref, osend_ref, o_ref[...], dproj)
        do_ref[...] = contract_cols(dproj, wo_ref[...]).astype(bf)


def middle(places, x, o, dz, gains, order, packed):
    rows, width = x.shape
    ratio = (packed.shape[1] - width) // (2 * width)
    whole = pl.BlockSpec(memory_space=pltpu.VMEM)
    line = jax.ShapeDtypeStruct((rows, width), f32)
    low = jax.ShapeDtypeStruct((rows, width), bf)
    half = width // 2
    part = pl.BlockSpec((half, width), lambda s, *_: (0, s))
    message = jax.ShapeDtypeStruct((half, ratio * width), bf)
    small = jax.ShapeDtypeStruct((half, width), bf)
    return pl.pallas_call(
        middle_kernel,
        grid_spec=pltpu.PrefetchScalarGridSpec(
            num_scalar_prefetch=1,
            grid=(ratio,),
            in_specs=[whole] * 5
            + [
                pl.BlockSpec((width, width), lambda s, *_: (0, 0)),
                pl.BlockSpec((width, width), lambda s, *_: (0, 1 + s)),
                pl.BlockSpec((width, width), lambda s, *_: (0, 1 + ratio + s)),
            ],
            out_specs=[whole, pl.BlockSpec((rows, width), lambda s, *_: (0, s))]
            + [part] * 4
            + [whole] * 4,
            scratch_shapes=[
                pltpu.VMEM((rows, width), f32),
                pltpu.VMEM((rows, 128), f32),
                pltpu.VMEM((rows, width), bf),
                pltpu.VMEM((rows, width), bf),
                pltpu.VMEM((rows, width), f32),
                pltpu.VMEM((width, width), f32),
            ],
        ),
        out_shape=[line, jax.ShapeDtypeStruct((rows, ratio * width), bf)]
        + [message] * 4
        + [small, small, line, low],
        compiler_params=pltpu.CompilerParams(vmem_limit_bytes=52 * 1024 * 1024),
        cost_estimate=BRIEF,
        name="middle",
    )(places, x, o, dz, gains, order, packed, packed, packed)


def out_kernel(mid_ref, hid_ref, wp_ref, out_ref, acc):
    step = pl.program_id(0)

    @pl.when(step == 0)
    def _():
        acc[...] = mid_ref[...]

    acc[...] += dot(hid_ref[...], wp_ref[...])

    @pl.when(step == pl.num_programs(0) - 1)
    def _():
        out_ref[...] = acc[...].astype(bf)


def layer_out(mid, hid, packed):
    rows, width = mid.shape
    ratio = hid.shape[1] // width
    whole = pl.BlockSpec(memory_space=pltpu.VMEM)
    return pl.pallas_call(
        out_kernel,
        grid=(ratio,),
        in_specs=[
            whole,
            pl.BlockSpec((rows, width), lambda s: (0, s)),
            pl.BlockSpec((width, width), lambda s: (0, 1 + ratio + s)),
        ],
        out_specs=whole,
        out_shape=jax.ShapeDtypeStruct((rows, width), bf),
        scratch_shapes=[pltpu.VMEM((rows, width), f32)],
        compiler_params=pltpu.CompilerParams(vmem_limit_bytes=58 * 1024 * 1024),
        cost_estimate=BRIEF,
        name="layer_out",
    )(mid, hid, packed)


def add(*arrays):
    total = arrays[0].astype(f32)
    for array in arrays[1:]:
        total += array.astype(f32)
    return total


class Links:
    def __init__(self, wide):
        self.wide = wide
        self.outer = wide // 4

    def swap(self, array, name):
        if name == "y":
            return lax.ppermute(array, "narrow", [(0, 1), (1, 0)])
        flip = 1 if name == "core" else 2
        return lax.ppermute(array, "wide", [(j, j ^ flip) for j in range(self.wide)])

    def flip_z(self, array, s):
        return lax.ppermute(array, "wide", [(j, j ^ (4 * s)) for j in range(self.wide)])

    def distance(self, at):
        bits = self.outer.bit_length() - 1
        return sum(((at >> b) & 1) << (bits - 1 - b) for b in range(bits))

    def order(self, width):
        place = lax.axis_index("wide")
        count = 2 * self.wide
        rows = width // count
        at = jnp.arange(count, dtype=jnp.int32)
        z, at = self.distance(at % self.outer) ^ (place // 4), at // self.outer
        y, at = (at + lax.axis_index("narrow")) % 2, at // 2
        x, at = (at + place // 2) % 2, at // 2
        core = (at + place) % 2
        places = ((z * 2 + x) * 2 + core) * 2 + y
        source = (places[:, None] * rows + jnp.arange(rows, dtype=jnp.int32)[None, :]).reshape(width)
        matrix = (jnp.arange(width, dtype=jnp.int32)[:, None] == source[None, :]).astype(bf)
        return places, matrix

    def along_z(self, shard):
        parts = [shard] + [self.flip_z(shard, self.distance(j)) for j in range(1, self.outer)]
        return jnp.concatenate(parts, axis=0)

    def along_xy(self, mine):
        cut = halfway(mine)
        one, two = mine[:, :cut], mine[:, cut:]
        one = jnp.concatenate([one, self.swap(one, "x")], axis=0)
        two = jnp.concatenate([two, self.swap(two, "y")], axis=0)
        one = (one, self.swap(one, "y"))
        two = (two, self.swap(two, "x"))
        return (
            one + tuple(self.swap(piece, "core") for piece in one),
            two + tuple(self.swap(piece, "core") for piece in two),
        )

    def first(self, pairs, *deps):
        rows = pairs[0][0].shape[0] // 4
        cuts = [halfway(keep) for keep, _ in pairs]
        wide = [sum(cuts), sum(keep.shape[1] for keep, _ in pairs) - sum(cuts)]

        def kernel(*refs):
            count = 2 * len(pairs)
            keep_x, send_x, keep_y, send_y = refs[-4:]
            at = [0, 0]
            for keep, got, cut in zip(refs[0:count:2], refs[1:count:2], cuts):
                rest = keep.shape[1] - cut
                one, two = slice(0, cut), slice(cut, cut + rest)
                to = slice(at[0], at[0] + cut)
                keep_x[:, to] = add(keep[:2 * rows, one], got[:2 * rows, one]).astype(bf)
                send_x[:, to] = add(keep[2 * rows:, one], got[2 * rows:, one]).astype(bf)
                to = slice(at[1], at[1] + rest)
                for j, out in enumerate((keep_y, send_y, keep_y, send_y)):
                    of = slice(j * rows, (j + 1) * rows)
                    into = slice(j // 2 * rows, (j // 2 + 1) * rows)
                    out[into, to] = add(keep[of, two], got[of, two]).astype(bf)
                at = [at[0] + cut, at[1] + rest]

        shapes = [(2 * rows, wide[0])] * 2 + [(2 * rows, wide[1])] * 2
        keep_x, send_x, keep_y, send_y = stage(kernel, sum(pairs, ()), deps, shapes)
        return (keep_x, keep_y), (self.swap(send_x, "x"), self.swap(send_y, "y"))

    def second(self, keep, got, *deps):
        rows = keep[0].shape[0] // 2

        def kernel(keep_x, keep_y, got_x, got_y, *refs):
            for keep, got, hold, send in ((keep_x, got_x, *refs[-4:-2]), (keep_y, got_y, *refs[-2:])):
                hold[...] = add(keep[:rows], got[:rows]).astype(bf)
                send[...] = add(keep[rows:], got[rows:]).astype(bf)

        shapes = [(rows, keep[0].shape[1])] * 2 + [(rows, keep[1].shape[1])] * 2
        keep_x, send_x, keep_y, send_y = stage(kernel, keep + got, deps, shapes)
        return (keep_x, keep_y), (self.swap(send_x, "y"), self.swap(send_y, "x"))

    def third(self, keep, got, *deps):
        cut = keep[0].shape[1]
        rows = keep[0].shape[0] // 2

        def kernel(keep_x, keep_y, got_x, got_y, *refs):
            hold, send = refs[-2:]
            for cols, keep, got in ((slice(0, cut), keep_x, got_x), (slice(cut, None), keep_y, got_y)):
                hold[:, cols] = add(keep[:rows], got[:rows]).astype(bf)
                send[:, cols] = add(keep[rows:], got[rows:]).astype(bf)

        hold, send = stage(kernel, keep + got, deps, [(rows, cut + keep[1].shape[1])] * 2)
        return hold, self.flip_z(send, 1)

    def fourth(self, keep, got, *deps):
        for bit in range(1, self.outer.bit_length() - 1):
            rows = keep.shape[0] // 2
            if rows % 8:
                total = add(keep, got).astype(bf)
                keep, send = total[:rows], total[rows:]
            else:
                keep, send = stage(halves_kernel, (keep, got), deps, [(rows, keep.shape[1])] * 2)
            got = self.flip_z(send, 1 << bit)
        return keep, got


def halves_kernel(keep, got, *refs):
    hold, send = refs[-2:]
    total = add(keep[...], got[...])
    hold[...] = total[:hold.shape[0]].astype(bf)
    send[...] = total[hold.shape[0]:].astype(bf)


def first_kernel(hidk, hidg, projk, projg, outk_x, outg_x, outk_y, outg_y, *refs):
    keep_x, send_x, keep_y, send_y = refs[-4:]
    rows = hidk.shape[0] // 4
    last = pl.num_programs(0) - 1

    def write(one, two):
        cols = slice(0, one[0].shape[1])
        keep_x[:, cols] = add(*(v[:2 * rows, :] for v in one)).astype(bf)
        send_x[:, cols] = add(*(v[2 * rows:, :] for v in one)).astype(bf)
        for j, out in enumerate((keep_y, send_y, keep_y, send_y)):
            of = slice(j * rows, (j + 1) * rows)
            out[j // 2 * rows:(j // 2 + 1) * rows, cols] = add(*(v[of, :] for v in two)).astype(bf)

    @pl.when(pl.program_id(0) < last)
    def _():
        write((hidk, hidg), (projk, projg))

    @pl.when(pl.program_id(0) == last)
    def _():
        write((outk_x, outg_x), (outk_y, outg_y))


class Middle:
    def __init__(self, links):
        self.links = links

    def first(self, hid, proj, out, *deps):
        rows, columns = hid[0].shape
        block = out[0].shape[1]
        steps = columns // block
        tile = pl.BlockSpec((rows, block), lambda j: (0, jnp.minimum(j, steps - 1)))
        half = [pl.BlockSpec((rows, block // 2), lambda j, at=at: (0, at)) for at in range(2)]
        shape = jax.ShapeDtypeStruct((rows // 2, columns + block // 2), bf)
        keep_x, send_x, keep_y, send_y = pl.pallas_call(
            first_kernel,
            grid=(steps + 1,),
            in_specs=[tile] * 4
            + [half[0]] * 2
            + [half[1]] * 2
            + [pl.BlockSpec(memory_space=pl.ANY)] * len(deps),
            out_specs=[pl.BlockSpec((rows // 2, block), lambda j: (0, j))] * 4,
            out_shape=[shape] * 4,
            compiler_params=pltpu.CompilerParams(vmem_limit_bytes=58 * 1024 * 1024),
            cost_estimate=BRIEF,
            name="first",
        )(*hid, *proj, *out, *out, *deps)
        return (keep_x, keep_y), (self.links.swap(send_x, "x"), self.links.swap(send_y, "y"))

    def second(self, keep, got, *deps):
        rows = keep[0].shape[0] // 4
        cut = keep[0].shape[1]

        def kernel(keep_x, keep_y, got_x, got_y, *refs):
            hold_x, hold_y, send = refs[-3:]
            halves = ((hold_x, slice(0, cut), keep_x, got_x), (hold_y, slice(cut, None), keep_y, got_y))
            for hold, cols, keep, got in halves:
                for j in range(2):
                    into = slice(j * rows, (j + 1) * rows)
                    of = slice(2 * j * rows, (2 * j + 1) * rows)
                    hold[into, :] = add(keep[of, :], got[of, :]).astype(bf)
                    of = slice((2 * j + 1) * rows, (2 * j + 2) * rows)
                    send[into, cols] = add(keep[of, :], got[of, :]).astype(bf)

        wide = keep[1].shape[1]
        shapes = [(2 * rows, cut), (2 * rows, wide), (2 * rows, cut + wide)]
        hold_x, hold_y, send = stage(kernel, keep + got, deps, shapes)
        return (hold_x, hold_y), self.links.flip_z(send, 1)

    def third(self, keep, got, *deps):
        rows = keep[0].shape[0] // 2
        cut = keep[0].shape[1]

        def kernel(keep_x, keep_y, got, *refs):
            for keep, cols, hold, send in (
                (keep_x, slice(0, cut), *refs[-4:-2]), (keep_y, slice(cut, None), *refs[-2:])
            ):
                hold[...] = add(keep[:rows, :], got[:rows, cols]).astype(bf)
                send[...] = add(keep[rows:, :], got[rows:, cols]).astype(bf)

        shapes = [(rows, cut)] * 2 + [(rows, keep[1].shape[1])] * 2
        hold_x, send_x, hold_y, send_y = stage(kernel, keep + (got,), deps, shapes)
        return (hold_x, hold_y), (self.links.swap(send_x, "y"), self.links.swap(send_y, "x"))

    def fourth(self, keep, got, *deps):
        rows = keep[0].shape[0] // 2
        cut = keep[0].shape[1]
        if rows % 8:
            total = jnp.concatenate([add(k, g).astype(bf) for k, g in zip(keep, got)], axis=1)
            hold, send = total[:rows], total[rows:]
        else:
            def kernel(keep_x, keep_y, got_x, got_y, *refs):
                hold, send = refs[-2:]
                for cols, keep, got in ((slice(0, cut), keep_x, got_x), (slice(cut, None), keep_y, got_y)):
                    total = add(keep[...], got[...])
                    hold[:, cols] = total[:rows].astype(bf)
                    send[:, cols] = total[rows:].astype(bf)

            hold, send = stage(kernel, keep + got, deps, [(rows, cut + keep[1].shape[1])] * 2)
        got = self.links.flip_z(send, 2)
        for bit in range(2, self.links.outer.bit_length() - 1):
            total = add(hold, got).astype(bf)
            rows = rows // 2
            hold, send = total[:rows], total[rows:]
            got = self.links.flip_z(send, 1 << bit)
        return hold, got


def collect(parts, *deps):
    def kernel(*refs):
        refs[-1][...] = add(*(ref[...] for ref in refs[:len(parts)]))

    return stage(kernel, parts, deps, [parts[0].shape], f32)[0]


def stage(kernel, operands, deps, shapes, kind=bf):
    whole = pl.BlockSpec(memory_space=pltpu.VMEM)
    elsewhere = pl.BlockSpec(memory_space=pl.ANY)
    return pl.pallas_call(
        kernel,
        in_specs=[whole] * len(operands) + [elsewhere] * len(deps),
        out_specs=[whole] * len(shapes),
        out_shape=[jax.ShapeDtypeStruct(shape, kind) for shape in shapes],
        compiler_params=pltpu.CompilerParams(vmem_limit_bytes=24 * 1024 * 1024),
        cost_estimate=BRIEF,
        name="stage",
    )(*operands, *deps)


def hold(values, *deps):
    count = len(values)
    elsewhere = pl.BlockSpec(memory_space=pl.ANY)
    return pl.pallas_call(
        lambda *refs: None,
        in_specs=[elsewhere] * (count + len(deps)),
        out_specs=[elsewhere] * count,
        out_shape=[jax.ShapeDtypeStruct(v.shape, v.dtype) for v in values],
        input_output_aliases={j: j for j in range(count)},
        cost_estimate=BRIEF,
        name="hold",
    )(*values, *deps)


def halfway(array):
    return (array.shape[1] // 2 + 127) // 128 * 128


def share_kernel(dq_ref, dk_ref, dv_ref, w_ref, *refs):
    refs[-1][...] = back_input(w_ref, (0, dq_ref[...]), (1, dk_ref[...]), (2, dv_ref[...]))


def own_share(own, weight, *deps):
    rows, width = own[0].shape
    tile = pl.BlockSpec((OWN, width), lambda i: (i, 0))
    return pl.pallas_call(
        share_kernel,
        grid=(rows // OWN,),
        in_specs=[tile] * 3
        + [pl.BlockSpec(memory_space=pltpu.VMEM)]
        + [pl.BlockSpec(memory_space=pl.ANY)] * len(deps),
        out_specs=tile,
        out_shape=jax.ShapeDtypeStruct((rows, width), f32),
        compiler_params=pltpu.CompilerParams(vmem_limit_bytes=58 * 1024 * 1024),
        cost_estimate=BRIEF,
        name="own_share",
    )(*own, weight, *deps)


def finish_kernel(x_ref, dx_ref, own_ref, b0, b1, b2, b3, gain_ref, out_ref):
    n, r = normalize_parts(x_ref[...].astype(f32))
    da = add(own_ref[...], b0[...], b1[...], b2[...], b3[...])
    out_ref[...] = (dx_ref[...] + normalize_back(da, n, r, gain_ref[0:1, :])).astype(bf)


def finish(x, dx, own, others, gains):
    rows, width = x.shape
    tile = pl.BlockSpec((OWN, width), lambda i: (i, 0))
    return pl.pallas_call(
        finish_kernel,
        grid=(rows // OWN,),
        in_specs=[tile] * 7 + [pl.BlockSpec(gains.shape, lambda i: (0, 0))],
        out_specs=tile,
        out_shape=jax.ShapeDtypeStruct((rows, width), bf),
        compiler_params=pltpu.CompilerParams(vmem_limit_bytes=58 * 1024 * 1024),
        cost_estimate=BRIEF,
        name="finish",
    )(x, dx, own, *others, gains)


def gain_sums(w_ref, grad, shape):
    product = w_ref[...].astype(bf).astype(f32) * grad
    return jnp.broadcast_to(jnp.sum(product, axis=1, keepdims=True), shape)


def update_kernel(rate_ref, sum_ref, hid_ref, proj_ref, w_ref, mom_out, mom_hid, mom_proj,
                  step_out, step_hid, step_proj, next_out, next_hid, next_proj, gain_ref):
    rate = rate_ref[0]
    hidden = hid_ref.shape[1]
    width = mom_out.shape[1]
    half = width // 2
    far = hidden + half

    def put(step, following, at, momentum, grad):
        value = momentum_rate * momentum + grad
        following[at] = value
        step[at] = rate * value

    gain_ref[...] = gain_sums(w_ref, hid_ref[...], gain_ref.shape)
    whole = slice(None)
    put(step_hid, next_hid, (whole, whole), mom_hid[...], hid_ref[...])
    for at, lo in ((slice(0, half), hidden), (slice(half, width), far + hidden)):
        put(step_out, next_out, (whole, at), mom_out[:, at], sum_ref[:, lo:lo + half])
    put(step_proj, next_proj, (whole, whole), mom_proj[...], proj_ref[...])


def update(rate, total, hid, proj, w_hid, mom_out, mom_hid, mom_proj):
    whole = pl.BlockSpec(memory_space=pltpu.VMEM)
    moms = (mom_out, mom_hid, mom_proj)
    return pl.pallas_call(
        update_kernel,
        in_specs=[pl.BlockSpec(memory_space=pltpu.SMEM)] + [whole] * 7,
        out_specs=[whole] * 7,
        out_shape=[jax.ShapeDtypeStruct(m.shape, f32) for m in moms + moms]
        + [jax.ShapeDtypeStruct((hid.shape[0], 128), f32)],
        cost_estimate=BRIEF,
        name="update",
    )(rate, total, hid, proj, w_hid, *moms)


def update_first_kernel(rate_ref, keep_ref, got_ref, w_ref, mom_ref, step_ref, next_ref, gain_ref):
    total = add(keep_ref[...], got_ref[...])
    gain_ref[...] = gain_sums(w_ref, total, gain_ref.shape)
    value = momentum_rate * mom_ref[...] + total
    next_ref[...] = value
    step_ref[...] = rate_ref[0] * value


def update_first(rate, keep, got, weight, mom):
    whole = pl.BlockSpec(memory_space=pltpu.VMEM)
    return pl.pallas_call(
        update_first_kernel,
        in_specs=[pl.BlockSpec(memory_space=pltpu.SMEM)] + [whole] * 4,
        out_specs=[whole] * 3,
        out_shape=[jax.ShapeDtypeStruct(mom.shape, f32)] * 2
        + [jax.ShapeDtypeStruct((mom.shape[0], 128), f32)],
        cost_estimate=BRIEF,
        name="update_first",
    )(rate, keep, got, weight, mom)


def body(
    joint_in,
    cotangent,
    segment_ids,
    layer_index,
    step_index,
    gain_one,
    w_qkv,
    w_attn_out,
    gain_two,
    w_hidden,
    w_proj,
    mom_gain_one,
    mom_qkv,
    mom_attn_out,
    mom_gain_two,
    mom_hidden,
    mom_proj,
):
    rows, width = joint_in.shape
    wide = lax.axis_size("wide")
    both = ("wide", "narrow")
    shard = w_qkv.shape[0]
    hidden = w_hidden.shape[1]
    ratio = hidden // width
    odd = lax.axis_index("narrow")
    place = lax.axis_index("wide") * 2 + odd
    window = 5 * rows
    is_even = odd == 0

    links = Links(wide)
    places, order = links.order(width)
    gains = jnp.stack([gain_one, gain_two], axis=1)
    gains = jnp.pad(gains, ((0, 0), (0, 126)))
    pack_a = jnp.concatenate([w_qkv.astype(bf), gains.astype(bf)], axis=1)
    hid_order = w_hidden.astype(bf).reshape(shard, width, ratio).transpose(0, 2, 1)
    pack_b = jnp.concatenate(
        [
            w_attn_out.astype(bf),
            hid_order.reshape(shard, hidden),
            w_proj.astype(bf).reshape(shard, hidden),
        ],
        axis=1,
    )

    fill = jnp.full((2 * rows,), -1, jnp.int32)
    ids = jnp.concatenate([fill, segment_ids, fill])
    key_ids = lax.dynamic_slice_in_dim(ids, place * rows, window, 0)
    own_ids = lax.dynamic_slice_in_dim(segment_ids, place * rows, rows, 0)
    tiles = own_ids.reshape(rows // QT, QT)
    far_ids = jnp.concatenate([key_ids[:2 * rows], key_ids[3 * rows:]])
    kseg = jnp.broadcast_to(far_ids[:, None], (4 * rows, QT))
    oseg = jnp.broadcast_to(own_ids[:, None], (rows, QT))
    qseg = jnp.broadcast_to(tiles[:, None, :], (rows // QT, 8, QT))
    origin = (place - 2) * rows
    low = jnp.sum(segment_ids[None, :] < tiles[:, :1], axis=1, dtype=jnp.int32) - origin
    high = jnp.sum(segment_ids[None, :] <= tiles[:, -1:], axis=1, dtype=jnp.int32) - origin
    low = jnp.clip(low, 0, window)
    high = jnp.clip(high, 0, window)
    side = 2 * rows // OUTER
    starts = [2 * rows + j * OWN for j in range(rows // OWN)]
    starts += [j * OUTER for j in range(side)] + [3 * rows + j * OUTER for j in range(side)]
    sizes = [OWN] * (rows // OWN) + [OUTER] * (2 * side)
    edges = jnp.asarray(starts, jnp.int32)[:, None]
    tops = jnp.asarray([at + size for at, size in zip(starts, sizes)], jnp.int32)[:, None]
    begin = jnp.sum(high[None, :] <= edges, axis=1, dtype=jnp.int32)
    end = jnp.sum(low[None, :] < tops, axis=1, dtype=jnp.int32)
    near = jnp.minimum(low[0] // OUTER, side)
    last = side - 1 + jnp.maximum(high[-1] - 3 * rows + OUTER - 1, 0) // OUTER
    span = jnp.stack([near, jnp.maximum(last, near)])
    scalars = (begin, end, span, odd.reshape(1), places)

    swap = [(0, 1), (1, 0)]
    up = [(j, j + 1) for j in range(wide - 1)]
    down = [(j + 1, j) for j in range(wide - 1)]
    across = [(2 * j, 2 * j + 2) for j in range(wide - 1)]
    across += [(2 * j + 3, 2 * j + 1) for j in range(wide - 1)]
    partner = lax.ppermute(joint_in, "narrow", swap)
    before = lax.ppermute(joint_in, "wide", up)
    behind = lax.ppermute(joint_in, "wide", down)
    mine_a = links.along_z(pack_a)
    fourth = lax.ppermute(partner, both, across)
    ones, twos = links.along_xy(mine_a)
    blocks = (before, partner, fourth, behind)
    (pack_b,) = hold((pack_b,), before, partner, behind, mine_a)
    full_b = lax.all_gather(pack_b, both, axis=0, tiled=True)

    weight, gains, a_own, k_own, v_own, a_far, k_far, v_far, q, o, lse = attend(
        scalars, blocks, kseg, oseg, joint_in, qseg, order, ones, twos
    )

    mid, hid, hid_keep, hid_send, proj_keep, proj_send, out_keep, out_send, dx, do = middle(
        places, joint_in, o, cotangent, gains, order, full_b
    )
    joint_out = layer_out(mid, hid, full_b)
    chain = Middle(links)
    keep_b, got_b = chain.first(
        (hid_keep, links.swap(hid_send, "core")),
        (proj_keep, links.swap(proj_send, "core")),
        (out_keep, links.swap(out_send, "core")),
        joint_out,
    )
    args = (q, do, o, lse, qseg)
    da_before, da_partner, da_fourth, da_behind, *partial = outer_back(
        scalars, k_far, v_far, a_far, kseg, *args, weight, *keep_b
    )

    keep_b, got_b = chain.second(keep_b, got_b, da_before)
    home = [(2 * j + 2, 2 * j + 1) for j in range(wide - 1)]
    home += [(t, s) for s, t in home]
    others = (
        lax.ppermute(da_before, "wide", down),
        lax.ppermute(da_partner, "narrow", swap),
        lax.ppermute(da_fourth, both, home),
        lax.ppermute(da_behind, "wide", up),
    )
    dk, dv, dq, keep_a, send_a, token = inner_back(
        scalars, k_own, v_own, a_own, oseg, *args, order, partial, *keep_b
    )

    keep_b, got_b = chain.third(keep_b, got_b, token)
    da_own = own_share((dq, dk, dv), weight, *keep_b)
    (send_a,) = hold((send_a,), da_own, *others, *keep_b)
    got_a = links.swap(send_a, "core")
    keep_a, got_a = links.first([(keep_a, got_a)])
    keep_b, got_b = chain.fourth(keep_b, got_b, *keep_a)
    (gains,) = hold((gains,), keep_b)
    grad_in = finish(joint_in, dx, da_own, others, gains)
    keep_a, got_a = links.second(keep_a, got_a, grad_in)
    sum_b = collect((keep_b, got_b), *keep_a)
    keep_a, got_a = links.third(keep_a, got_a, sum_b)
    keep_a, got_a = links.fourth(keep_a, got_a)

    rate = base_rate * jnp.power(jnp.float32(decay_rate), (11 - layer_index).astype(f32))
    rate = rate * jnp.power(1.0 - step_index.astype(f32) / total_steps, 0.9)
    sum_hid = sum_b[:, :hidden].reshape(shard, ratio, width).transpose(0, 2, 1)
    sum_hid = sum_hid.reshape(shard, hidden)
    far = hidden + width // 2
    sum_proj = sum_b[:, far:far + hidden].reshape(shard * ratio, width)
    step_out, step_hid, step_proj, next_out, next_hid, next_proj, gain_b = update(
        rate, sum_b, sum_hid, sum_proj, w_hidden, mom_attn_out, mom_hidden, mom_proj
    )
    step_qkv, next_qkv, gain_a = update_first(rate, keep_a, got_a, w_qkv, mom_qkv)
    next_g1 = momentum_rate * mom_gain_one + gain_a[:, 0] / gain_one.astype(bf).astype(f32)
    next_g2 = momentum_rate * mom_gain_two + gain_b[:, 0] / gain_two.astype(bf).astype(f32)
    return (
        joint_out,
        grad_in,
        rate * next_g1,
        step_qkv,
        step_out,
        rate * next_g2,
        step_hid,
        step_proj,
        next_g1,
        next_qkv,
        next_out,
        next_g2,
        next_hid,
        next_proj,
    )


def solution(mesh):
    split = P(("wide", "narrow"), None)
    line = P(("wide", "narrow"))
    params = (line, split, split, line, split, split)
    return jax.shard_map(
        body,
        mesh=mesh,
        in_specs=(split, split, P(), P(), P()) + params + params,
        out_specs=(split, split) + params + params,
        check_vma=False,
    )
```

```python
import functools

import jax
import jax.numpy as jnp
from jax import lax
from jax.experimental import pallas as pl
from jax.experimental.pallas import tpu as pltpu
from jax.sharding import PartitionSpec as P

HEAD = 64
PAIR = 2 * HEAD
QT = 128
OWN = 320
OUTER = 256
GROUP = 3
BRIEF = pl.CostEstimate(flops=1, bytes_accessed=1, transcendentals=0)

eps = 1e-06
base_rate = 0.01
decay_rate = 0.65
total_steps = 100000.0
momentum_rate = 0.9

bf = jnp.bfloat16
f32 = jnp.float32


def dot(left, right):
    return jnp.dot(left, right, preferred_element_type=f32)


def contract_rows(left, right):
    return lax.dot_general(
        left, right, (((0,), (0,)), ((), ())), preferred_element_type=f32
    )


def contract_cols(left, right):
    return lax.dot_general(
        left, right, (((1,), (1,)), ((), ())), preferred_element_type=f32
    )


def normalize_parts(values):
    centre = jnp.mean(values, axis=-1, keepdims=True)
    centred = values - centre
    inverse = lax.rsqrt(jnp.mean(centred * centred, axis=-1, keepdims=True) + eps)
    return (centred * inverse, inverse)


def normalize_back(grad_out, normed, inverse, gain):
    grad_normed = grad_out * gain
    inner = grad_normed - jnp.mean(grad_normed, axis=-1, keepdims=True)
    inner = inner - normed * jnp.mean(grad_normed * normed, axis=-1, keepdims=True)
    return inverse * inner


def diag_wide(block):
    row = lax.broadcasted_iota(jnp.int32, block.shape, 0)
    zero = jnp.zeros_like(block)
    return jnp.concatenate(
        [jnp.where(row < HEAD, block, zero), jnp.where(row >= HEAD, block, zero)], axis=1
    )


def diag_tall(block):
    col = lax.broadcasted_iota(jnp.int32, block.shape, 1)
    zero = jnp.zeros_like(block)
    return jnp.concatenate(
        [jnp.where(col < HEAD, block, zero), jnp.where(col >= HEAD, block, zero)], axis=0
    )


def tile_bias(segments, qseg_ref, t):
    bias = jnp.where(segments == qseg_ref[t, 0:1, :], 0.0, -1e30).astype(f32)
    return jnp.concatenate([bias, bias], axis=1)


def columns_of(pair):
    return slice(pair * PAIR, (pair + 1) * PAIR)


def block_starts(odd, size):
    return (0, (2 - odd) * size, (1 + odd) * size, 3 * size)


def pieces_of(tile, odd, refs, size):
    for part in range(OUTER // QT):
        at = tile * (OUTER // QT) + part
        for ref, start in zip(refs, block_starts(odd, size)):
            yield (at >= start) & (at < start + size), ref, at - start, part


def copy_rows(tile, odd, refs, size, out):
    for number, (here, _, _, part) in enumerate(pieces_of(tile, odd, refs[:4], size)):
        ref = refs[number]

        @pl.when(here)
        def _(ref=ref, part=part):
            out[part * QT:(part + 1) * QT, :] = ref[...]


def block_specs(width, size, key):
    def spec(part, number):
        def index(step, begin, end, span, odd, places):
            at = key(step) * (OUTER // QT) + part
            return (jnp.clip(at - block_starts(odd[0], size)[number], 0, size - 1), 0)

        return pl.BlockSpec((QT, width), index)

    return [spec(part, number) for part in range(OUTER // QT) for number in range(4)]


def in_pairs(first, last, visit):
    twos = (last - first) // 2

    def two(j, carry):
        visit([first + 2 * j, first + 2 * j + 1])
        return carry

    lax.fori_loop(0, twos, two, 0)

    @pl.when(first + 2 * twos < last)
    def _():
        visit([last - 1])


def attend_kernel(begin, end, span, odd, places, *refs, pieces):
    count = 4 * OUTER // QT
    blocks, (kseg_ref, oseg_ref, own_ref, qseg_ref, order_ref) = refs[:count], refs[count:count + 5]
    parts = refs[count + 5:count + 5 + 2 * pieces]
    (w_ref, gains_ref, ao_ref, ko_ref, vo_ref, a_ref, k_ref, v_ref, q_ref, o_ref, lse_ref,
     qbd, top, total, acc, x_ref, rel_ref) = refs[count + 5 + 2 * pieces:]
    step = pl.program_id(0)
    rows, width = own_ref.shape
    pairs = width // PAIR
    tiles = qseg_ref.shape[0]
    scale = HEAD ** (-0.5)

    def project(x):
        n, _ = normalize_parts(x.astype(f32))
        a = (n * gains_ref[0:1, :]).astype(bf)
        k = dot(a, w_ref[:, width:2 * width]).astype(bf)
        return a, k, dot(a, w_ref[:, 2 * width:3 * width]).astype(bf)

    def visit(queries, keys, values, segments):
        group = [(t, p) for t in queries for p in range(pairs)]
        bias = [tile_bias(segments, qseg_ref, t) for t in queries]
        scores = [
            dot(keys(columns_of(p)), qbd[t, p]) + bias[j // pairs] for j, (t, p) in enumerate(group)
        ]
        olds = [top[t, p:p + 1, :] for t, p in group]
        news = [jnp.maximum(old, jnp.max(s, axis=0, keepdims=True)) for old, s in zip(olds, scores)]
        expo = [jnp.exp(s - new) for s, new in zip(scores, news)]
        shrinks = [jnp.exp(old - new) for old, new in zip(olds, news)]
        sums = [
            total[t, p:p + 1, :] * shrink + jnp.sum(e, axis=0, keepdims=True)
            for (t, p), shrink, e in zip(group, shrinks, expo)
        ]
        gots = [
            contract_rows(values(columns_of(p)), e.astype(bf)) for (t, p), e in zip(group, expo)
        ]
        for (t, p), new, shrink, summed, got in zip(group, news, shrinks, sums, gots):
            top[t, p:p + 1, :] = new
            total[t, p:p + 1, :] = summed
            lo, mid, hi = p * PAIR, p * PAIR + HEAD, (p + 1) * PAIR
            acc[t, lo:mid, :] = acc[t, lo:mid, :] * shrink[:, :QT] + got[:HEAD, :QT]
            acc[t, mid:hi, :] = acc[t, mid:hi, :] * shrink[:, QT:] + got[HEAD:, QT:]

    @pl.when(step == 0)
    def _():
        size = parts[0].shape[0] // 2
        cut = parts[0].shape[1]
        shard = size // (places.shape[0] // 8)
        halves = (slice(0, cut), slice(cut, rel_ref.shape[1]))
        for j in range(pieces):
            for h in range(2):
                of = slice(h * size, (h + 1) * size)
                core, other = j // 2 * 4, j % 2
                for block, cols, part in (
                    (core + 2 * h + other, halves[0], parts[j]),
                    (core + 2 * other + h, halves[1], parts[pieces + j]),
                ):
                    value = part[of, :].astype(f32)
                    if shard % 8:
                        rel_ref[block * size:(block + 1) * size, cols] = value
                        continue
                    for z in range(size // shard):
                        to = pl.multiple_of(places[block * (size // shard) + z] * shard, 8)
                        rel_ref[pl.ds(to, shard), cols] = value[z * shard:(z + 1) * shard]
        if shard % 8:
            w_ref[...] = dot(order_ref[...], rel_ref[...].astype(bf)).astype(bf)
        else:
            w_ref[...] = rel_ref[...].astype(bf)
        gains_ref[...] = w_ref[:, 3 * width:].astype(f32).T[:8]
        a, k, v = project(own_ref[...])
        ao_ref[...] = a
        ko_ref[...] = k
        vo_ref[...] = v
        q = dot(a, w_ref[:, :width]).astype(bf)
        q_ref[...] = q
        q = q.astype(f32) * scale
        for t in range(tiles):
            for p in range(pairs):
                qbd[t, p] = diag_wide(q[t * QT:(t + 1) * QT, columns_of(p)].T.astype(bf))
        top[...] = jnp.full(top.shape, -1e30, f32)
        total[...] = jnp.zeros(total.shape, f32)
        acc[...] = jnp.zeros(acc.shape, f32)

        def own(h, carry):
            at = pl.ds(pl.multiple_of(h * OWN, OWN), OWN)
            in_pairs(
                begin[h], end[h],
                lambda ts: visit(
                    ts, lambda c: ko_ref[at, c], lambda c: vo_ref[at, c], oseg_ref[at, :]
                ),
            )
            return carry

        lax.fori_loop(0, rows // OWN, own, 0)

    number = step - 1 + rows // OWN

    @pl.when((step > 0) & (begin[number] < end[number]))
    def _():
        copy_rows(step - 1, odd[0], blocks, rows // QT, x_ref)
        a, k, v = project(x_ref[...])
        a_ref[...] = a
        k_ref[...] = k
        v_ref[...] = v
        in_pairs(
            begin[number], end[number],
            lambda ts: visit(ts, lambda c: k_ref[:, c], lambda c: v_ref[:, c], kseg_ref[...]),
        )

    @pl.when(step == pl.num_programs(0) - 1)
    def _():
        for t in range(tiles):
            for p in range(pairs):
                sums = total[t, p:p + 1, :]
                lse_ref[t, p] = top[t, p:p + 1, :] + jnp.log(sums)
                inv = 1.0 / sums
                lo, mid, hi = p * PAIR, p * PAIR + HEAD, (p + 1) * PAIR
                out = jnp.concatenate(
                    [acc[t, lo:mid, :] * inv[:, :QT], acc[t, mid:hi, :] * inv[:, QT:]], axis=0
                )
                o_ref[t * QT:(t + 1) * QT, lo:hi] = out.T.astype(bf)


def attend(scalars, blocks, kseg, oseg, x_own, qseg, order, ones, twos):
    rows, width = x_own.shape
    outer = 4 * rows
    tiles = rows // QT
    pairs = width // PAIR
    columns = ones[0].shape[1] + twos[0].shape[1]
    whole = pl.BlockSpec(memory_space=pltpu.VMEM)

    def at_used(step, begin, end, span, odd, places):
        return (jnp.clip(step - 1, span[0], span[1]), 0)

    tile = pl.BlockSpec((OUTER, width), at_used)
    own = jax.ShapeDtypeStruct((rows, width), bf)
    far = jax.ShapeDtypeStruct((outer, width), bf)
    return pl.pallas_call(
        functools.partial(attend_kernel, pieces=len(ones)),
        grid_spec=pltpu.PrefetchScalarGridSpec(
            num_scalar_prefetch=5,
            grid=(1 + outer // OUTER,),
            in_specs=block_specs(width, rows // QT, lambda step: step - 1)
            + [pl.BlockSpec((OUTER, QT), at_used)]
            + [whole] * (4 + 2 * len(ones)),
            out_specs=[whole] * 5 + [tile] * 3 + [whole] * 3,
            scratch_shapes=[
                pltpu.VMEM((tiles, pairs, PAIR, 2 * QT), bf),
                pltpu.VMEM((tiles, 8, 2 * QT), f32),
                pltpu.VMEM((tiles, 8, 2 * QT), f32),
                pltpu.VMEM((tiles, width, QT), f32),
                pltpu.VMEM((OUTER, width), bf),
                pltpu.VMEM((width, columns), f32),
            ],
        ),
        out_shape=[
            jax.ShapeDtypeStruct((width, columns), bf),
            jax.ShapeDtypeStruct((8, width), f32),
            own,
            own,
            own,
            far,
            far,
            far,
            own,
            own,
            jax.ShapeDtypeStruct((tiles, pairs, 1, 2 * QT), f32),
        ],
        compiler_params=pltpu.CompilerParams(vmem_limit_bytes=56 * 1024 * 1024),
        cost_estimate=BRIEF,
        name="attend",
    )(*scalars, *(blocks * (OUTER // QT)), kseg, oseg, x_own, qseg, order, *ones, *twos)


def back_tile(first, last, refs, scratch):
    k_ref, v_ref, kseg_ref, qseg_ref, lse_ref = refs
    qbd, dobd, qn, don, delta, dq_acc, dk_acc, dv_acc = scratch
    pairs = qbd.shape[1]
    dk_acc[...] = jnp.zeros(dk_acc.shape, f32)
    dv_acc[...] = jnp.zeros(dv_acc.shape, f32)

    def visit(t):
        bias = tile_bias(kseg_ref[...], qseg_ref, t)
        for base in range(0, pairs, GROUP):
            group = range(base, min(pairs, base + GROUP))
            keys = [k_ref[:, columns_of(p)] for p in group]
            scores = [dot(kp, qbd[t, p]) for kp, p in zip(keys, group)]
            dprobs = [dot(v_ref[:, columns_of(p)], dobd[t, p]) for p in group]
            probs = [jnp.exp(s + bias - lse_ref[t, p]) for s, p in zip(scores, group)]
            ds = [
                (pr * (dp - delta[t, p:p + 1, :])).astype(bf)
                for pr, dp, p in zip(probs, dprobs, group)
            ]
            got_v = [dot(pr.astype(bf), don[t, p]) for pr, p in zip(probs, group)]
            got_k = [dot(d, qn[t, p]) for d, p in zip(ds, group)]
            got_q = [contract_rows(kp, d) for kp, d in zip(keys, ds)]
            for i, p in enumerate(group):
                lo, mid, hi = p * PAIR, p * PAIR + HEAD, (p + 1) * PAIR
                dv_acc[:, lo:hi] += got_v[i]
                dk_acc[:, lo:hi] += got_k[i]
                dq_acc[t, lo:mid, :] += got_q[i][:HEAD, :QT]
                dq_acc[t, mid:hi, :] += got_q[i][HEAD:, QT:]

    def visits(ts):
        for t in ts:
            visit(t)

    in_pairs(first, last, visits)
    return dk_acc[...].astype(bf), dv_acc[...].astype(bf)


def back_prepare(q_ref, do_ref, o_ref, scratch):
    qbd, dobd, qn, don, delta = scratch
    tiles, pairs = qbd.shape[:2]
    scale = HEAD ** (-0.5)
    for t in range(tiles):
        at = slice(t * QT, (t + 1) * QT)
        for p in range(pairs):
            cols = columns_of(p)
            q = q_ref[at, cols].astype(f32) * scale
            do = do_ref[at, cols].astype(f32)
            do_t = do.T
            qbd[t, p] = diag_wide(q.T.astype(bf))
            dobd[t, p] = diag_wide(do_t.astype(bf))
            qn[t, p] = diag_tall(q.astype(bf))
            don[t, p] = diag_tall(do.astype(bf))
            both = do_t * o_ref[at, cols].astype(f32).T
            delta[t, p:p + 1, :QT] = jnp.sum(both[:HEAD], axis=0, keepdims=True)
            delta[t, p:p + 1, QT:] = jnp.sum(both[HEAD:], axis=0, keepdims=True)


def back_input(w_ref, *grads):
    width = w_ref.shape[0]
    total = 0.0
    for number, grad in grads:
        total += contract_cols(grad, w_ref[:, number * width:(number + 1) * width])
    return total


def back_weights(dk, dv, a, acc, lo):
    width = dk.shape[1]
    acc[:, lo:lo + width] += contract_rows(a, dk)
    acc[:, lo + width:lo + 2 * width] += contract_rows(a, dv)


def outer_kernel(begin, end, span, odd, places, k_ref, v_ref, a_ref, kseg_ref, q_ref, do_ref, o_ref,
                 lse_ref, qseg_ref, w_ref, *refs):
    da_refs = refs[-13:-9]
    acc_ref, dq_ref, qbd, dobd, qn, don, delta, dk_acc, dv_acc = refs[-9:]
    step = pl.program_id(0)
    size = q_ref.shape[0] // QT
    number = step + q_ref.shape[0] // OWN

    @pl.when(step == 0)
    def _():
        back_prepare(q_ref, do_ref, o_ref, (qbd, dobd, qn, don, delta))
        acc_ref[...] = jnp.zeros(acc_ref.shape, f32)
        dq_ref[...] = jnp.zeros(dq_ref.shape, f32)

    used = begin[number] < end[number]

    def put(value):
        for here, ref, at, part in pieces_of(step, odd[0], da_refs, size):
            @pl.when(here)
            def _(ref=ref, at=at, part=part):
                ref[pl.ds(pl.multiple_of(at * QT, QT), QT), :] = value[part * QT:(part + 1) * QT]

    @pl.when(used)
    def _():
        dk, dv = back_tile(
            begin[number], end[number], (k_ref, v_ref, kseg_ref, qseg_ref, lse_ref),
            (qbd, dobd, qn, don, delta, dq_ref, dk_acc, dv_acc),
        )
        back_weights(dk, dv, a_ref[...], acc_ref, 0)
        put(back_input(w_ref, (1, dk), (2, dv)).astype(bf))

    @pl.when(jnp.logical_not(used))
    def _():
        put(jnp.zeros(k_ref.shape, bf))


def inner_kernel(begin, end, span, odd, places, k_ref, v_ref, a_ref, kseg_ref, q_ref, do_ref, o_ref,
                 lse_ref, qseg_ref, order_ref, acc_in, dq_in, *refs):
    (dk_ref, dv_ref, dq_ref, keep_ref, send_ref, token_ref,
     qbd, dobd, qn, don, delta, dk_acc, dv_acc, acc, dq_acc, a_all) = refs[-16:]
    step = pl.program_id(0)
    width = k_ref.shape[1]
    half = width // 2
    tiles, pairs = qbd.shape[:2]

    @pl.when(step == 0)
    def _():
        back_prepare(q_ref, do_ref, o_ref, (qbd, dobd, qn, don, delta))
        token_ref[...] = jnp.zeros(token_ref.shape, f32)
        acc[:, width:3 * width] = acc_in[...]
        dq_acc[...] = dq_in[...]

    dk, dv = back_tile(
        begin[step], end[step], (k_ref, v_ref, kseg_ref, qseg_ref, lse_ref),
        (qbd, dobd, qn, don, delta, dq_acc, dk_acc, dv_acc),
    )
    dk_ref[...] = dk
    dv_ref[...] = dv
    back_weights(dk, dv, a_ref[...], acc, width)
    a_all[pl.ds(pl.multiple_of(step * OWN, OWN), OWN), :] = a_ref[...]

    @pl.when(step == pl.num_programs(0) - 1)
    def _():
        scale = HEAD ** (-0.5)
        for t in range(tiles):
            for p in range(pairs):
                cols = columns_of(p)
                dq_ref[t * QT:(t + 1) * QT, cols] = (dq_acc[t, cols, :] * scale).T.astype(bf)
        acc[:, :width] = contract_rows(a_all[...], dq_ref[...])
        blocks = places.shape[0]
        shard = width // blocks
        if shard % 8:
            both = contract_rows(order_ref[...], acc[...].astype(bf)).astype(bf)
            keep_ref[...] = both[:half]
            send_ref[...] = both[half:]
            return
        for j in range(0, blocks, 2):
            both = [
                acc[pl.ds(pl.multiple_of(places[j + i] * shard, 8), shard), :] for i in range(2)
            ]
            out, to = (keep_ref, j) if j < blocks // 2 else (send_ref, j - blocks // 2)
            out[to * shard:(to + 2) * shard, :] = jnp.concatenate(both, axis=0).astype(bf)


def back_specs(rows, width, tile_rows, at_key):
    tiles = rows // QT
    pairs = width // PAIR
    whole = pl.BlockSpec(memory_space=pltpu.VMEM)
    tile = pl.BlockSpec((tile_rows, width), at_key)
    specs = [tile, tile, tile, pl.BlockSpec((tile_rows, QT), at_key)] + [whole] * 5
    scratch = [
        pltpu.VMEM((tiles, pairs, PAIR, 2 * QT), bf),
        pltpu.VMEM((tiles, pairs, PAIR, 2 * QT), bf),
        pltpu.VMEM((tiles, pairs, 2 * QT, PAIR), bf),
        pltpu.VMEM((tiles, pairs, 2 * QT, PAIR), bf),
        pltpu.VMEM((tiles, 8, 2 * QT), f32),
        pltpu.VMEM((tile_rows, width), f32),
        pltpu.VMEM((tile_rows, width), f32),
    ]
    return specs, scratch, whole


def outer_back(scalars, k, v, a, kseg, q, do, o, lse, qseg, weight, *deps):
    rows, width = q.shape

    def at_key(step, begin, end, span, odd, places):
        return (jnp.clip(step, span[0], span[1]), 0)

    specs, scratch, whole = back_specs(rows, width, OUTER, at_key)
    return pl.pallas_call(
        outer_kernel,
        grid_spec=pltpu.PrefetchScalarGridSpec(
            num_scalar_prefetch=5,
            grid=(k.shape[0] // OUTER,),
            in_specs=specs + [whole] + [pl.BlockSpec(memory_space=pl.ANY)] * len(deps),
            out_specs=[whole] * 6,
            scratch_shapes=scratch,
        ),
        out_shape=[
            *[jax.ShapeDtypeStruct((rows, width), bf)] * 4,
            jax.ShapeDtypeStruct((width, 2 * width), f32),
            jax.ShapeDtypeStruct((rows // QT, width, QT), f32),
        ],
        compiler_params=pltpu.CompilerParams(vmem_limit_bytes=50 * 1024 * 1024),
        cost_estimate=BRIEF,
        name="outer_back",
    )(*scalars, k, v, a, kseg, q, do, o, lse, qseg, weight, *deps)


def inner_back(scalars, k, v, a, kseg, q, do, o, lse, qseg, order, partial, *deps):
    rows, width = q.shape
    half = width // 2
    specs, scratch, whole = back_specs(rows, width, OWN, lambda step, *_: (step, 0))
    scratch += [
        pltpu.VMEM((width, 3 * width), f32),
        pltpu.VMEM((rows // QT, width, QT), f32),
        pltpu.VMEM((rows, width), bf),
    ]
    own = jax.ShapeDtypeStruct((rows, width), bf)
    message = jax.ShapeDtypeStruct((half, 3 * width), bf)
    return pl.pallas_call(
        inner_kernel,
        grid_spec=pltpu.PrefetchScalarGridSpec(
            num_scalar_prefetch=5,
            grid=(rows // OWN,),
            in_specs=specs + [whole] * 3 + [pl.BlockSpec(memory_space=pl.ANY)] * len(deps),
            out_specs=[specs[0], specs[0], whole, whole, whole, whole],
            scratch_shapes=scratch,
        ),
        out_shape=[own, own, own, message, message, jax.ShapeDtypeStruct((8, 128), f32)],
        compiler_params=pltpu.CompilerParams(vmem_limit_bytes=46 * 1024 * 1024),
        cost_estimate=BRIEF,
        name="inner_back",
    )(*scalars, k, v, a, kseg, q, do, o, lse, qseg, order, *partial, *deps)


def middle_kernel(places, x_ref, o_ref, dz_ref, gain_ref, order_ref, wo_ref, wh_ref, wp_ref,
                  mid_ref, hid_ref, hkeep_ref, hsend_ref, pkeep_ref, psend_ref, okeep_ref, osend_ref,
                  dx_ref, do_ref, normed, inverse, second, ordered, dsec, grads):
    step = pl.program_id(0)
    width = x_ref.shape[1]
    half = width // 2

    @pl.when(step == 0)
    def _():
        value = x_ref[...].astype(f32) + dot(o_ref[...], wo_ref[...])
        mid_ref[...] = value
        n, r = normalize_parts(value)
        normed[...] = n
        inverse[...] = jnp.broadcast_to(r, inverse.shape)
        b = (n * gain_ref[1:2, :]).astype(bf)
        second[...] = b
        if width // places.shape[0] % 8:
            ordered[...] = dot(b, order_ref[...]).astype(bf)
        dsec[...] = jnp.zeros(dsec.shape, f32)

    dz = dz_ref[...]
    wh = wh_ref[...]
    wp = wp_ref[...]
    u = dot(second[...], wh)
    cdf = 0.5 * (1.0 + lax.erf(u * (0.5 ** 0.5)))
    pdf = jnp.exp(-0.5 * u * u) * 0.3989422804014327
    hid = (u * cdf).astype(bf)
    du = (contract_cols(dz, wp) * (cdf + u * pdf)).astype(bf)
    hid_ref[...] = hid

    def put(keep_ref, send_ref, grad):
        grad = grad.astype(bf)
        keep_ref[...] = grad[:half]
        send_ref[...] = grad[half:]

    def put_rows(keep_ref, send_ref, left, right):
        blocks = places.shape[0]
        shard = width // blocks
        if shard % 8:
            put(keep_ref, send_ref, contract_rows(dot(left, order_ref[...]).astype(bf), right))
            return
        grads[...] = contract_rows(left, right)
        for j in range(0, blocks, 2):
            both = [
                grads[pl.ds(pl.multiple_of(places[j + i] * shard, 8), shard), :] for i in range(2)
            ]
            out, to = (keep_ref, j) if j < blocks // 2 else (send_ref, j - blocks // 2)
            out[to * shard:(to + 2) * shard, :] = jnp.concatenate(both, axis=0).astype(bf)

    if width // places.shape[0] % 8:
        put(hkeep_ref, hsend_ref, contract_rows(ordered[...], du))
    else:
        put_rows(hkeep_ref, hsend_ref, second[...], du)
    put_rows(pkeep_ref, psend_ref, hid, dz)
    dsec[...] += contract_cols(du, wh)

    @pl.when(step == pl.num_programs(0) - 1)
    def _():
        n = normed[...]
        db = dsec[...]
        dx = dz.astype(f32) + normalize_back(db, n, inverse[:, 0:1], gain_ref[1:2, :])
        dx_ref[...] = dx
        dproj = dx.astype(bf)
        put_rows(okeep_ref, osend_ref, o_ref[...], dproj)
        do_ref[...] = contract_cols(dproj, wo_ref[...]).astype(bf)


def middle(places, x, o, dz, gains, order, packed):
    rows, width = x.shape
    ratio = (packed.shape[1] - width) // (2 * width)
    whole = pl.BlockSpec(memory_space=pltpu.VMEM)
    line = jax.ShapeDtypeStruct((rows, width), f32)
    low = jax.ShapeDtypeStruct((rows, width), bf)
    half = width // 2
    part = pl.BlockSpec((half, width), lambda s, *_: (0, s))
    message = jax.ShapeDtypeStruct((half, ratio * width), bf)
    small = jax.ShapeDtypeStruct((half, width), bf)
    return pl.pallas_call(
        middle_kernel,
        grid_spec=pltpu.PrefetchScalarGridSpec(
            num_scalar_prefetch=1,
            grid=(ratio,),
            in_specs=[whole] * 5
            + [
                pl.BlockSpec((width, width), lambda s, *_: (0, 0)),
                pl.BlockSpec((width, width), lambda s, *_: (0, 1 + s)),
                pl.BlockSpec((width, width), lambda s, *_: (0, 1 + ratio + s)),
            ],
            out_specs=[whole, pl.BlockSpec((rows, width), lambda s, *_: (0, s))]
            + [part] * 4
            + [whole] * 4,
            scratch_shapes=[
                pltpu.VMEM((rows, width), f32),
                pltpu.VMEM((rows, 128), f32),
                pltpu.VMEM((rows, width), bf),
                pltpu.VMEM((rows, width), bf),
                pltpu.VMEM((rows, width), f32),
                pltpu.VMEM((width, width), f32),
            ],
        ),
        out_shape=[line, jax.ShapeDtypeStruct((rows, ratio * width), bf)]
        + [message] * 4
        + [small, small, line, low],
        compiler_params=pltpu.CompilerParams(vmem_limit_bytes=52 * 1024 * 1024),
        cost_estimate=BRIEF,
        name="middle",
    )(places, x, o, dz, gains, order, packed, packed, packed)


def out_kernel(mid_ref, hid_ref, wp_ref, out_ref, acc):
    step = pl.program_id(0)

    @pl.when(step == 0)
    def _():
        acc[...] = mid_ref[...]

    acc[...] += dot(hid_ref[...], wp_ref[...])

    @pl.when(step == pl.num_programs(0) - 1)
    def _():
        out_ref[...] = acc[...].astype(bf)


def layer_out(mid, hid, packed):
    rows, width = mid.shape
    ratio = hid.shape[1] // width
    whole = pl.BlockSpec(memory_space=pltpu.VMEM)
    return pl.pallas_call(
        out_kernel,
        grid=(ratio,),
        in_specs=[
            whole,
            pl.BlockSpec((rows, width), lambda s: (0, s)),
            pl.BlockSpec((width, width), lambda s: (0, 1 + ratio + s)),
        ],
        out_specs=whole,
        out_shape=jax.ShapeDtypeStruct((rows, width), bf),
        scratch_shapes=[pltpu.VMEM((rows, width), f32)],
        compiler_params=pltpu.CompilerParams(vmem_limit_bytes=58 * 1024 * 1024),
        cost_estimate=BRIEF,
        name="layer_out",
    )(mid, hid, packed)


def add(*arrays):
    total = arrays[0].astype(f32)
    for array in arrays[1:]:
        total += array.astype(f32)
    return total


class Links:
    def __init__(self, wide):
        self.wide = wide
        self.outer = wide // 4

    def swap(self, array, name):
        if name == "y":
            return lax.ppermute(array, "narrow", [(0, 1), (1, 0)])
        flip = 1 if name == "core" else 2
        return lax.ppermute(array, "wide", [(j, j ^ flip) for j in range(self.wide)])

    def flip_z(self, array, s):
        return lax.ppermute(array, "wide", [(j, j ^ (4 * s)) for j in range(self.wide)])

    def distance(self, at):
        bits = self.outer.bit_length() - 1
        return sum(((at >> b) & 1) << (bits - 1 - b) for b in range(bits))

    def order(self, width):
        place = lax.axis_index("wide")
        count = 2 * self.wide
        rows = width // count
        at = jnp.arange(count, dtype=jnp.int32)
        z, at = self.distance(at % self.outer) ^ (place // 4), at // self.outer
        y, at = (at + lax.axis_index("narrow")) % 2, at // 2
        x, at = (at + place // 2) % 2, at // 2
        core = (at + place) % 2
        places = ((z * 2 + x) * 2 + core) * 2 + y
        source = (places[:, None] * rows + jnp.arange(rows, dtype=jnp.int32)[None, :]).reshape(width)
        matrix = (jnp.arange(width, dtype=jnp.int32)[:, None] == source[None, :]).astype(bf)
        return places, matrix

    def along_z(self, shard):
        parts = [shard] + [self.flip_z(shard, self.distance(j)) for j in range(1, self.outer)]
        return jnp.concatenate(parts, axis=0)

    def along_xy(self, mine):
        cut = halfway(mine)
        one, two = mine[:, :cut], mine[:, cut:]
        one = jnp.concatenate([one, self.swap(one, "x")], axis=0)
        two = jnp.concatenate([two, self.swap(two, "y")], axis=0)
        one = (one, self.swap(one, "y"))
        two = (two, self.swap(two, "x"))
        return (
            one + tuple(self.swap(piece, "core") for piece in one),
            two + tuple(self.swap(piece, "core") for piece in two),
        )

    def first(self, pairs, *deps):
        rows = pairs[0][0].shape[0] // 4
        cuts = [halfway(keep) for keep, _ in pairs]
        wide = [sum(cuts), sum(keep.shape[1] for keep, _ in pairs) - sum(cuts)]

        def kernel(*refs):
            count = 2 * len(pairs)
            keep_x, send_x, keep_y, send_y = refs[-4:]
            at = [0, 0]
            for keep, got, cut in zip(refs[0:count:2], refs[1:count:2], cuts):
                rest = keep.shape[1] - cut
                one, two = slice(0, cut), slice(cut, cut + rest)
                to = slice(at[0], at[0] + cut)
                keep_x[:, to] = add(keep[:2 * rows, one], got[:2 * rows, one]).astype(bf)
                send_x[:, to] = add(keep[2 * rows:, one], got[2 * rows:, one]).astype(bf)
                to = slice(at[1], at[1] + rest)
                for j, out in enumerate((keep_y, send_y, keep_y, send_y)):
                    of = slice(j * rows, (j + 1) * rows)
                    into = slice(j // 2 * rows, (j // 2 + 1) * rows)
                    out[into, to] = add(keep[of, two], got[of, two]).astype(bf)
                at = [at[0] + cut, at[1] + rest]

        shapes = [(2 * rows, wide[0])] * 2 + [(2 * rows, wide[1])] * 2
        keep_x, send_x, keep_y, send_y = stage(kernel, sum(pairs, ()), deps, shapes)
        return (keep_x, keep_y), (self.swap(send_x, "x"), self.swap(send_y, "y"))

    def second(self, keep, got, *deps):
        rows = keep[0].shape[0] // 2

        def kernel(keep_x, keep_y, got_x, got_y, *refs):
            for keep, got, hold, send in ((keep_x, got_x, *refs[-4:-2]), (keep_y, got_y, *refs[-2:])):
                hold[...] = add(keep[:rows], got[:rows]).astype(bf)
                send[...] = add(keep[rows:], got[rows:]).astype(bf)

        shapes = [(rows, keep[0].shape[1])] * 2 + [(rows, keep[1].shape[1])] * 2
        keep_x, send_x, keep_y, send_y = stage(kernel, keep + got, deps, shapes)
        return (keep_x, keep_y), (self.swap(send_x, "y"), self.swap(send_y, "x"))

    def third(self, keep, got, *deps):
        cut = keep[0].shape[1]
        rows = keep[0].shape[0] // 2

        def kernel(keep_x, keep_y, got_x, got_y, *refs):
            hold, send = refs[-2:]
            for cols, keep, got in ((slice(0, cut), keep_x, got_x), (slice(cut, None), keep_y, got_y)):
                hold[:, cols] = add(keep[:rows], got[:rows]).astype(bf)
                send[:, cols] = add(keep[rows:], got[rows:]).astype(bf)

        hold, send = stage(kernel, keep + got, deps, [(rows, cut + keep[1].shape[1])] * 2)
        return hold, self.flip_z(send, 1)

    def fourth(self, keep, got, *deps):
        for bit in range(1, self.outer.bit_length() - 1):
            rows = keep.shape[0] // 2
            if rows % 8:
                total = add(keep, got).astype(bf)
                keep, send = total[:rows], total[rows:]
            else:
                keep, send = stage(halves_kernel, (keep, got), deps, [(rows, keep.shape[1])] * 2)
            got = self.flip_z(send, 1 << bit)
        return keep, got


def halves_kernel(keep, got, *refs):
    hold, send = refs[-2:]
    total = add(keep[...], got[...])
    hold[...] = total[:hold.shape[0]].astype(bf)
    send[...] = total[hold.shape[0]:].astype(bf)


def first_kernel(hidk, hidg, projk, projg, outk_x, outg_x, outk_y, outg_y, *refs):
    keep_x, send_x, keep_y, send_y = refs[-4:]
    rows = hidk.shape[0] // 4
    last = pl.num_programs(0) - 1

    def write(one, two):
        cols = slice(0, one[0].shape[1])
        keep_x[:, cols] = add(*(v[:2 * rows, :] for v in one)).astype(bf)
        send_x[:, cols] = add(*(v[2 * rows:, :] for v in one)).astype(bf)
        for j, out in enumerate((keep_y, send_y, keep_y, send_y)):
            of = slice(j * rows, (j + 1) * rows)
            out[j // 2 * rows:(j // 2 + 1) * rows, cols] = add(*(v[of, :] for v in two)).astype(bf)

    @pl.when(pl.program_id(0) < last)
    def _():
        write((hidk, hidg), (projk, projg))

    @pl.when(pl.program_id(0) == last)
    def _():
        write((outk_x, outg_x), (outk_y, outg_y))


class Middle:
    def __init__(self, links):
        self.links = links

    def first(self, hid, proj, out, *deps):
        rows, columns = hid[0].shape
        block = out[0].shape[1]
        steps = columns // block
        tile = pl.BlockSpec((rows, block), lambda j: (0, jnp.minimum(j, steps - 1)))
        half = [pl.BlockSpec((rows, block // 2), lambda j, at=at: (0, at)) for at in range(2)]
        shape = jax.ShapeDtypeStruct((rows // 2, columns + block // 2), bf)
        keep_x, send_x, keep_y, send_y = pl.pallas_call(
            first_kernel,
            grid=(steps + 1,),
            in_specs=[tile] * 4
            + [half[0]] * 2
            + [half[1]] * 2
            + [pl.BlockSpec(memory_space=pl.ANY)] * len(deps),
            out_specs=[pl.BlockSpec((rows // 2, block), lambda j: (0, j))] * 4,
            out_shape=[shape] * 4,
            compiler_params=pltpu.CompilerParams(vmem_limit_bytes=58 * 1024 * 1024),
            cost_estimate=BRIEF,
            name="first",
        )(*hid, *proj, *out, *out, *deps)
        return (keep_x, keep_y), (self.links.swap(send_x, "x"), self.links.swap(send_y, "y"))

    def second(self, keep, got, *deps):
        rows = keep[0].shape[0] // 4
        cut = keep[0].shape[1]

        def kernel(keep_x, keep_y, got_x, got_y, *refs):
            hold_x, hold_y, send = refs[-3:]
            halves = ((hold_x, slice(0, cut), keep_x, got_x), (hold_y, slice(cut, None), keep_y, got_y))
            for hold, cols, keep, got in halves:
                for j in range(2):
                    into = slice(j * rows, (j + 1) * rows)
                    of = slice(2 * j * rows, (2 * j + 1) * rows)
                    hold[into, :] = add(keep[of, :], got[of, :]).astype(bf)
                    of = slice((2 * j + 1) * rows, (2 * j + 2) * rows)
                    send[into, cols] = add(keep[of, :], got[of, :]).astype(bf)

        wide = keep[1].shape[1]
        shapes = [(2 * rows, cut), (2 * rows, wide), (2 * rows, cut + wide)]
        hold_x, hold_y, send = stage(kernel, keep + got, deps, shapes)
        return (hold_x, hold_y), self.links.flip_z(send, 1)

    def third(self, keep, got, *deps):
        rows = keep[0].shape[0] // 2
        cut = keep[0].shape[1]

        def kernel(keep_x, keep_y, got, *refs):
            for keep, cols, hold, send in (
                (keep_x, slice(0, cut), *refs[-4:-2]), (keep_y, slice(cut, None), *refs[-2:])
            ):
                hold[...] = add(keep[:rows, :], got[:rows, cols]).astype(bf)
                send[...] = add(keep[rows:, :], got[rows:, cols]).astype(bf)

        shapes = [(rows, cut)] * 2 + [(rows, keep[1].shape[1])] * 2
        hold_x, send_x, hold_y, send_y = stage(kernel, keep + (got,), deps, shapes)
        return (hold_x, hold_y), (self.links.swap(send_x, "y"), self.links.swap(send_y, "x"))

    def fourth(self, keep, got, *deps):
        rows = keep[0].shape[0] // 2
        cut = keep[0].shape[1]
        if rows % 8:
            total = jnp.concatenate([add(k, g).astype(bf) for k, g in zip(keep, got)], axis=1)
            hold, send = total[:rows], total[rows:]
        else:
            def kernel(keep_x, keep_y, got_x, got_y, *refs):
                hold, send = refs[-2:]
                for cols, keep, got in ((slice(0, cut), keep_x, got_x), (slice(cut, None), keep_y, got_y)):
                    total = add(keep[...], got[...])
                    hold[:, cols] = total[:rows].astype(bf)
                    send[:, cols] = total[rows:].astype(bf)

            hold, send = stage(kernel, keep + got, deps, [(rows, cut + keep[1].shape[1])] * 2)
        got = self.links.flip_z(send, 2)
        for bit in range(2, self.links.outer.bit_length() - 1):
            total = add(hold, got).astype(bf)
            rows = rows // 2
            hold, send = total[:rows], total[rows:]
            got = self.links.flip_z(send, 1 << bit)
        return hold, got


def collect(parts, *deps):
    def kernel(*refs):
        refs[-1][...] = add(*(ref[...] for ref in refs[:len(parts)]))

    return stage(kernel, parts, deps, [parts[0].shape], f32)[0]


def stage(kernel, operands, deps, shapes, kind=bf):
    whole = pl.BlockSpec(memory_space=pltpu.VMEM)
    elsewhere = pl.BlockSpec(memory_space=pl.ANY)
    return pl.pallas_call(
        kernel,
        in_specs=[whole] * len(operands) + [elsewhere] * len(deps),
        out_specs=[whole] * len(shapes),
        out_shape=[jax.ShapeDtypeStruct(shape, kind) for shape in shapes],
        compiler_params=pltpu.CompilerParams(vmem_limit_bytes=24 * 1024 * 1024),
        cost_estimate=BRIEF,
        name="stage",
    )(*operands, *deps)


def hold(values, *deps):
    count = len(values)
    elsewhere = pl.BlockSpec(memory_space=pl.ANY)
    return pl.pallas_call(
        lambda *refs: None,
        in_specs=[elsewhere] * (count + len(deps)),
        out_specs=[elsewhere] * count,
        out_shape=[jax.ShapeDtypeStruct(v.shape, v.dtype) for v in values],
        input_output_aliases={j: j for j in range(count)},
        cost_estimate=BRIEF,
        name="hold",
    )(*values, *deps)


def halfway(array):
    return (array.shape[1] // 2 + 127) // 128 * 128


def share_kernel(dq_ref, dk_ref, dv_ref, w_ref, *refs):
    refs[-1][...] = back_input(w_ref, (0, dq_ref[...]), (1, dk_ref[...]), (2, dv_ref[...]))


def own_share(own, weight, *deps):
    rows, width = own[0].shape
    tile = pl.BlockSpec((OWN, width), lambda i: (i, 0))
    return pl.pallas_call(
        share_kernel,
        grid=(rows // OWN,),
        in_specs=[tile] * 3
        + [pl.BlockSpec(memory_space=pltpu.VMEM)]
        + [pl.BlockSpec(memory_space=pl.ANY)] * len(deps),
        out_specs=tile,
        out_shape=jax.ShapeDtypeStruct((rows, width), f32),
        compiler_params=pltpu.CompilerParams(vmem_limit_bytes=58 * 1024 * 1024),
        cost_estimate=BRIEF,
        name="own_share",
    )(*own, weight, *deps)


def finish_kernel(x_ref, dx_ref, own_ref, b0, b1, b2, b3, gain_ref, out_ref):
    n, r = normalize_parts(x_ref[...].astype(f32))
    da = add(own_ref[...], b0[...], b1[...], b2[...], b3[...])
    out_ref[...] = (dx_ref[...] + normalize_back(da, n, r, gain_ref[0:1, :])).astype(bf)


def finish(x, dx, own, others, gains):
    rows, width = x.shape
    tile = pl.BlockSpec((OWN, width), lambda i: (i, 0))
    return pl.pallas_call(
        finish_kernel,
        grid=(rows // OWN,),
        in_specs=[tile] * 7 + [pl.BlockSpec(gains.shape, lambda i: (0, 0))],
        out_specs=tile,
        out_shape=jax.ShapeDtypeStruct((rows, width), bf),
        compiler_params=pltpu.CompilerParams(vmem_limit_bytes=58 * 1024 * 1024),
        cost_estimate=BRIEF,
        name="finish",
    )(x, dx, own, *others, gains)


def gain_sums(w_ref, grad, shape):
    product = w_ref[...].astype(bf).astype(f32) * grad
    return jnp.broadcast_to(jnp.sum(product, axis=1, keepdims=True), shape)


def update_kernel(rate_ref, sum_ref, hid_ref, proj_ref, w_ref, mom_out, mom_hid, mom_proj,
                  step_out, step_hid, step_proj, next_out, next_hid, next_proj, gain_ref):
    rate = rate_ref[0]
    hidden = hid_ref.shape[1]
    width = mom_out.shape[1]
    half = width // 2
    far = hidden + half

    def put(step, following, at, momentum, grad):
        value = momentum_rate * momentum + grad
        following[at] = value
        step[at] = rate * value

    gain_ref[...] = gain_sums(w_ref, hid_ref[...], gain_ref.shape)
    whole = slice(None)
    put(step_hid, next_hid, (whole, whole), mom_hid[...], hid_ref[...])
    for at, lo in ((slice(0, half), hidden), (slice(half, width), far + hidden)):
        put(step_out, next_out, (whole, at), mom_out[:, at], sum_ref[:, lo:lo + half])
    put(step_proj, next_proj, (whole, whole), mom_proj[...], proj_ref[...])


def update(rate, total, hid, proj, w_hid, mom_out, mom_hid, mom_proj):
    whole = pl.BlockSpec(memory_space=pltpu.VMEM)
    moms = (mom_out, mom_hid, mom_proj)
    return pl.pallas_call(
        update_kernel,
        in_specs=[pl.BlockSpec(memory_space=pltpu.SMEM)] + [whole] * 7,
        out_specs=[whole] * 7,
        out_shape=[jax.ShapeDtypeStruct(m.shape, f32) for m in moms + moms]
        + [jax.ShapeDtypeStruct((hid.shape[0], 128), f32)],
        cost_estimate=BRIEF,
        name="update",
    )(rate, total, hid, proj, w_hid, *moms)


def update_first_kernel(rate_ref, keep_ref, got_ref, w_ref, mom_ref, step_ref, next_ref, gain_ref):
    total = add(keep_ref[...], got_ref[...])
    gain_ref[...] = gain_sums(w_ref, total, gain_ref.shape)
    value = momentum_rate * mom_ref[...] + total
    next_ref[...] = value
    step_ref[...] = rate_ref[0] * value


def update_first(rate, keep, got, weight, mom):
    whole = pl.BlockSpec(memory_space=pltpu.VMEM)
    return pl.pallas_call(
        update_first_kernel,
        in_specs=[pl.BlockSpec(memory_space=pltpu.SMEM)] + [whole] * 4,
        out_specs=[whole] * 3,
        out_shape=[jax.ShapeDtypeStruct(mom.shape, f32)] * 2
        + [jax.ShapeDtypeStruct((mom.shape[0], 128), f32)],
        cost_estimate=BRIEF,
        name="update_first",
    )(rate, keep, got, weight, mom)


def body(
    joint_in,
    cotangent,
    segment_ids,
    layer_index,
    step_index,
    gain_one,
    w_qkv,
    w_attn_out,
    gain_two,
    w_hidden,
    w_proj,
    mom_gain_one,
    mom_qkv,
    mom_attn_out,
    mom_gain_two,
    mom_hidden,
    mom_proj,
):
    rows, width = joint_in.shape
    wide = lax.axis_size("wide")
    both = ("wide", "narrow")
    shard = w_qkv.shape[0]
    hidden = w_hidden.shape[1]
    ratio = hidden // width
    odd = lax.axis_index("narrow")
    place = lax.axis_index("wide") * 2 + odd
    window = 5 * rows
    is_even = odd == 0

    links = Links(wide)
    places, order = links.order(width)
    if shard % 8 == 0:
        order = jnp.zeros((8, 128), bf)
    gains = jnp.stack([gain_one, gain_two], axis=1)
    gains = jnp.pad(gains, ((0, 0), (0, 126)))
    pack_a = jnp.concatenate([w_qkv.astype(bf), gains.astype(bf)], axis=1)
    hid_order = w_hidden.astype(bf).reshape(shard, width, ratio).transpose(0, 2, 1)
    pack_b = jnp.concatenate(
        [
            w_attn_out.astype(bf),
            hid_order.reshape(shard, hidden),
            w_proj.astype(bf).reshape(shard, hidden),
        ],
        axis=1,
    )

    fill = jnp.full((2 * rows,), -1, jnp.int32)
    ids = jnp.concatenate([fill, segment_ids, fill])
    key_ids = lax.dynamic_slice_in_dim(ids, place * rows, window, 0)
    own_ids = lax.dynamic_slice_in_dim(segment_ids, place * rows, rows, 0)
    tiles = own_ids.reshape(rows // QT, QT)
    far_ids = jnp.concatenate([key_ids[:2 * rows], key_ids[3 * rows:]])
    kseg = jnp.broadcast_to(far_ids[:, None], (4 * rows, QT))
    oseg = jnp.broadcast_to(own_ids[:, None], (rows, QT))
    qseg = jnp.broadcast_to(tiles[:, None, :], (rows // QT, 8, QT))
    origin = (place - 2) * rows
    low = jnp.sum(segment_ids[None, :] < tiles[:, :1], axis=1, dtype=jnp.int32) - origin
    high = jnp.sum(segment_ids[None, :] <= tiles[:, -1:], axis=1, dtype=jnp.int32) - origin
    low = jnp.clip(low, 0, window)
    high = jnp.clip(high, 0, window)
    side = 2 * rows // OUTER
    starts = [2 * rows + j * OWN for j in range(rows // OWN)]
    starts += [j * OUTER for j in range(side)] + [3 * rows + j * OUTER for j in range(side)]
    sizes = [OWN] * (rows // OWN) + [OUTER] * (2 * side)
    edges = jnp.asarray(starts, jnp.int32)[:, None]
    tops = jnp.asarray([at + size for at, size in zip(starts, sizes)], jnp.int32)[:, None]
    begin = jnp.sum(high[None, :] <= edges, axis=1, dtype=jnp.int32)
    end = jnp.sum(low[None, :] < tops, axis=1, dtype=jnp.int32)
    near = jnp.minimum(low[0] // OUTER, side)
    last = side - 1 + jnp.maximum(high[-1] - 3 * rows + OUTER - 1, 0) // OUTER
    span = jnp.stack([near, jnp.maximum(last, near)])
    scalars = (begin, end, span, odd.reshape(1), places)

    swap = [(0, 1), (1, 0)]
    up = [(j, j + 1) for j in range(wide - 1)]
    down = [(j + 1, j) for j in range(wide - 1)]
    across = [(2 * j, 2 * j + 2) for j in range(wide - 1)]
    across += [(2 * j + 3, 2 * j + 1) for j in range(wide - 1)]
    partner = lax.ppermute(joint_in, "narrow", swap)
    before = lax.ppermute(joint_in, "wide", up)
    behind = lax.ppermute(joint_in, "wide", down)
    mine_a = links.along_z(pack_a)
    fourth = lax.ppermute(partner, both, across)
    ones, twos = links.along_xy(mine_a)
    blocks = (before, partner, fourth, behind)
    (pack_b,) = hold((pack_b,), before, partner, behind, mine_a)
    full_b = lax.all_gather(pack_b, both, axis=0, tiled=True)

    weight, gains, a_own, k_own, v_own, a_far, k_far, v_far, q, o, lse = attend(
        scalars, blocks, kseg, oseg, joint_in, qseg, order, ones, twos
    )

    mid, hid, hid_keep, hid_send, proj_keep, proj_send, out_keep, out_send, dx, do = middle(
        places, joint_in, o, cotangent, gains, order, full_b
    )
    joint_out = layer_out(mid, hid, full_b)
    chain = Middle(links)
    keep_b, got_b = chain.first(
        (hid_keep, links.swap(hid_send, "core")),
        (proj_keep, links.swap(proj_send, "core")),
        (out_keep, links.swap(out_send, "core")),
        joint_out,
    )
    args = (q, do, o, lse, qseg)
    da_before, da_partner, da_fourth, da_behind, *partial = outer_back(
        scalars, k_far, v_far, a_far, kseg, *args, weight, *keep_b
    )

    keep_b, got_b = chain.second(keep_b, got_b, da_before)
    home = [(2 * j + 2, 2 * j + 1) for j in range(wide - 1)]
    home += [(t, s) for s, t in home]
    others = (
        lax.ppermute(da_before, "wide", down),
        lax.ppermute(da_partner, "narrow", swap),
        lax.ppermute(da_fourth, both, home),
        lax.ppermute(da_behind, "wide", up),
    )
    dk, dv, dq, keep_a, send_a, token = inner_back(
        scalars, k_own, v_own, a_own, oseg, *args, order, partial, *keep_b
    )

    keep_b, got_b = chain.third(keep_b, got_b, token)
    da_own = own_share((dq, dk, dv), weight, *keep_b)
    (send_a,) = hold((send_a,), da_own, *others, *keep_b)
    got_a = links.swap(send_a, "core")
    keep_a, got_a = links.first([(keep_a, got_a)])
    keep_b, got_b = chain.fourth(keep_b, got_b, *keep_a)
    (gains,) = hold((gains,), keep_b)
    grad_in = finish(joint_in, dx, da_own, others, gains)
    keep_a, got_a = links.second(keep_a, got_a, grad_in)
    sum_b = collect((keep_b, got_b), *keep_a)
    keep_a, got_a = links.third(keep_a, got_a, sum_b)
    keep_a, got_a = links.fourth(keep_a, got_a)

    rate = base_rate * jnp.power(jnp.float32(decay_rate), (11 - layer_index).astype(f32))
    rate = rate * jnp.power(1.0 - step_index.astype(f32) / total_steps, 0.9)
    sum_hid = sum_b[:, :hidden].reshape(shard, ratio, width).transpose(0, 2, 1)
    sum_hid = sum_hid.reshape(shard, hidden)
    far = hidden + width // 2
    sum_proj = sum_b[:, far:far + hidden].reshape(shard * ratio, width)
    step_out, step_hid, step_proj, next_out, next_hid, next_proj, gain_b = update(
        rate, sum_b, sum_hid, sum_proj, w_hidden, mom_attn_out, mom_hidden, mom_proj
    )
    step_qkv, next_qkv, gain_a = update_first(rate, keep_a, got_a, w_qkv, mom_qkv)
    next_g1 = momentum_rate * mom_gain_one + gain_a[:, 0] / gain_one.astype(bf).astype(f32)
    next_g2 = momentum_rate * mom_gain_two + gain_b[:, 0] / gain_two.astype(bf).astype(f32)
    return (
        joint_out,
        grad_in,
        rate * next_g1,
        step_qkv,
        step_out,
        rate * next_g2,
        step_hid,
        step_proj,
        next_g1,
        next_qkv,
        next_out,
        next_g2,
        next_hid,
        next_proj,
    )


def solution(mesh):
    split = P(("wide", "narrow"), None)
    line = P(("wide", "narrow"))
    params = (line, split, split, line, split, split)
    return jax.shard_map(
        body,
        mesh=mesh,
        in_specs=(split, split, P(), P(), P()) + params + params,
        out_specs=(split, split) + params + params,
        check_vma=False,
    )
```
